32 devices in a mesh: dp: 8 (over y, x, core), mp: 4 (over z).
Axes of the slice: x: 2, y: 2, z: 4, core: 2. Of those that a mesh axis runs over, the one named last changes fastest.
Arguments:
- patches: bfloat16 [16928, 768], P(('dp', 'mp')), may hold values from -6 to 6
- lengths: int32 [32], P('dp'), may hold values from 40 to 529, as said below
- encoder_attention_gain: float32 [768], replicated, may hold values from 0.1 to 1.9
- encoder_attention_shift: float32 [768], replicated, may hold values from -2 to 2
- encoder_projections: bfloat16 [3, 768, 768], P(None, None, 'mp'), may hold values from -0.21875 to 0.21875
- encoder_head_bias: float32 [2, 768], P(None, 'mp'), may hold values from -2 to 2
- encoder_output_weight: bfloat16 [768, 768], P('mp'), may hold values from -0.875 to 0.875
- encoder_output_bias: float32 [768], replicated, may hold values from -2 to 2
- encoder_feed_gain: float32 [768], replicated, may hold values from 0.1 to 1.9
- encoder_feed_shift: float32 [768], replicated, may hold values from -2 to 2
- encoder_up_weight: bfloat16 [768, 3072], P(None, 'mp'), may hold values from -0.21875 to 0.21875
- encoder_up_bias: float32 [3072], P('mp'), may hold values from -2 to 2
- encoder_down_weight: bfloat16 [3072, 768], P('mp'), may hold values from -0.109375 to 0.109375
- encoder_down_bias: float32 [768], replicated, may hold values from -2 to 2
- bridge_weight: bfloat16 [768, 512], replicated, may hold values from -0.21875 to 0.21875
- bridge_bias: float32 [512], replicated, may hold values from -2 to 2
- decoder_attention_gain: float32 [512], replicated, may hold values from 0.1 to 1.9
- decoder_attention_shift: float32 [512], replicated, may hold values from -2 to 2
- decoder_projections: bfloat16 [3, 512, 512], P(None, None, 'mp'), may hold values from -0.25 to 0.25
- decoder_head_bias: float32 [2, 512], P(None, 'mp'), may hold values from -2 to 2
- decoder_output_weight: bfloat16 [512, 512], P('mp'), may hold values from -1 to 1
- decoder_output_bias: float32 [512], replicated, may hold values from -2 to 2
- decoder_feed_gain: float32 [512], replicated, may hold values from 0.1 to 1.9
- decoder_feed_shift: float32 [512], replicated, may hold values from -2 to 2
- decoder_up_weight: bfloat16 [512, 2048], P(None, 'mp'), may hold values from -0.25 to 0.25
- decoder_up_bias: float32 [2048], P('mp'), may hold values from -2 to 2
- decoder_down_weight: bfloat16 [2048, 512], P('mp'), may hold values from -0.125 to 0.125
- decoder_down_bias: float32 [512], replicated, may hold values from -2 to 2
- cotangent: bfloat16 [16928, 512], P(('dp', 'mp')), may hold values from -6 to 6
Outputs:
- decoded: bfloat16 [16928, 512], P(('dp', 'mp'))
- patches_gradient: bfloat16 [16928, 768], P(('dp', 'mp'))
- encoder_attention_gain_gradient: float32 [768], P(('dp', 'mp'))
- encoder_attention_shift_gradient: float32 [768], P(('dp', 'mp'))
- encoder_projections_gradient: float32 [3, 768, 768], P(None, 'dp', 'mp')
- encoder_head_bias_gradient: float32 [2, 768], P(None, ('mp', 'dp'))
- encoder_output_weight_gradient: float32 [768, 768], P('mp', 'dp')
- encoder_output_bias_gradient: float32 [768], P(('dp', 'mp'))
- encoder_feed_gain_gradient: float32 [768], P(('dp', 'mp'))
- encoder_feed_shift_gradient: float32 [768], P(('dp', 'mp'))
- encoder_up_weight_gradient: float32 [768, 3072], P('dp', 'mp')
- encoder_up_bias_gradient: float32 [3072], P(('mp', 'dp'))
- encoder_down_weight_gradient: float32 [3072, 768], P('mp', 'dp')
- encoder_down_bias_gradient: float32 [768], P(('dp', 'mp'))
- bridge_weight_gradient: float32 [768, 512], P(('dp', 'mp'))
- bridge_bias_gradient: float32 [512], P(('dp', 'mp'))
- decoder_attention_gain_gradient: float32 [512], P(('dp', 'mp'))
- decoder_attention_shift_gradient: float32 [512], P(('dp', 'mp'))
- decoder_projections_gradient: float32 [3, 512, 512], P(None, 'dp', 'mp')
- decoder_head_bias_gradient: float32 [2, 512], P(None, ('mp', 'dp'))
- decoder_output_weight_gradient: float32 [512, 512], P('mp', 'dp')
- decoder_output_bias_gradient: float32 [512], P(('dp', 'mp'))
- decoder_feed_gain_gradient: float32 [512], P(('dp', 'mp'))
- decoder_feed_shift_gradient: float32 [512], P(('dp', 'mp'))
- decoder_up_weight_gradient: float32 [512, 2048], P('dp', 'mp')
- decoder_up_bias_gradient: float32 [2048], P(('mp', 'dp'))
- decoder_down_weight_gradient: float32 [2048, 512], P('mp', 'dp')
- decoder_down_bias_gradient: float32 [512], P(('dp', 'mp'))
The draws below stay inside these ranges and needn't reach their ends.
Inputs may be any that keep to these rules, and one draw needn't show every extreme that they name: `lengths`: slots at or past a strip's length are blanks that no query attends to; some strip has length 529 and some has 40.
All inputs are finite; a program needn't handle non-finite values.
Results may differ from the reference program's by a relative error of at most 0.035.
Values may be sent and summed in bfloat16 or wider, within the bound.
A program may use at most 192 MiB of HBM per device.

```python
from functools import partial
import jax
import jax.numpy as jnp
from jax import lax

D = 768
HEAD = 64
FF = 3072
DD = 512
DHEAD = 32
DFF = 2048
S = 529
LMIN = 40
STRIPS = 32
TOKENS = 16928


def draw_lengths(key, part):
    key = jax.random.fold_in(key, 11)
    first_key, second_key, third_key = jax.random.split(key, 3)
    drawn_lengths = jax.random.randint(first_key, (STRIPS,), LMIN, S + 1)
    longest = jax.random.randint(second_key, (), 0, STRIPS)
    offset = jax.random.randint(third_key, (), 1, STRIPS)
    shortest = (longest + offset) % STRIPS
    return drawn_lengths.at[longest].set(S).at[shortest].set(LMIN).astype(jnp.int32)


def steps_of(rng, shape, cuts, low, largest):
    gain, own = 1.0, jax.random.fold_in(rng, 6)
    for position, parts in cuts:
        steps = jnp.exp(jax.random.uniform(jax.random.fold_in(own, position), (parts,), jnp.float32, low / len(cuts), largest / len(cuts)))
        gain = gain * jnp.repeat(steps, shape[position] // parts).reshape([-1 if axis == position else 1 for axis in range(len(shape))])
    return gain


def scatter_about(own_key, extent, deviation, bound, shards=(), dtype=jnp.bfloat16):
    entries = deviation * jax.random.normal(own_key, extent, jnp.float32)
    if shards:
        entries = entries * steps_of(own_key, extent, shards, -0.22, 0.18)
    return jnp.clip(entries, -bound, bound).astype(dtype)


def setup_inputs(seed: int = 0) -> dict:
    streams_of = jax.random.split(jax.random.key(seed), 30)
    patches = scatter_about(streams_of[0], (TOKENS, D), 1.0, 6.0, ((0, 32),))
    lengths = draw_lengths(jax.random.fold_in(streams_of[29], 71), 0)
    encoder_attention_gain = jnp.clip(1.0 + 0.18 * jax.random.normal(streams_of[2], (D,), jnp.float32), 0.1, 1.9)
    encoder_attention_shift = scatter_about(streams_of[3], (D,), 0.3, 2.0, (), jnp.float32)
    encoder_projections = scatter_about(streams_of[4], (3, D, D), D ** -0.5, 0.21875, ((2, 4),))
    encoder_head_bias = scatter_about(streams_of[5], (2, D), 0.3, 2.0, ((1, 4),), jnp.float32)
    encoder_output_weight = scatter_about(streams_of[6], (D, D), (D // 16) ** -0.5, 0.875, ((0, 4),))
    encoder_output_bias = scatter_about(streams_of[7], (D,), 0.3, 2.0, (), jnp.float32)
    encoder_feed_gain = jnp.clip(1.0 + 0.18 * jax.random.normal(streams_of[8], (D,), jnp.float32), 0.1, 1.9)
    encoder_feed_shift = scatter_about(streams_of[9], (D,), 0.3, 2.0, (), jnp.float32)
    encoder_up_weight = scatter_about(streams_of[10], (D, FF), D ** -0.5, 0.21875, ((1, 4),))
    encoder_up_bias = scatter_about(streams_of[11], (FF,), 0.3, 2.0, ((0, 4),), jnp.float32)
    encoder_down_weight = scatter_about(streams_of[12], (FF, D), FF ** -0.5, 0.109375, ((0, 4),))
    encoder_down_bias = scatter_about(streams_of[13], (D,), 0.3, 2.0, (), jnp.float32)
    bridge_weight = scatter_about(streams_of[14], (D, DD), D ** -0.5, 0.21875)
    bridge_bias = scatter_about(streams_of[15], (DD,), 0.3, 2.0, (), jnp.float32)
    decoder_attention_gain = jnp.clip(1.0 + 0.18 * jax.random.normal(streams_of[16], (DD,), jnp.float32), 0.1, 1.9)
    decoder_attention_shift = scatter_about(streams_of[17], (DD,), 0.3, 2.0, (), jnp.float32)
    decoder_projections = scatter_about(streams_of[18], (3, DD, DD), DD ** -0.5, 0.25, ((2, 4),))
    decoder_head_bias = scatter_about(streams_of[19], (2, DD), 0.3, 2.0, ((1, 4),), jnp.float32)
    decoder_output_weight = scatter_about(streams_of[20], (DD, DD), (DD // 16) ** -0.5, 1.0, ((0, 4),))
    decoder_output_bias = scatter_about(streams_of[21], (DD,), 0.3, 2.0, (), jnp.float32)
    decoder_feed_gain = jnp.clip(1.0 + 0.18 * jax.random.normal(streams_of[22], (DD,), jnp.float32), 0.1, 1.9)
    decoder_feed_shift = scatter_about(streams_of[23], (DD,), 0.3, 2.0, (), jnp.float32)
    decoder_up_weight = scatter_about(streams_of[24], (DD, DFF), DD ** -0.5, 0.25, ((1, 4),))
    decoder_up_bias = scatter_about(streams_of[25], (DFF,), 0.3, 2.0, ((0, 4),), jnp.float32)
    decoder_down_weight = scatter_about(streams_of[26], (DFF, DD), DFF ** -0.5, 0.125, ((0, 4),))
    decoder_down_bias = scatter_about(streams_of[27], (DD,), 0.3, 2.0, (), jnp.float32)
    cotangent = scatter_about(streams_of[28], (TOKENS, DD), 1.0, 6.0, ((0, 32),))
    return {"patches": patches, "lengths": lengths, "encoder_attention_gain": encoder_attention_gain, "encoder_attention_shift": encoder_attention_shift, "encoder_projections": encoder_projections, "encoder_head_bias": encoder_head_bias, "encoder_output_weight": encoder_output_weight, "encoder_output_bias": encoder_output_bias, "encoder_feed_gain": encoder_feed_gain, "encoder_feed_shift": encoder_feed_shift, "encoder_up_weight": encoder_up_weight, "encoder_up_bias": encoder_up_bias, "encoder_down_weight": encoder_down_weight, "encoder_down_bias": encoder_down_bias, "bridge_weight": bridge_weight, "bridge_bias": bridge_bias, "decoder_attention_gain": decoder_attention_gain, "decoder_attention_shift": decoder_attention_shift, "decoder_projections": decoder_projections, "decoder_head_bias": decoder_head_bias, "decoder_output_weight": decoder_output_weight, "decoder_output_bias": decoder_output_bias, "decoder_feed_gain": decoder_feed_gain, "decoder_feed_shift": decoder_feed_shift, "decoder_up_weight": decoder_up_weight, "decoder_up_bias": decoder_up_bias, "decoder_down_weight": decoder_down_weight, "decoder_down_bias": decoder_down_bias, "cotangent": cotangent}


EPSILON = 1e-06

@jax.custom_vjp
def low(v):
    return lax.optimization_barrier(v.astype(jnp.bfloat16)).astype(jnp.float32)

@jax.custom_vjp
def low_back(v):
    return v

def low_keep(v):
    return (low(v), None)

def low_pass(kept, grad):
    return (grad,)

def back_keep(v):
    return (v, None)

def back_low(kept, grad):
    return (low(grad),)
low.defvjp(low_keep, low_pass)
low_back.defvjp(back_keep, back_low)

def matmul(left, right):
    return jnp.dot(left, right, precision=lax.Precision.HIGHEST)

def normalize(stream, gain_vector, shift_vector):
    centered = stream - lax.optimization_barrier(jnp.mean(stream, -1, keepdims=True))
    variance = lax.optimization_barrier(jnp.mean(centered * centered, -1, keepdims=True))
    return centered * lax.rsqrt(variance + EPSILON) * gain_vector + shift_vector

def strip_attention(member, head_dim):
    queries, key_rows, values, length = member
    positions = queries.shape[0]
    head_count = queries.shape[1] // head_dim
    query_heads = queries.reshape(positions, head_count, head_dim)
    key_heads = key_rows.reshape(positions, head_count, head_dim)
    value_heads = values.reshape(positions, head_count, head_dim)
    scores = jnp.einsum('qhd,khd->hqk', query_heads, key_heads, precision=lax.Precision.HIGHEST) * head_dim ** (-0.5)
    visible = lax.iota(jnp.int32, positions) < length.astype(jnp.int32)
    scores = low_back(jnp.where(visible[None, None, :], scores, -1e+30))
    chances = low(jax.nn.softmax(scores, axis=-1))
    attended = jnp.einsum('hqk,khd->qhd', chances, value_heads, precision=lax.Precision.HIGHEST)
    return attended.reshape(positions, head_count * head_dim)

def block(stream, params, lengths, head_dim):
    attention_gain, attention_shift, projections, head_bias, output_weight, output_bias, feed_gain, feed_shift, up_weight, up_bias, down_weight, down_bias = params
    strips = lengths.shape[0]
    local_width = projections.shape[2]
    normed = low(normalize(stream, attention_gain, attention_shift))
    queries = low(low_back(matmul(normed, projections[0]) + head_bias[0]))
    key_rows = low(low_back(matmul(normed, projections[1])))
    values = low(low_back(matmul(normed, projections[2]) + head_bias[1]))
    attended = lax.map(jax.checkpoint(partial(strip_attention, head_dim=head_dim)), (queries.reshape(strips, S, local_width), key_rows.reshape(strips, S, local_width), values.reshape(strips, S, local_width), lengths))
    attended = low(low_back(attended.reshape(strips * S, local_width)))
    middle = stream + low_back(matmul(attended, output_weight) + output_bias)
    feed_input = low(normalize(middle, feed_gain, feed_shift))
    hidden = low(jax.nn.gelu(low_back(matmul(feed_input, up_weight) + up_bias), approximate=False))
    return middle + low_back(matmul(hidden, down_weight) + down_bias)

def network(patches, encoder, bridge_weight, bridge_bias, decoder, lengths):
    encoded = block(patches, encoder, lengths, HEAD)
    bridged = low_back(matmul(low(encoded), bridge_weight) + bridge_bias)
    return block(bridged, decoder, lengths, DHEAD)

def reference(patches, lengths, encoder_attention_gain, encoder_attention_shift, encoder_projections, encoder_head_bias, encoder_output_weight, encoder_output_bias, encoder_feed_gain, encoder_feed_shift, encoder_up_weight, encoder_up_bias, encoder_down_weight, encoder_down_bias, bridge_weight, bridge_bias, decoder_attention_gain, decoder_attention_shift, decoder_projections, decoder_head_bias, decoder_output_weight, decoder_output_bias, decoder_feed_gain, decoder_feed_shift, decoder_up_weight, decoder_up_bias, decoder_down_weight, decoder_down_bias, cotangent):
    encoder = tuple((member.astype(jnp.float32) for member in (encoder_attention_gain, encoder_attention_shift, encoder_projections, encoder_head_bias, encoder_output_weight, encoder_output_bias, encoder_feed_gain, encoder_feed_shift, encoder_up_weight, encoder_up_bias, encoder_down_weight, encoder_down_bias)))
    decoder = tuple((member.astype(jnp.float32) for member in (decoder_attention_gain, decoder_attention_shift, decoder_projections, decoder_head_bias, decoder_output_weight, decoder_output_bias, decoder_feed_gain, decoder_feed_shift, decoder_up_weight, decoder_up_bias, decoder_down_weight, decoder_down_bias)))
    primal, pullback = jax.vjp(partial(network, lengths=lengths), patches.astype(jnp.float32), encoder, bridge_weight.astype(jnp.float32), bridge_bias.astype(jnp.float32), decoder)
    patch_grad, enc_grads, bridge_wgrad, bridge_bgrad, dec_grads = pullback(cotangent.astype(jnp.float32))
    return (primal.astype(jnp.bfloat16), patch_grad.astype(jnp.bfloat16), enc_grads[0], enc_grads[1], enc_grads[2], enc_grads[3], enc_grads[4], enc_grads[5], enc_grads[6], enc_grads[7], enc_grads[8], enc_grads[9], enc_grads[10], enc_grads[11], bridge_wgrad, bridge_bgrad, dec_grads[0], dec_grads[1], dec_grads[2], dec_grads[3], dec_grads[4], dec_grads[5], dec_grads[6], dec_grads[7], dec_grads[8], dec_grads[9], dec_grads[10], dec_grads[11])
```

```python
from functools import partial

import jax
import jax.numpy as jnp
from jax import lax
from jax.experimental import pallas as pl
from jax.experimental.pallas import tpu as pltpu
from jax.sharding import PartitionSpec as P

HEAD = 64
DHEAD = 32
EPSILON = 1e-06
MESH = pl.DeviceIdType.MESH
F32 = jnp.float32
BF16 = jnp.bfloat16
VMEM_BYTES = 60 * 1024 * 1024


def neighbours():
    dp, mp = lax.axis_index("dp"), lax.axis_index("mp")
    core, x, y = dp % 2, (dp // 2) % 2, dp // 4
    across_core = dp + 1 - 2 * core
    across_x = dp + 2 - 4 * x
    across_y = dp + 4 - 8 * y
    return dp, mp, core, x, y, across_core, across_x, across_y


def entry_barrier(parts):
    mp, across_core, across_x, across_y = parts
    dp = lax.axis_index("dp")
    barrier = pltpu.get_barrier_semaphore()
    planes = lax.axis_size("mp")
    for other in (across_core, across_x, across_y):
        pl.semaphore_signal(barrier, inc=1, device_id=(other, mp), device_id_type=MESH)
    for step in range(1, planes):
        pl.semaphore_signal(
            barrier, inc=1, device_id=(dp, (mp + step) % planes), device_id_type=MESH
        )
    pl.semaphore_wait(barrier, 3 + planes - 1)


def gather_kernel(count, planes, *refs):
    shards, wholes = refs[:count], refs[count : 2 * count]
    local_sem, send_sem, recv_sem = refs[2 * count :]
    dp, mp, core, x, y, across_core, across_x, across_y = neighbours()
    entry_barrier((mp, across_core, across_x, across_y))
    sends = []

    def send(src, dst, m, plane, kind, target, slot=None):
        copy = pltpu.make_async_remote_copy(
            src_ref=src,
            dst_ref=dst,
            send_sem=send_sem.at[m, plane if slot is None else slot, kind],
            recv_sem=recv_sem.at[m, plane, kind],
            device_id=target,
            device_id_type=MESH,
        )
        copy.start()
        sends.append(copy)

    def arrived(m, plane, kind, ref):
        pltpu.make_async_remote_copy(
            src_ref=ref,
            dst_ref=ref,
            send_sem=send_sem.at[m, plane, kind],
            recv_sem=recv_sem.at[m, plane, kind],
            device_id=(across_core, mp),
            device_id_type=MESH,
        ).wait_recv()

    def rows_of(m, owner, half=None):
        piece = shards[m].shape[0] // 8
        if half is None:
            return pl.ds(owner * piece, piece)
        return pl.ds(owner * piece + half * (piece // 2), piece // 2)

    A, X, Y, S, DY, DX, SX, SY, SDY, SDX = range(10)
    others = [(mp + step) % planes for step in range(1, planes)]
    copies = []
    for m in range(count):
        own = rows_of(m, dp)
        for plane in others:
            send(shards[m].at[own], wholes[m].at[mp, own], m, mp, A, (dp, plane), plane)
    for m in range(count):
        copy = pltpu.make_async_copy(shards[m], wholes[m].at[mp], local_sem.at[m])
        copy.start()
        copies.append(copy)

    diag = across_x + across_y - dp

    def stage_b(m):
        own = rows_of(m, dp)
        for plane in others:
            piece = wholes[m].at[plane, own]
            arrived(m, plane, A, piece)
            send(piece, piece, m, plane, X, (across_x, mp))
            send(piece, piece, m, plane, Y, (across_y, mp))
            send(piece, piece, m, plane, S, (across_core, mp))

    def stage_c(m):
        for plane in others:
            piece = wholes[m].at[plane, rows_of(m, across_x)]
            half = wholes[m].at[plane, rows_of(m, across_x, 0)]
            arrived(m, plane, X, piece)
            send(half, half, m, plane, DY, (across_y, mp))
            send(piece, piece, m, plane, SX, (across_core, mp))
            piece = wholes[m].at[plane, rows_of(m, across_y)]
            half = wholes[m].at[plane, rows_of(m, across_y, 1)]
            arrived(m, plane, Y, piece)
            send(half, half, m, plane, DX, (across_x, mp))
            send(piece, piece, m, plane, SY, (across_core, mp))

    def stage_d(m):
        for plane in others:
            half = wholes[m].at[plane, rows_of(m, diag, 0)]
            arrived(m, plane, DY, half)
            send(half, half, m, plane, SDY, (across_core, mp))
            half = wholes[m].at[plane, rows_of(m, diag, 1)]
            arrived(m, plane, DX, half)
            send(half, half, m, plane, SDX, (across_core, mp))

    shift = across_core - dp

    def stage_e(m):
        for plane in others:
            arrived(m, plane, S, wholes[m].at[plane, rows_of(m, across_core)])
            arrived(m, plane, SX, wholes[m].at[plane, rows_of(m, across_x + shift)])
            arrived(m, plane, SY, wholes[m].at[plane, rows_of(m, across_y + shift)])
            arrived(m, plane, SDY, wholes[m].at[plane, rows_of(m, diag + shift, 0)])
            arrived(m, plane, SDX, wholes[m].at[plane, rows_of(m, diag + shift, 1)])

    stages = (stage_b, stage_c, stage_d, stage_e)
    for tick in range(count + len(stages) - 1):
        for late, stage in enumerate(stages):
            if 0 <= tick - late < count:
                stage(tick - late)
    for copy in copies:
        copy.wait()
    for copy in sends:
        copy.wait_send()


def gather_weights(shards, planes):
    count = len(shards)
    kinds = 10
    return pl.pallas_call(
        partial(gather_kernel, count, planes),
        out_shape=[jax.ShapeDtypeStruct((planes,) + s.shape, s.dtype) for s in shards],
        in_specs=[pl.BlockSpec(memory_space=pl.ANY)] * count,
        out_specs=[pl.BlockSpec(memory_space=pl.ANY)] * count,
        scratch_shapes=[
            pltpu.SemaphoreType.DMA((count,)),
            pltpu.SemaphoreType.DMA((count, planes, kinds)),
            pltpu.SemaphoreType.DMA((count, planes, kinds)),
        ],
        compiler_params=pltpu.CompilerParams(
            collective_id=0, has_side_effects=True, vmem_limit_bytes=VMEM_BYTES
        ),
        name="gather_weights",
    )(*shards)


def reduce_kernel(count, planes, *refs):
    parts, sums = refs[:count], refs[count : 2 * count]
    rest = refs[2 * count :]
    mine, from_core, from_x, from_y, then_y, then_x, from_z = (
        rest[k * count : (k + 1) * count] for k in range(7)
    )
    local_sem, send_sem, recv_sem = rest[7 * count :]
    dp, mp, core, x, y, across_core, across_x, across_y = neighbours()
    entry_barrier((mp, across_core, across_x, across_y))
    sends = []
    C, X, Y, XY, YX, Z = range(6)

    def send(src, dst, m, kind, target, send_slot=None, recv_slot=None):
        copy = pltpu.make_async_remote_copy(
            src_ref=src,
            dst_ref=dst,
            send_sem=send_sem.at[m, kind if send_slot is None else send_slot],
            recv_sem=recv_sem.at[m, kind if recv_slot is None else recv_slot],
            device_id=target,
            device_id_type=MESH,
        )
        copy.start()
        sends.append(copy)

    def arrived(m, kind, ref):
        pltpu.make_async_remote_copy(
            src_ref=ref,
            dst_ref=ref,
            send_sem=send_sem.at[m, kind],
            recv_sem=recv_sem.at[m, kind],
            device_id=(across_core, mp),
            device_id_type=MESH,
        ).wait_recv()

    local = []
    for m in range(count):
        copy = pltpu.make_async_copy(parts[m].at[:, :, :, core], mine[m], local_sem.at[m])
        copy.start()
        local.append(copy)
        send(parts[m].at[:, :, :, 1 - core], from_core[m], m, C, (across_core, mp))

    def stage_core(m):
        local[m].wait()
        arrived(m, C, from_core[m])
        half = mine[m].shape[3] // 2

        @pl.loop(0, planes)
        def _(p):
            for b in range(2):
                for a in range(2):
                    mine[m][p, b, a] = mine[m][p, b, a] + from_core[m][p, b, a]

        send(mine[m].at[:, :, 1 - x, pl.ds(0, half)], from_x[m], m, X, (across_x, mp))
        send(mine[m].at[:, 1 - y, :, pl.ds(half, half)], from_y[m], m, Y, (across_y, mp))

    def stage_plane(m):
        half = mine[m].shape[3] // 2
        first, second = pl.ds(0, half), pl.ds(half, half)
        arrived(m, X, from_x[m])

        @pl.loop(0, planes)
        def _(p):
            for b in range(2):
                mine[m][p, b, x, first] = mine[m][p, b, x, first] + from_x[m][p, b]

        send(mine[m].at[:, 1 - y, x, first], then_y[m], m, XY, (across_y, mp))
        arrived(m, Y, from_y[m])

        @pl.loop(0, planes)
        def _(p):
            for a in range(2):
                mine[m][p, y, a, second] = mine[m][p, y, a, second] + from_y[m][p, a]

        send(mine[m].at[:, y, 1 - x, second], then_x[m], m, YX, (across_x, mp))

    def stage_corner(m):
        half = mine[m].shape[3] // 2
        first, second = pl.ds(0, half), pl.ds(half, half)
        arrived(m, XY, then_y[m])
        arrived(m, YX, then_x[m])

        @pl.loop(0, planes)
        def _(p):
            mine[m][p, y, x, first] = mine[m][p, y, x, first] + then_y[m][p]
            mine[m][p, y, x, second] = mine[m][p, y, x, second] + then_x[m][p]

        for step in range(1, planes):
            plane = (mp + step) % planes
            send(
                mine[m].at[plane, y, x],
                from_z[m].at[mp],
                m,
                Z,
                (dp, plane),
                Z + plane,
                Z + mp,
            )

    def stage_line(m):
        total = mine[m][mp, y, x].astype(F32)
        for step in range(1, planes):
            plane = (mp + step) % planes
            arrived(m, Z + plane, from_z[m].at[plane])
            total = total + from_z[m][plane].astype(F32)
        sums[m][...] = total

    stages = (stage_core, stage_plane, stage_corner, stage_line)
    for tick in range(count + len(stages) - 1):
        for late, stage in enumerate(stages):
            if 0 <= tick - late < count:
                stage(tick - late)
    for copy in sends:
        copy.wait_send()


def reduce_gradients(parts, planes):
    count = len(parts)
    shapes = [part.shape[4:] for part in parts]

    def buffers(*lead, halves=False):
        return [
            pltpu.VMEM(lead + (r // 2 if halves else r, c), BF16) for r, c in shapes
        ]

    return pl.pallas_call(
        partial(reduce_kernel, count, planes),
        out_shape=[jax.ShapeDtypeStruct(s, F32) for s in shapes],
        in_specs=[pl.BlockSpec(memory_space=pl.ANY)] * count,
        out_specs=[pl.BlockSpec(memory_space=pltpu.VMEM)] * count,
        scratch_shapes=buffers(planes, 2, 2)
        + buffers(planes, 2, 2)
        + buffers(planes, 2, halves=True)
        + buffers(planes, 2, halves=True)
        + buffers(planes, halves=True)
        + buffers(planes, halves=True)
        + buffers(planes)
        + [
            pltpu.SemaphoreType.DMA((count,)),
            pltpu.SemaphoreType.DMA((count, 5 + planes)),
            pltpu.SemaphoreType.DMA((count, 5 + planes)),
        ],
        compiler_params=pltpu.CompilerParams(
            collective_id=1, has_side_effects=True, vmem_limit_bytes=VMEM_BYTES
        ),
        name="reduce_gradients",
    )(*parts)


def spread(shards, sizes):
    planes = sizes["mp"]
    if sizes["dp"] == 8:
        return gather_weights(shards, planes)
    return [lax.all_gather(s, "mp", axis=0) for s in shards]


def collect(parts, sizes):
    planes = sizes["mp"]
    if sizes["dp"] == 8:
        return reduce_gradients(
            [p.reshape((planes, 2, 2, 2) + p.shape[2:]) for p in parts], planes
        )
    sums = []
    for part in parts:
        part = lax.psum_scatter(part, "mp", scatter_dimension=0, tiled=False)
        sums.append(lax.psum_scatter(part.astype(F32), "dp", scatter_dimension=0, tiled=False))
    return sums


def attention_forward_kernel(head_dim, length_ref, triple_ref, out_ref, logsum_ref):
    rows, width = triple_ref.shape[0], triple_ref.shape[1] // 3
    visible = lax.broadcasted_iota(jnp.int32, (1, rows), 1) < length_ref[0]
    for head in range(width // head_dim):
        low = head * head_dim
        query = triple_ref[:, low : low + head_dim]
        key = triple_ref[:, width + low : width + low + head_dim]
        value = triple_ref[:, 2 * width + low : 2 * width + low + head_dim]
        scores = lax.dot_general(
            query, key, (((1,), (1,)), ((), ())), preferred_element_type=F32
        ) * head_dim ** (-0.5)
        scores = jnp.where(visible, scores, -1e30)
        ceiling = jnp.max(scores, -1, keepdims=True)
        exponent = jnp.exp(scores - ceiling)
        denominator = jnp.sum(exponent, -1, keepdims=True)
        chances = (exponent / denominator).astype(BF16)
        attended = jnp.dot(chances, value, preferred_element_type=F32)
        out_ref[:, low : low + head_dim] = attended.astype(BF16)
        logsum_ref[:, head : head + 1] = ceiling + jnp.log(denominator)


def attention_backward_kernel(
    head_dim, length_ref, triple_ref, attended_ref, mixed_ref, logsum_ref, out_ref
):
    rows, width = triple_ref.shape[0], triple_ref.shape[1] // 3
    factor = head_dim ** (-0.5)
    visible = lax.broadcasted_iota(jnp.int32, (1, rows), 1) < length_ref[0]
    for head in range(width // head_dim):
        low = head * head_dim
        query = triple_ref[:, low : low + head_dim]
        key = triple_ref[:, width + low : width + low + head_dim]
        value = triple_ref[:, 2 * width + low : 2 * width + low + head_dim]
        mixed = mixed_ref[:, low : low + head_dim]
        attended = attended_ref[:, low : low + head_dim]
        scores = (
            lax.dot_general(query, key, (((1,), (1,)), ((), ())), preferred_element_type=F32)
            * factor
        )
        scores = jnp.where(visible, scores, -1e30)
        chances = jnp.exp(scores - logsum_ref[:, head : head + 1])
        chance_grad = lax.dot_general(
            mixed, value, (((1,), (1,)), ((), ())), preferred_element_type=F32
        )
        row_sums = jnp.sum(mixed.astype(F32) * attended.astype(F32), -1, keepdims=True)
        score_grad = (chances * (chance_grad - row_sums)).astype(BF16)
        query_grad = jnp.dot(score_grad, key, preferred_element_type=F32) * factor
        key_grad = (
            lax.dot_general(
                score_grad, query, (((0,), (0,)), ((), ())), preferred_element_type=F32
            )
            * factor
        )
        value_grad = lax.dot_general(
            chances.astype(BF16), mixed, (((0,), (0,)), ((), ())), preferred_element_type=F32
        )
        out_ref[:, low : low + head_dim] = query_grad.astype(BF16)
        out_ref[:, width + low : width + low + head_dim] = key_grad.astype(BF16)
        out_ref[:, 2 * width + low : 2 * width + low + head_dim] = value_grad.astype(BF16)


def plane_spec(*shape):
    return pl.BlockSpec((None,) + shape, lambda p: (p, 0, 0))


LENGTH_SPEC = pl.BlockSpec(memory_space=pltpu.SMEM)


def attention_forward(triple, length, head_dim):
    planes, rows, width = triple.shape
    width //= 3
    heads = width // head_dim
    return pl.pallas_call(
        partial(attention_forward_kernel, head_dim),
        grid=(planes,),
        out_shape=[
            jax.ShapeDtypeStruct((planes, rows, width), BF16),
            jax.ShapeDtypeStruct((planes, rows, heads), F32),
        ],
        in_specs=[LENGTH_SPEC, plane_spec(rows, 3 * width)],
        out_specs=[plane_spec(rows, width), plane_spec(rows, heads)],
        compiler_params=pltpu.CompilerParams(vmem_limit_bytes=VMEM_BYTES),
        name="attention_forward",
    )(length, triple)


def attention_backward(triple, attended, mixed, logsum, length, head_dim):
    planes, rows, width = attended.shape
    heads = width // head_dim
    return pl.pallas_call(
        partial(attention_backward_kernel, head_dim),
        grid=(planes,),
        out_shape=jax.ShapeDtypeStruct((planes, rows, 3 * width), BF16),
        in_specs=[
            LENGTH_SPEC,
            plane_spec(rows, 3 * width),
            plane_spec(rows, width),
            plane_spec(rows, width),
            plane_spec(rows, heads),
        ],
        out_specs=plane_spec(rows, 3 * width),
        compiler_params=pltpu.CompilerParams(vmem_limit_bytes=VMEM_BYTES),
        name="attention_backward",
    )(length, triple, attended, mixed, logsum)


def normalize(stream, gain_vector, shift_vector):
    centered = stream - jnp.mean(stream, -1, keepdims=True)
    variance = jnp.mean(centered * centered, -1, keepdims=True)
    return centered * lax.rsqrt(variance + EPSILON) * gain_vector + shift_vector


def layer_back(stream, gain_vector, shift_vector, upstream):
    unused, pullback = jax.vjp(normalize, stream, gain_vector, shift_vector)
    return pullback(upstream)


def gelu_exact(inputs):
    return jax.nn.gelu(inputs, approximate=False)


def mm(spec, left, right):
    return jnp.einsum(spec, left, right, preferred_element_type=F32)


def block_forward(stream, params, weights, length, head_dim):
    (gain, shift, head_bias, output_bias, feed_gain, feed_shift, up_bias, down_bias) = params
    attn, up, down = weights
    planes, width = attn.shape[0], attn.shape[2] // 4
    normed = normalize(stream, gain, shift).astype(BF16)
    bias = jnp.concatenate([head_bias[0], jnp.zeros_like(head_bias[0]), head_bias[1]], -1)
    triple = mm("td,zde->zte", normed, attn[:, :, : 3 * width])
    triple = (triple + bias[:, None]).astype(BF16)
    attended, logsum = attention_forward(triple, length, head_dim)
    middle = stream + (mm("zte,zde->td", attended, attn[:, :, 3 * width :]) + output_bias)
    feed_input = normalize(middle, feed_gain, feed_shift).astype(BF16)
    before = mm("td,zdf->ztf", feed_input, up) + up_bias[:, None]
    hidden = gelu_exact(before).astype(BF16)
    result = middle + (mm("ztf,zfd->td", hidden, down) + down_bias)
    return result, (stream, normed, triple, logsum, attended, middle, feed_input, before, hidden)


def column_sums(values):
    return jnp.sum(values.astype(F32), -2)


def block_backward(upstream, params, weights, stored, length, head_dim):
    (gain, shift, head_bias, output_bias, feed_gain, feed_shift, up_bias, down_bias) = params
    attn, up, down = weights
    stream, normed, triple, logsum, attended, middle, feed_input, before, hidden = stored
    planes, width = attn.shape[0], attn.shape[2] // 4
    branch_grad = upstream.astype(BF16)
    down_bias_grad = column_sums(branch_grad)
    down_grad = mm("td,ztf->zdf", branch_grad, hidden).astype(BF16)
    hidden_grad = mm("td,zfd->ztf", branch_grad, down)
    unused, gelu_pull = jax.vjp(gelu_exact, before)
    before_grad = gelu_pull(hidden_grad)[0].astype(BF16)
    up_bias_grad = column_sums(before_grad)
    up_grad = mm("td,ztf->zdf", feed_input, before_grad).astype(BF16)
    feed_rows = mm("ztf,zdf->td", before_grad, up)
    middle_part, feed_gain_grad, feed_shift_grad = layer_back(
        middle, feed_gain, feed_shift, feed_rows
    )
    middle_grad = upstream + middle_part
    attn_grad = middle_grad.astype(BF16)
    output_bias_grad = column_sums(attn_grad)
    output_grad = mm("td,zte->zde", attn_grad, attended)
    mixed_grad = mm("td,zde->zte", attn_grad, attn[:, :, 3 * width :]).astype(BF16)
    triple_grad = attention_backward(triple, attended, mixed_grad, logsum, length, head_dim)
    triple_sums = column_sums(triple_grad)
    head_bias_grad = jnp.stack([triple_sums[:, :width], triple_sums[:, 2 * width :]])
    triple_weight_grad = mm("td,zte->zde", normed, triple_grad)
    attn_weight_grad = jnp.concatenate([triple_weight_grad, output_grad], -1).astype(BF16)
    input_rows = mm("zte,zde->td", triple_grad, attn[:, :, : 3 * width])
    stream_part, gain_grad, shift_grad = layer_back(stream, gain, shift, input_rows)
    vectors = (
        gain_grad,
        shift_grad,
        output_bias_grad,
        feed_gain_grad,
        feed_shift_grad,
        down_bias_grad,
    )
    return middle_grad + stream_part, (attn_weight_grad, up_grad, down_grad), vectors, (
        head_bias_grad,
        up_bias_grad,
    )


def shards(sizes, *inputs):
    patches, lengths = inputs[:2]
    cotangent = inputs[28]
    planes, groups = sizes["mp"], sizes["dp"]
    mp = lax.axis_index("mp")
    length = lax.dynamic_slice_in_dim(lengths, mp, 1)

    def block_of(at):
        (gain, shift, proj, head_bias, out, out_bias, f_gain, f_shift, up, up_bias, down, d_bias) = (
            inputs[at : at + 12]
        )
        packed = jnp.concatenate([proj[0], proj[1], proj[2], out.T], -1)
        vectors = (gain, shift, out_bias, f_gain, f_shift, d_bias)
        return (packed, up, down), vectors, (head_bias, up_bias)

    enc_shards, enc_vectors, enc_split = block_of(2)
    bridge_weight, bridge_bias = inputs[14:16]
    dec_shards, dec_vectors, dec_split = block_of(16)
    wholes = spread(enc_shards + dec_shards, sizes)
    small = jnp.concatenate([v.reshape(-1) for v in enc_split + dec_split])
    small = lax.all_gather(small, "mp", axis=0)

    def params_of(vectors, split, at):
        gain, shift, out_bias, f_gain, f_shift, d_bias = vectors
        width, hidden = split[0].shape[1], split[1].shape[0]
        head_bias = small[:, at : at + 2 * width].reshape(planes, 2, width).transpose(1, 0, 2)
        up_bias = small[:, at + 2 * width : at + 2 * width + hidden]
        return (gain, shift, head_bias, out_bias, f_gain, f_shift, up_bias, d_bias)

    encoder = params_of(enc_vectors, enc_split, 0)
    decoder = params_of(dec_vectors, dec_split, 2 * enc_split[0].shape[1] + enc_split[1].shape[0])

    rows = patches.shape[0]
    padded = -(-rows // 32) * 32
    stream = jnp.pad(patches, ((0, padded - rows), (0, 0))).astype(F32)
    upstream = jnp.pad(cotangent, ((0, padded - rows), (0, 0))).astype(F32)

    encoded, enc_stored = block_forward(stream, encoder, wholes[:3], length, HEAD)
    bridge_input = encoded.astype(BF16)
    bridged = mm("td,de->te", bridge_input, bridge_weight) + bridge_bias
    decoded, dec_stored = block_forward(bridged, decoder, wholes[3:], length, DHEAD)
    bridged_grad, dec_mats, dec_vecs, dec_splits = block_backward(
        upstream, decoder, wholes[3:], dec_stored, length, DHEAD
    )
    bridge_rows = bridged_grad.astype(BF16)
    bridge_weight_grad = mm("td,te->de", bridge_input, bridge_rows)
    bridge_bias_grad = column_sums(bridge_rows)
    encoded_grad = mm("te,de->td", bridge_rows, bridge_weight)
    patches_grad, enc_mats, enc_vecs, enc_splits = block_backward(
        encoded_grad, encoder, wholes[:3], enc_stored, length, HEAD
    )

    def by_group(vector):
        return vector.reshape(groups, planes, -1).transpose(1, 0, 2)

    def by_plane(vector):
        return vector.reshape(planes, groups, -1)

    pieces = [by_group(v) for v in enc_vecs + dec_vecs + (bridge_bias_grad,)]
    for head_bias_grad, up_bias_grad in (enc_splits, dec_splits):
        pieces += [by_plane(head_bias_grad[0]), by_plane(head_bias_grad[1]), by_plane(up_bias_grad)]
    lengths_of = [p.shape[-1] for p in pieces]
    packed = jnp.concatenate(pieces, -1)
    wide = bridge_weight.shape[1]
    bridge_part = bridge_weight_grad.reshape(groups, planes, -1, wide).transpose(1, 0, 2, 3)
    deep = bridge_part.shape[2]
    lines = -(-packed.shape[-1] // wide)
    packed = jnp.pad(packed, ((0, 0), (0, 0), (0, lines * wide - packed.shape[-1])))
    packed = packed.reshape(planes, groups, lines, wide)
    spare = -(deep + lines) % 32
    misc = jnp.concatenate(
        [bridge_part, packed, jnp.zeros((planes, groups, spare, wide), F32)], 2
    ).astype(BF16)

    def in_groups(grad):
        return grad.reshape(planes, groups, -1, grad.shape[-1])

    sums = collect([in_groups(g) for g in enc_mats + dec_mats] + [misc], sizes)
    misc_sum = sums[6]
    bridge_out = misc_sum[:deep]
    flat = misc_sum[deep : deep + lines].reshape(-1)
    taken, at = [], 0
    for size in lengths_of:
        taken.append(flat[at : at + size])
        at += size

    def block_out(mats, vectors, splits):
        attn, up, down = mats
        width = attn.shape[1] // 4
        proj = attn[:, : 3 * width].reshape(-1, 3, width).transpose(1, 0, 2)
        gain, shift, out_bias, f_gain, f_shift, d_bias = vectors
        head_bias = jnp.stack([splits[0], splits[1]])
        return (
            gain,
            shift,
            proj,
            head_bias,
            attn[:, 3 * width :].T,
            out_bias,
            f_gain,
            f_shift,
            up,
            splits[2],
            down.T,
            d_bias,
        )

    enc_out = block_out(sums[0:3], taken[0:6], taken[13:16])
    dec_out = block_out(sums[3:6], taken[6:12], taken[16:19])
    return (
        (decoded[:rows].astype(BF16), patches_grad[:rows].astype(BF16))
        + enc_out
        + (bridge_out, taken[12])
        + dec_out
    )


def solution(mesh):
    block_in = (
        P(),
        P(),
        P(None, None, "mp"),
        P(None, "mp"),
        P("mp", None),
        P(),
        P(),
        P(),
        P(None, "mp"),
        P("mp"),
        P("mp", None),
        P(),
    )
    both = P(("dp", "mp"))
    block_out = (
        both,
        both,
        P(None, "dp", "mp"),
        P(None, ("mp", "dp")),
        P("mp", "dp"),
        both,
        both,
        both,
        P("dp", "mp"),
        P(("mp", "dp")),
        P("mp", "dp"),
        both,
    )
    rows = P(("dp", "mp"), None)
    return jax.shard_map(
        partial(shards, dict(mesh.shape)),
        mesh=mesh,
        in_specs=(rows, P("dp")) + block_in + (P(), P()) + block_in + (rows,),
        out_specs=(rows, rows) + block_out + (rows, both) + block_out,
        check_vma=False,
    )
```

```python
from functools import partial

import jax
import jax.numpy as jnp
from jax import lax
from jax.experimental import pallas as pl
from jax.experimental.pallas import tpu as pltpu
from jax.sharding import PartitionSpec as P

HEAD = 64
DHEAD = 32
EPSILON = 1e-06
MESH = pl.DeviceIdType.MESH
F32 = jnp.float32
BF16 = jnp.bfloat16
VMEM_BYTES = 60 * 1024 * 1024


def neighbours():
    dp, mp = lax.axis_index("dp"), lax.axis_index("mp")
    core, x, y = dp % 2, (dp // 2) % 2, dp // 4
    across_core = dp + 1 - 2 * core
    across_x = dp + 2 - 4 * x
    across_y = dp + 4 - 8 * y
    return dp, mp, core, x, y, across_core, across_x, across_y


def entry_barrier(parts):
    mp, across_core, across_x, across_y = parts
    dp = lax.axis_index("dp")
    barrier = pltpu.get_barrier_semaphore()
    planes = lax.axis_size("mp")
    for other in (across_core, across_x, across_y):
        pl.semaphore_signal(barrier, inc=1, device_id=(other, mp), device_id_type=MESH)
    for step in range(1, planes):
        pl.semaphore_signal(
            barrier, inc=1, device_id=(dp, (mp + step) % planes), device_id_type=MESH
        )
    pl.semaphore_wait(barrier, 3 + planes - 1)


def plane_order(mp, planes):
    if planes != 4:
        return [(mp + step) % planes for step in range(1, planes)]
    upper = mp // 2
    place = mp + upper * (3 - 2 * mp)
    return [o + upper * (3 - 2 * o) for o in (place + 1, 2 - 2 * place, 3)]


def gather_kernel(count, planes, *refs):
    shards, small = refs[:count], refs[count]
    wholes, smalls = refs[count + 1 : 2 * count + 1], refs[2 * count + 1]
    holds = refs[2 * count + 2 : 3 * count + 2]
    local_sem, send_sem, recv_sem = refs[3 * count + 2 :]
    dp, mp, core, x, y, across_core, across_x, across_y = neighbours()
    entry_barrier((mp, across_core, across_x, across_y))
    diag = across_x + across_y - dp
    shift = across_core - dp
    others = plane_order(mp, planes)
    A, X, Y, S, DY, DX, SX, SY, SDY, SDX = range(10)
    sends = []

    def send(src, dst, m, plane, kind, target, slot=None):
        copy = pltpu.make_async_remote_copy(
            src_ref=src,
            dst_ref=dst,
            send_sem=send_sem.at[m, plane if slot is None else slot, kind],
            recv_sem=recv_sem.at[m, plane, kind],
            device_id=target,
            device_id_type=MESH,
        )
        copy.start()
        sends.append(copy)

    def arrived(m, plane, kind, ref):
        pltpu.make_async_remote_copy(
            src_ref=ref,
            dst_ref=ref,
            send_sem=send_sem.at[m, plane, kind],
            recv_sem=recv_sem.at[m, plane, kind],
            device_id=(across_core, mp),
            device_id_type=MESH,
        ).wait_recv()

    def rows_of(m, owner, half=None):
        piece = shards[m].shape[0] // 8
        if half is None:
            return pl.ds(owner * piece, piece)
        return pl.ds(owner * piece + half * (piece // 2), piece // 2)

    def along_z(m, i):
        own, plane = rows_of(m, dp), others[i]
        send(shards[m].at[own], wholes[m].at[mp, own], m, mp, A, (dp, plane), plane)

    def to_plane(m, i):
        plane = others[i]
        piece = wholes[m].at[plane, rows_of(m, dp)]
        arrived(m, plane, A, piece)
        send(piece, piece, m, plane, X, (across_x, mp))
        send(piece, piece, m, plane, Y, (across_y, mp))
        send(piece, piece, m, plane, S, (across_core, mp))

    def to_corner(m, i):
        plane = others[i]
        piece = wholes[m].at[plane, rows_of(m, across_x)]
        half = wholes[m].at[plane, rows_of(m, across_x, 0)]
        arrived(m, plane, X, piece)
        send(half, half, m, plane, DY, (across_y, mp))
        send(piece, piece, m, plane, SX, (across_core, mp))
        piece = wholes[m].at[plane, rows_of(m, across_y)]
        half = wholes[m].at[plane, rows_of(m, across_y, 1)]
        arrived(m, plane, Y, piece)
        send(half, half, m, plane, DX, (across_x, mp))
        send(piece, piece, m, plane, SY, (across_core, mp))

    def to_core(m, i):
        plane = others[i]
        half = wholes[m].at[plane, rows_of(m, diag, 0)]
        arrived(m, plane, DY, half)
        send(half, half, m, plane, SDY, (across_core, mp))
        half = wholes[m].at[plane, rows_of(m, diag, 1)]
        arrived(m, plane, DX, half)
        send(half, half, m, plane, SDX, (across_core, mp))

    def whole(m, i):
        plane = others[i]
        arrived(m, plane, S, wholes[m].at[plane, rows_of(m, across_core)])
        arrived(m, plane, SX, wholes[m].at[plane, rows_of(m, across_x + shift)])
        arrived(m, plane, SY, wholes[m].at[plane, rows_of(m, across_y + shift)])
        arrived(m, plane, SDY, wholes[m].at[plane, rows_of(m, diag + shift, 0)])
        arrived(m, plane, SDX, wholes[m].at[plane, rows_of(m, diag + shift, 1)])

    for i in range(planes - 1):
        send(small, smalls.at[mp], count, mp, A, (dp, others[i]), others[i])
    own_small = pltpu.make_async_copy(small, smalls.at[mp], local_sem.at[count])
    own_small.start()
    held = []
    for m in range(count):
        copy = pltpu.make_async_copy(shards[m], holds[m], local_sem.at[m])
        copy.start()
        held.append(copy)
    units = [(m, i) for m in range(count) for i in range(planes - 1)]
    lag, ahead = 2, 6
    stages = (
        (0, along_z),
        (ahead, to_plane),
        (ahead + lag, to_corner),
        (ahead + 2 * lag, to_core),
        (ahead + 3 * lag, whole),
    )
    for tick in range(len(units) + ahead + 3 * lag):
        if tick == ahead:
            for m in range(count):
                held[m].wait()
                held[m] = pltpu.make_async_copy(holds[m], wholes[m].at[mp], local_sem.at[m])
                held[m].start()
        for late, stage in stages:
            if 0 <= tick - late < len(units):
                stage(*units[tick - late])
    for i in range(planes - 1):
        arrived(count, others[i], A, smalls.at[others[i]])
    for copy in held + [own_small]:
        copy.wait()
    for copy in sends:
        copy.wait_send()


def gather_weights(shards, small, planes):
    count = len(shards)
    kinds = 10
    everything = list(shards) + [small]
    return pl.pallas_call(
        partial(gather_kernel, count, planes),
        out_shape=[jax.ShapeDtypeStruct((planes,) + s.shape, s.dtype) for s in everything],
        in_specs=[pl.BlockSpec(memory_space=pl.ANY)] * (count + 1),
        out_specs=[pl.BlockSpec(memory_space=pl.ANY)] * (count + 1),
        scratch_shapes=[pltpu.VMEM(s.shape, s.dtype) for s in shards]
        + [
            pltpu.SemaphoreType.DMA((count + 1,)),
            pltpu.SemaphoreType.DMA((count + 1, planes, kinds)),
            pltpu.SemaphoreType.DMA((count + 1, planes, kinds)),
        ],
        compiler_params=pltpu.CompilerParams(
            collective_id=0, has_side_effects=True, vmem_limit_bytes=VMEM_BYTES
        ),
        name="gather_weights",
    )(*everything)


class Reducer:
    def __init__(self, shapes, planes, refs):
        self.planes, self.count = planes, len(shapes)
        refs = list(refs)
        take = lambda: [refs.pop(0) for _ in range(self.count)]
        self.mine, self.from_core, self.from_x, self.from_y = take(), take(), take(), take()
        self.then_y, self.then_x, self.from_z = take(), take(), take()
        self.local_sem, self.send_sem, self.recv_sem = refs
        self.dp, self.mp, self.core_id, self.x, self.y, *across = neighbours()
        self.across_core, self.across_x, self.across_y = across
        self.halves = [rows // 2 for rows, columns in shapes]
        self.parts = [None] * self.count

    @staticmethod
    def scratch(shapes, planes, resident=()):
        count = len(shapes)

        def buffers(*lead, halves=False, skip=()):
            return [
                pltpu.VMEM((1, 16, 128), BF16)
                if m in skip
                else pltpu.VMEM(lead + (r // 2 if halves else r, c), BF16)
                for m, (r, c) in enumerate(shapes)
            ]

        return (
            buffers(planes, 2, 2, skip=resident)
            + buffers(planes, 2, 2)
            + buffers(planes, 2, halves=True)
            + buffers(planes, 2, halves=True)
            + buffers(planes, halves=True)
            + buffers(planes, halves=True)
            + buffers(planes)
            + [
                pltpu.SemaphoreType.DMA((count, planes)),
                pltpu.SemaphoreType.DMA((count, planes, 6)),
                pltpu.SemaphoreType.DMA((count, planes, 6)),
            ]
        )

    def remote(self, m, p, kind, src, dst, target, recv_plane=None):
        return pltpu.make_async_remote_copy(
            src_ref=src,
            dst_ref=dst,
            send_sem=self.send_sem.at[m, p, kind],
            recv_sem=self.recv_sem.at[m, p if recv_plane is None else recv_plane, kind],
            device_id=target,
            device_id_type=MESH,
        )

    def own(self, m, p, b, a):
        if self.resident(m):
            return self.parts[m].at[p, b, a, self.core_id]
        return self.mine[m].at[p, b, a]

    def owned(self, m, p, b, a, rows):
        if self.resident(m):
            return self.parts[m].at[p, b, a, self.core_id, rows]
        return self.mine[m].at[p, b, a, rows]

    def resident(self, m):
        return self.mine[m].shape[0] == 1

    def begin(self, m, p):
        if not self.resident(m):
            pltpu.make_async_copy(
                self.parts[m].at[p, :, :, self.core_id], self.mine[m].at[p], self.local_sem.at[m, p]
            ).start()
        self.to_core(m, p).start()

    def to_core(self, m, p):
        return self.remote(
            m,
            p,
            0,
            self.parts[m].at[p, :, :, 1 - self.core_id],
            self.from_core[m].at[p],
            (self.across_core, self.mp),
        )

    def to_x(self, m, p):
        src = self.owned(m, p, slice(None), 1 - self.x, pl.ds(0, self.halves[m]))
        return self.remote(m, p, 1, src, self.from_x[m].at[p], (self.across_x, self.mp))

    def to_y(self, m, p):
        half = self.halves[m]
        src = self.owned(m, p, 1 - self.y, slice(None), pl.ds(half, half))
        return self.remote(m, p, 2, src, self.from_y[m].at[p], (self.across_y, self.mp))

    def x_to_y(self, m, p):
        src = self.owned(m, p, 1 - self.y, self.x, pl.ds(0, self.halves[m]))
        return self.remote(m, p, 3, src, self.then_y[m].at[p], (self.across_y, self.mp))

    def y_to_x(self, m, p):
        half = self.halves[m]
        src = self.owned(m, p, self.y, 1 - self.x, pl.ds(half, half))
        return self.remote(m, p, 4, src, self.then_x[m].at[p], (self.across_x, self.mp))

    def to_z(self, m, p):
        src = self.own(m, p, self.y, self.x)
        return self.remote(m, p, 5, src, self.from_z[m].at[self.mp], (self.dp, p), self.mp)

    def core(self, m, p):
        if not self.resident(m):
            pltpu.make_async_copy(
                self.parts[m].at[p, :, :, self.core_id], self.mine[m].at[p], self.local_sem.at[m, p]
            ).wait()
        self.to_core(m, p).wait_recv()
        for b in range(2):
            for a in range(2):
                ref = self.own(m, p, b, a)
                ref[...] = ref[...] + self.from_core[m][p, b, a]
        self.to_x(m, p).start()
        self.to_y(m, p).start()

    def plane(self, m, p):
        half = self.halves[m]
        self.to_x(m, p).wait_recv()
        for b in range(2):
            ref = self.owned(m, p, b, self.x, pl.ds(0, half))
            ref[...] = ref[...] + self.from_x[m][p, b]
        self.x_to_y(m, p).start()
        self.to_y(m, p).wait_recv()
        for a in range(2):
            ref = self.owned(m, p, self.y, a, pl.ds(half, half))
            ref[...] = ref[...] + self.from_y[m][p, a]
        self.y_to_x(m, p).start()

    def corner(self, m, p):
        half = self.halves[m]
        self.x_to_y(m, p).wait_recv()
        self.y_to_x(m, p).wait_recv()
        ref = self.owned(m, p, self.y, self.x, pl.ds(0, half))
        ref[...] = ref[...] + self.then_y[m][p]
        ref = self.owned(m, p, self.y, self.x, pl.ds(half, half))
        ref[...] = ref[...] + self.then_x[m][p]

        @pl.when(p != self.mp)
        def _():
            self.to_z(m, p).start()

    def finish(self, m, out):
        total = self.own(m, self.mp, self.y, self.x)[...].astype(F32)
        for step in range(1, self.planes):
            plane = (self.mp + step) % self.planes
            src = self.from_z[m].at[plane]
            self.remote(m, plane, 5, src, src, (self.dp, plane)).wait_recv()
            total = total + src[...].astype(F32)
        out[...] = total

    def drain(self):
        @pl.loop(0, self.planes)
        def _(p):
            for m in range(self.count):
                for copy in (self.to_core, self.to_x, self.to_y, self.x_to_y, self.y_to_x):
                    copy(m, p).wait_send()

                @pl.when(p != self.mp)
                def _():
                    self.to_z(m, p).wait_send()


def spread(shards, small, sizes):
    planes = sizes["mp"]
    if sizes["dp"] == 8:
        lines = -(-small.shape[0] // 1024) * 8
        small = jnp.pad(small, (0, lines * 128 - small.shape[0])).reshape(lines, 128)
        return gather_weights(shards, small, planes)
    return [lax.all_gather(s, "mp", axis=0) for s in shards + (small,)]


def collect(part, sizes):
    part = lax.psum_scatter(part, "mp", scatter_dimension=0, tiled=False)
    return lax.psum_scatter(part.astype(F32), "dp", scatter_dimension=0, tiled=False)


LOG2E = 1.4426950408889634
ROW_BLOCK = 32
NT = (((1,), (1,)), ((), ()))


def dot(left, right, dims=(((1,), (0,)), ((), ()))):
    return lax.dot_general(left, right, dims, preferred_element_type=F32)


def standardize(x):
    centered = x - jnp.mean(x, -1, keepdims=True)
    scale = lax.rsqrt(jnp.mean(centered * centered, -1, keepdims=True) + EPSILON)
    return centered * scale, scale


def gelu_and_slope(b):
    cdf = 0.5 * (1.0 + lax.erf(b * 0.7071067811865476))
    density = jnp.exp(-0.5 * b * b) * 0.3989422804014327
    return b * cdf, cdf + b * density


def fold_rows(x):
    return jnp.sum(x.reshape(x.shape[0] // 8, 8, x.shape[1]), 0)


def row_blocks(rows):
    return pl.loop(0, rows // ROW_BLOCK)


def block_at(i):
    return pl.ds(pl.multiple_of(i * ROW_BLOCK, ROW_BLOCK), ROW_BLOCK)


def strip_forward(head_dim, length, p, triple, attended, logsum):
    rows, width = triple.shape[1], triple.shape[2] // 3
    visible = lax.broadcasted_iota(jnp.int32, (rows, 1), 0) < length
    factor = head_dim**-0.5 * LOG2E
    outs = []
    for head in range(width // head_dim):
        low = head * head_dim
        query = triple[p, :, low : low + head_dim]
        key = triple[p, :, width + low : width + low + head_dim]
        value = triple[p, :, 2 * width + low : 2 * width + low + head_dim]
        scores = jnp.where(visible, dot(key, query, NT) * factor, -1e30)
        ceiling = jnp.max(scores, 0, keepdims=True)
        exponent = jnp.exp2(scores - ceiling)
        denominator = jnp.sum(exponent, 0, keepdims=True)
        outs.append(dot(value.T, exponent.astype(BF16)) * (1.0 / denominator))
        logsum[p, head : head + 1, :] = ceiling + jnp.log2(denominator)
    attended[p] = jnp.concatenate(outs, 0).T.astype(BF16)


def strip_backward(head_dim, length, p, triple, attended, mixed, logsum, out):
    rows, width = triple.shape[1], triple.shape[2] // 3
    visible = lax.broadcasted_iota(jnp.int32, (rows, 1), 0) < length
    factor = head_dim**-0.5
    products = (mixed.astype(F32) * attended[p].astype(F32)).T
    query_grads = []
    for head in range(width // head_dim):
        low = head * head_dim
        query = triple[p, :, low : low + head_dim]
        key = triple[p, :, width + low : width + low + head_dim]
        value = triple[p, :, 2 * width + low : 2 * width + low + head_dim]
        mixed_head = mixed[:, low : low + head_dim]
        row_sums = jnp.sum(products[low : low + head_dim], 0, keepdims=True)
        scores = dot(key, query, NT) * (factor * LOG2E) - logsum[p, head : head + 1, :]
        chances = jnp.exp2(jnp.where(visible, scores, -1e30))
        chance_grad = dot(value, mixed_head, NT)
        score_grad = (chances * (chance_grad - row_sums)).astype(BF16)
        key_grad = dot(score_grad, query) * factor
        value_grad = dot(chances.astype(BF16), mixed_head)
        query_grads.append(dot(key.T, score_grad) * factor)
        out[:, width + low : width + low + head_dim] = key_grad.astype(BF16)
        out[:, 2 * width + low : 2 * width + low + head_dim] = value_grad.astype(BF16)
    out[:, :width] = jnp.concatenate(query_grads, 0).T.astype(BF16)


def attn_forward(head_dim, length, stream, weight, gain, shift, bias, out_bias, outs):
    normed, triple, attended, logsum, middle = outs
    planes, rows = triple.shape[:2]
    width = attended.shape[2]

    @row_blocks(rows)
    def _(i):
        x = stream[block_at(i), :].astype(F32)
        normed[block_at(i), :] = (standardize(x)[0] * gain[...] + shift[...]).astype(BF16)
        middle[block_at(i), :] = x + out_bias[...]

    @pl.loop(0, planes)
    def _(p):
        triple[p] = (dot(normed[...], weight[p, :, : 3 * width]) + bias[p]).astype(BF16)
        strip_forward(head_dim, length, p, triple, attended, logsum)
        middle[...] += dot(attended[p], weight[p, :, 3 * width :], NT)


def feed_forward(middle, up, down, up_bias, gain, shift, down_bias, outs, total):
    feed_input, hidden, slope = outs
    planes, rows, width = hidden.shape

    @row_blocks(rows)
    def _(i):
        x = middle[block_at(i), :]
        feed_input[block_at(i), :] = (standardize(x)[0] * gain[...] + shift[...]).astype(BF16)
        total[block_at(i), :] = x + down_bias[...]

    @pl.loop(0, planes)
    def _(p):
        for low in range(0, width, 256):
            part = slice(low, low + 256)
            before = dot(feed_input[...], up[p, :, part]) + up_bias[p, :, part]
            activated, rise = gelu_and_slope(before)
            hidden[p, :, part] = activated.astype(BF16)
            slope[p, :, part] = rise.astype(BF16)
        total[...] += dot(hidden[p], down[p])


def layer_backward(stream, gain, upstream, spare, gain_sums, shift_sums):
    gain_sums[...] = jnp.zeros_like(gain_sums)
    shift_sums[...] = jnp.zeros_like(shift_sums)

    @row_blocks(stream.shape[0])
    def _(i):
        hat, scale = standardize(stream[block_at(i), :].astype(F32))
        grad = spare[block_at(i), :]
        gain_sums[...] += fold_rows(grad * hat)
        shift_sums[...] += fold_rows(grad)
        grad = grad * gain[...]
        part = grad - jnp.mean(grad, -1, keepdims=True)
        part = part - hat * jnp.mean(grad * hat, -1, keepdims=True)
        spare[block_at(i), :] = upstream[block_at(i), :].astype(F32) + part * scale


def put_transposed(values, turned):
    columns = values.shape[1]
    turned[:columns, :] = values.T
    turned[columns:, :] = jnp.ones((16, values.shape[0]), BF16)


def feed_backward(upstream, saved, weights, gain, outs, scratch, hook):
    hidden, slope, feed_input, middle = saved
    up, down = weights
    down_grad, up_grad, up_sums, middle_grad, branch_sums, gain_sums, shift_sums = outs
    branch, branch_turned, feed_turned = scratch
    planes, rows, width = hidden.ref.shape
    wide = branch.shape[1]
    branch_sums[...] = jnp.zeros_like(branch_sums)
    upstream = upstream.use()
    total = middle_grad.ref

    @row_blocks(rows)
    def _(i):
        rounded = upstream[block_at(i), :].astype(BF16)
        branch[block_at(i), :] = rounded
        branch_sums[...] += fold_rows(rounded.astype(F32))
        total[block_at(i), :] = jnp.zeros((ROW_BLOCK, wide), F32)

    branch_turned[...] = branch[...].T
    put_transposed(feed_input.use()[...], feed_turned)
    hidden, slope, up, down = hidden.use(), slope.use(), up.use(), down.use()

    @pl.loop(0, planes)
    def _(p):
        down_grad.ref[p] = dot(branch_turned[...], hidden[p]).astype(BF16)
        down_grad.flush(p)
        hidden_grad = dot(branch[...], down[p], NT)
        before_grad = (hidden_grad * slope[p].astype(F32)).astype(BF16)
        both = dot(feed_turned[...], before_grad)
        up_grad.ref[p] = both[:wide].astype(BF16)
        up_grad.flush(p)
        up_sums[p] = both[wide : wide + 8]
        total[...] += dot(before_grad, up[p], NT)
        hook(p)

    layer_backward(middle.use(), gain, upstream, total, gain_sums, shift_sums)
    middle_grad.flush()


def attn_backward(head_dim, length, middle_grad, saved, weight, gain, put, outs, scratch, hook):
    attended, triple, logsum, normed, stream = saved
    head_sums, input_grad, branch_sums, gain_sums, shift_sums = outs
    branch, branch_turned, normed_turned, triple_grad, total = scratch
    planes, rows, width = attended.ref.shape
    wide = branch.shape[1]
    branch_sums[...] = jnp.zeros_like(branch_sums)
    middle_grad = middle_grad.use()

    @row_blocks(rows)
    def _(i):
        rounded = middle_grad[block_at(i), :].astype(BF16)
        branch[block_at(i), :] = rounded
        branch_sums[...] += fold_rows(rounded.astype(F32))
        total[block_at(i), :] = jnp.zeros((ROW_BLOCK, wide), F32)

    branch_turned[...] = branch[...].T
    put_transposed(normed.use()[...], normed_turned)
    attended, triple, logsum, weight = attended.use(), triple.use(), logsum.use(), weight.use()

    @pl.loop(0, planes)
    def _(p):
        mixed = dot(branch[...], weight[p, :, 3 * width :]).astype(BF16)
        strip_backward(head_dim, length, p, triple, attended, mixed, logsum, triple_grad)
        both = dot(normed_turned[...], triple_grad[...])
        out_grad = dot(branch_turned[...], attended[p])
        put(p, jnp.concatenate([both[:wide].astype(BF16), out_grad.astype(BF16)], -1))
        head_sums[p] = both[wide : wide + 8]
        total[...] += dot(triple_grad[...], weight[p, :, : 3 * width], NT)
        hook(p)

    layer_backward(stream.use(), gain, middle_grad, total, gain_sums, shift_sums)

    @row_blocks(rows)
    def _(i):
        input_grad.ref[block_at(i), :] = total[block_at(i), :].astype(BF16)

    input_grad.flush()


IN_VMEM = pl.BlockSpec(memory_space=pltpu.VMEM)
IN_SMEM = pl.BlockSpec(memory_space=pltpu.SMEM)


def whole_call(kernel, name, ins, outs, scratch=()):
    return pl.pallas_call(
        kernel,
        out_shape=[jax.ShapeDtypeStruct(shape, dtype) for shape, dtype in outs],
        in_specs=[IN_SMEM if v.dtype == jnp.int32 else IN_VMEM for v in ins],
        out_specs=[IN_VMEM] * len(outs),
        scratch_shapes=list(scratch),
        compiler_params=pltpu.CompilerParams(vmem_limit_bytes=VMEM_BYTES),
        name=name,
    )(*ins)


class Load:
    def __init__(self, source, ref, sem):
        self.ref, self.copy, self.waits = ref, pltpu.make_async_copy(source, ref, sem), True
        self.copy.start()

    def use(self):
        if self.waits:
            self.copy.wait()
            self.waits = False
        return self.ref


class Store:
    def __init__(self, ref, target, sems):
        self.ref, self.target, self.sems, self.by_plane = ref, target, sems, False

    def flush(self, p=None):
        if p is None:
            pltpu.make_async_copy(self.ref, self.target, self.sems.at[0]).start()
        else:
            self.by_plane = True
            pltpu.make_async_copy(self.ref.at[p], self.target.at[p], self.sems.at[p]).start()

    def finish(self):
        if not self.by_plane:
            pltpu.make_async_copy(self.ref, self.target, self.sems.at[0]).wait()
            return
        for p in range(self.ref.shape[0]):
            pltpu.make_async_copy(self.ref.at[p], self.target.at[p], self.sems.at[p]).wait()


def staged_call(name, body, ins, outs, scratch=(), collective_id=None):
    any_spec = pl.BlockSpec(memory_space=pl.ANY)
    near = lambda v: IN_SMEM if v.dtype == jnp.int32 else IN_VMEM
    loads = [v for mode, v in ins if mode == "load"]
    stores = [(shape, dtype) for mode, shape, dtype in outs if mode == "store"]
    scratch = list(scratch)

    def kernel(*refs):
        refs = list(refs)
        take = lambda n: [refs.pop(0) for _ in range(n)]
        in_refs, out_refs = take(len(ins)), take(len(outs))
        load_refs, store_refs, rest = take(len(loads)), take(len(stores)), take(len(scratch))
        load_sem, store_sem = refs
        given, load_at = [], 0
        for (mode, _), ref in zip(ins, in_refs):
            if mode == "load":
                given.append(Load(ref, load_refs[load_at], load_sem.at[load_at]))
                load_at += 1
            else:
                given.append(ref)
        results, store_at = [], 0
        for (mode, _, _), ref in zip(outs, out_refs):
            if mode == "store":
                results.append(Store(store_refs[store_at], ref, store_sem.at[store_at]))
                store_at += 1
            else:
                results.append(ref)
        body(given, results, rest)
        for item in given:
            if isinstance(item, Load):
                item.use()
        for item in results:
            if isinstance(item, Store):
                item.finish()

    params = {"vmem_limit_bytes": VMEM_BYTES}
    if collective_id is not None:
        params.update(collective_id=collective_id, has_side_effects=True)
    return pl.pallas_call(
        kernel,
        out_shape=[jax.ShapeDtypeStruct(shape, dtype) for _, shape, dtype in outs],
        in_specs=[near(v) if mode == "near" else any_spec for mode, v in ins],
        out_specs=[any_spec if mode == "store" else IN_VMEM for mode, _, _ in outs],
        scratch_shapes=[pltpu.VMEM(v.shape, v.dtype) for v in loads]
        + [pltpu.VMEM(shape, dtype) for shape, dtype in stores]
        + scratch
        + [pltpu.SemaphoreType.DMA((max(len(loads), 1),))]
        + [pltpu.SemaphoreType.DMA((max(len(stores), 1), 4))],
        compiler_params=pltpu.CompilerParams(**params),
        name=name,
    )(*[v for _, v in ins])


def run_attn_forward(stream, weight, params, length, head_dim):
    gain, shift, bias, out_bias = params
    planes, wide, width = weight.shape
    width //= 4
    rows = stream.shape[0]

    def kernel(length, stream, weight, gain, shift, bias, out_bias, *outs):
        attn_forward(head_dim, length[0], stream, weight, gain, shift, bias, out_bias, outs)

    return whole_call(
        kernel,
        "attn_forward",
        (length, stream, weight, gain, shift, bias, out_bias),
        (
            ((rows, wide), BF16),
            ((planes, rows, 3 * width), BF16),
            ((planes, rows, width), BF16),
            ((planes, width // head_dim, rows), F32),
            ((rows, wide), F32),
        ),
    )


def run_feed_forward(middle, up, down, params, bridge=None):
    up_bias, gain, shift, down_bias = params
    planes, wide, width = up.shape
    rows = middle.shape[0]
    saved = (
        ((rows, wide), BF16),
        ((planes, rows, width), BF16),
        ((planes, rows, width), BF16),
        ((rows, wide), BF16),
    )
    ins = (middle, up, down, up_bias, gain, shift, down_bias)
    scratch = [pltpu.VMEM((rows, wide), F32)]
    if bridge is None:

        def kernel(*refs):
            outs, result, total = refs[7:10], refs[10], refs[11]
            feed_forward(*refs[:7], outs, total)
            result[...] = total[...].astype(BF16)

        return whole_call(kernel, "feed_forward", ins, saved, scratch)

    def kernel_bridge(*refs):
        weight, bias = refs[7:9]
        outs, result, bridged, total = refs[9:12], refs[12], refs[13], refs[14]
        feed_forward(*refs[:7], outs, total)
        result[...] = total[...].astype(BF16)
        bridged[...] = dot(result[...], weight[...]) + bias[...]

    outs = saved + (((rows, bridge[0].shape[1]), F32),)
    return whole_call(kernel_bridge, "feed_forward", ins + tuple(bridge), outs, scratch)


def nothing(p):
    pass


def at_planes(schedule):
    def hook(p):
        for k, work in enumerate(schedule):

            @pl.when(p == k)
            def _():
                for step in work:
                    step()

    return hook


def six_deep(grad):
    planes, rows, columns = grad.shape
    return grad.reshape(planes, 2, 2, 2, rows // 8, columns)


def even_schedule(reducer, matrices):
    every = lambda step, ps: [partial(step, m, p) for p in ps for m in matrices]
    return [
        every(reducer.core, (0, 1)),
        every(reducer.core, (2, 3)) + every(reducer.plane, (0, 1)),
        every(reducer.plane, (2, 3)) + every(reducer.corner, (0, 1)),
        every(reducer.corner, (2, 3)),
    ]


def feed_scratch(rows, wide):
    return [
        pltpu.VMEM((rows, wide), BF16),
        pltpu.VMEM((wide, rows), BF16),
        pltpu.VMEM((wide + 16, rows), BF16),
    ]


def feed_outs(planes, rows, wide, width):
    return [
        ("store", (planes, wide, width), BF16),
        ("store", (planes, wide, width), BF16),
        ("near", (planes, 8, width), F32),
        ("store", (rows, wide), F32),
        ("near", (8, wide), F32),
        ("near", (8, wide), F32),
        ("near", (8, wide), F32),
    ]


def run_feed_backward(upstream, saved, weights, gain):
    hidden, slope, feed_input, middle = saved
    planes, rows, width = hidden.shape
    wide = feed_input.shape[1]

    def body(ins, outs, scratch):
        feed_backward(ins[0], ins[1:5], ins[5:7], ins[7], outs, scratch, nothing)

    return staged_call(
        "feed_backward",
        body,
        [("load", v) for v in (upstream,) + saved + weights] + [("near", gain)],
        feed_outs(planes, rows, wide, width),
        feed_scratch(rows, wide),
    )


def run_bridge_feed_backward(bridge, saved, weights, gain, partial_grad):
    hidden, slope, feed_input, middle = saved
    planes, rows, width = hidden.shape
    wide = feed_input.shape[1]
    grad_rows, bridge_input, bridge_weight = bridge
    narrow = grad_rows.shape[1]
    ins = [("load", v) for v in bridge + saved + weights] + [("near", gain)]
    scratch = feed_scratch(rows, wide) + [pltpu.VMEM((rows, wide), F32)]
    outs = feed_outs(planes, rows, wide, width) + [("near", (8, narrow), F32)]
    deep = wide // 8 // planes
    tall = -(-deep // 32) * 32

    def prologue(ins, scratch, sums):
        turned = scratch[2]
        put_transposed(ins[1].use()[...], turned)
        both = dot(turned[...], ins[0].use()[...])
        sums[...] = both[wide : wide + 8]
        scratch[3][...] = dot(ins[0].use()[...], ins[2].use()[...], NT)
        return both[:wide]

    class Ready:
        def __init__(self, ref):
            self.ref = ref

        def use(self):
            return self.ref

    if partial_grad is None:
        outs += [("near", (wide, narrow), F32)]

        def body(ins, outs, scratch):
            outs[8][...] = prologue(ins, scratch, outs[7])
            upstream = Ready(scratch[3])
            feed_backward(upstream, ins[3:7], ins[7:9], ins[9], outs[:7], scratch[:3], nothing)

        return staged_call("feed_backward", body, ins, outs, scratch)

    parts = six_deep(partial_grad)
    shapes = (parts.shape[4:], (tall, narrow))
    outs += [("near", shape, F32) for shape in shapes]
    scratch = scratch + [pltpu.VMEM((planes, 2, 2, 2, tall, narrow), BF16)]
    own = len(scratch)
    scratch = scratch + Reducer.scratch(shapes, planes, resident=(1,))

    def body(ins, outs, scratch):
        reducer = Reducer(shapes, planes, scratch[own:])
        entry_barrier((reducer.mp, reducer.across_core, reducer.across_x, reducer.across_y))
        reducer.parts = [ins[10], scratch[4]]
        for p in range(planes):
            reducer.begin(0, p)
        grad = prologue(ins, scratch, outs[7])
        for g in range(8):
            for p in range(planes):
                low = (g * planes + p) * deep
                block = jnp.concatenate(
                    [grad[low : low + deep], jnp.zeros((tall - deep, narrow), F32)], 0
                )
                scratch[4][p, g // 4, g // 2 % 2, g % 2] = block.astype(BF16)
        for p in range(planes):
            reducer.begin(1, p)
        upstream = Ready(scratch[3])
        hook = at_planes(even_schedule(reducer, (0, 1)))
        feed_backward(upstream, ins[3:7], ins[7:9], ins[9], outs[:7], scratch[:3], hook)
        reducer.finish(0, outs[8])
        reducer.finish(1, outs[9])
        reducer.drain()

    return staged_call("feed_backward_sums", body, ins + [("raw", parts)], outs, scratch, 2)


def attn_parts(planes, rows, wide, width):
    outs = [
        ("near", (planes, 8, 3 * width), F32),
        ("store", (rows, wide), BF16),
        ("near", (8, wide), F32),
        ("near", (8, wide), F32),
        ("near", (8, wide), F32),
    ]
    scratch = feed_scratch(rows, wide) + [
        pltpu.VMEM((rows, 3 * width), BF16),
        pltpu.VMEM((rows, wide), F32),
    ]
    return outs, scratch


def run_attn_backward(middle_grad, saved, weight, gain, length, head_dim, partial_grads=None):
    planes, rows, width = saved[0].shape
    wide = weight.shape[1]
    outs, scratch = attn_parts(planes, rows, wide, width)
    outs = outs + [("store", (planes, wide, 4 * width), BF16)]
    ins = [("near", length)] + [("load", v) for v in (middle_grad,) + saved + (weight,)]
    ins = ins + [("near", gain)]

    def compute(ins, outs, scratch, hook):
        def put(p, value):
            outs[5].ref[p] = value
            outs[5].flush(p)

        attn_backward(
            head_dim,
            ins[0][0],
            ins[1],
            ins[2:7],
            ins[7],
            ins[8],
            put,
            outs[:5],
            scratch[:5],
            hook,
        )

    if partial_grads is None:

        def body(ins, outs, scratch):
            compute(ins, outs, scratch, nothing)

        return staged_call("attn_backward", body, ins, outs, scratch)

    parts = [six_deep(g) for g in partial_grads]
    shapes = tuple(part.shape[4:] for part in parts)
    outs += [("near", shape, F32) for shape in shapes]
    scratch = scratch + Reducer.scratch(shapes, planes)

    def body(ins, outs, scratch):
        reducer = Reducer(shapes, planes, scratch[5:])
        entry_barrier((reducer.mp, reducer.across_core, reducer.across_x, reducer.across_y))
        reducer.parts = ins[9:11]
        for p in range(planes):
            for m in range(2):
                reducer.begin(m, p)
        compute(ins, outs, scratch, at_planes(even_schedule(reducer, (0, 1))))
        reducer.finish(0, outs[6])
        reducer.finish(1, outs[7])
        reducer.drain()

    ins = ins + [("raw", part) for part in parts]
    return staged_call("attn_backward_sums", body, ins, outs, scratch, 1)


class VectorSum:
    def __init__(self, refs):
        self.levels, self.came, self.from_z, self.send_sem, self.recv_sem = refs
        self.dp, self.mp, core, x, y, *across = neighbours()
        self.across = across

    @staticmethod
    def scratch(rows, columns, planes):
        return [
            pltpu.VMEM((4, rows, columns), F32),
            pltpu.VMEM((3, rows, columns), F32),
            pltpu.VMEM((planes, rows, columns), F32),
            pltpu.SemaphoreType.DMA((3 + planes,)),
            pltpu.SemaphoreType.DMA((3 + planes,)),
        ]

    def hop(self, level):
        return pltpu.make_async_remote_copy(
            src_ref=self.levels.at[level],
            dst_ref=self.came.at[level],
            send_sem=self.send_sem.at[level],
            recv_sem=self.recv_sem.at[level],
            device_id=(self.across[level], self.mp),
            device_id_type=MESH,
        )

    def along(self, plane, receiving=False):
        slot = plane if receiving else self.mp
        return pltpu.make_async_remote_copy(
            src_ref=self.levels.at[3],
            dst_ref=self.from_z.at[slot],
            send_sem=self.send_sem.at[3 + plane],
            recv_sem=self.recv_sem.at[3 + slot],
            device_id=(self.dp, plane),
            device_id_type=MESH,
        )

    def begin(self):
        self.hop(0).start()

    def others(self):
        planes = self.from_z.shape[0]
        return [(self.mp + step) % planes for step in range(1, planes)]

    def advance(self, level):
        self.hop(level).wait_recv()
        self.levels[level + 1] = self.levels[level] + self.came[level]
        if level < 2:
            self.hop(level + 1).start()
        else:
            for plane in self.others():
                self.along(plane).start()

    def finish(self, out):
        total = self.levels[3]
        for plane in self.others():
            self.along(plane, receiving=True).wait_recv()
            total = total + self.from_z[plane]
        out[...] = total
        for level in range(3):
            self.hop(level).wait_send()
        for plane in self.others():
            self.along(plane).wait_send()


def stack_rows(rows, columns):
    wide = [
        row
        if row.shape[1] == columns
        else jnp.concatenate([row, jnp.zeros((1, columns - row.shape[1]), F32)], -1)
        for row in rows
    ]
    spare = -len(wide) % 8
    if spare:
        wide.append(jnp.zeros((spare, columns), F32))
    return jnp.concatenate(wide, 0)


def folded(sums):
    return jnp.sum(sums[...], 0, keepdims=True)


def first_rows(sums):
    return [sums[p, 0:1] for p in range(sums.shape[0])]


def early_rows(feed_sums, dec_sums, bridge_sums):
    f_gain, f_shift, down_bias, up_bias = feed_sums
    rows = [folded(f_gain), folded(f_shift), folded(down_bias)] + first_rows(up_bias)
    gain, shift, out_bias, head, f_gain, f_shift, down_bias, up_bias = dec_sums
    rows += [folded(v) for v in (gain, shift, out_bias, f_gain, f_shift, down_bias)]
    return rows + first_rows(up_bias) + first_rows(head) + [bridge_sums[0:1]]


def late_rows(gain, shift, out_bias, head):
    return [folded(gain), folded(shift), folded(out_bias)] + first_rows(head)


def run_last_backward(
    middle_grad, saved, weight, gain, length, head_dim, partial_grads, feed_sums, dec_sums, bridge_sums
):
    planes, rows, width = saved[0].shape
    wide = weight.shape[1]
    outs, scratch = attn_parts(planes, rows, wide, width)
    outs = outs[1:2]
    parts = [six_deep(g) for g in partial_grads]
    shapes = tuple(part.shape[4:] for part in parts) + ((wide // 8, 4 * width),)
    early = -(-(3 + 6 + 3 * planes + 1) // 8) * 8
    late = -(-(3 + planes) // 8) * 8
    outs += [("near", shape, F32) for shape in shapes]
    outs += [("near", (early, wide), F32), ("near", (late, wide), F32)]
    sums_scratch = [
        pltpu.VMEM((planes, 8, 3 * width), F32),
        pltpu.VMEM((8, wide), F32),
        pltpu.VMEM((8, wide), F32),
        pltpu.VMEM((8, wide), F32),
    ]
    sizes = [5, 4, 1, 5, 5]
    groups = [
        scratch,
        sums_scratch,
        [pltpu.VMEM((planes, 2, 2, 2, wide // 8, 4 * width), BF16)],
        VectorSum.scratch(early, wide, planes),
        VectorSum.scratch(late, wide, planes),
        Reducer.scratch(shapes, planes, resident=(2,)),
    ]
    loads = (middle_grad,) + saved + (weight,)
    small = tuple(feed_sums) + tuple(dec_sums) + (bridge_sums,)
    ins = [("near", length)] + [("load", v) for v in loads] + [("near", gain)]
    ins += [("raw", part) for part in parts] + [("near", v) for v in small]

    def body(ins, outs, scratch):
        cuts, at = [], 0
        for size in sizes:
            cuts.append(scratch[at : at + size])
            at += size
        compute_scratch, sums, (grads,), early_refs, late_refs = cuts
        reducer = Reducer(shapes, planes, scratch[at:])
        early_sum, late_sum = VectorSum(early_refs), VectorSum(late_refs)
        entry_barrier((reducer.mp, reducer.across_core, reducer.across_x, reducer.across_y))
        reducer.parts = ins[9:11] + [grads]
        for p in range(planes):
            for m in range(2):
                reducer.begin(m, p)
        small = ins[11:]
        early_sum.levels[0] = stack_rows(early_rows(small[:4], small[4:12], small[12]), wide)
        early_sum.begin()

        def put(p, value):
            grads[p] = value.reshape(grads.shape[1:])
            reducer.begin(2, p)

        every = lambda step, ps: [partial(step, m, p) for p in ps for m in range(2)]
        schedule = [
            every(reducer.core, range(planes)) + [partial(early_sum.advance, 0)],
            every(reducer.plane, (0, 1)) + [partial(early_sum.advance, 1)],
            every(reducer.plane, (2, 3)) + every(reducer.corner, (0,)),
            every(reducer.corner, (1, 2)) + [partial(early_sum.advance, 2)],
        ]
        head_sums, branch_sums, gain_sums, shift_sums = sums
        attn_backward(
            head_dim,
            ins[0][0],
            ins[1],
            ins[2:7],
            ins[7],
            ins[8],
            put,
            (head_sums, outs[0], branch_sums, gain_sums, shift_sums),
            compute_scratch,
            at_planes(schedule),
        )
        for p in range(planes):
            reducer.core(2, p)
        late_sum.levels[0] = stack_rows(
            late_rows(gain_sums, shift_sums, branch_sums, head_sums), wide
        )
        late_sum.begin()
        for step in every(reducer.corner, (3,)):
            step()
        late_sum.advance(0)
        for p in range(planes):
            reducer.plane(2, p)
        late_sum.advance(1)
        for p in range(planes):
            reducer.corner(2, p)
        late_sum.advance(2)
        early_sum.finish(outs[4])
        for m in range(3):
            reducer.finish(m, outs[1 + m])
        late_sum.finish(outs[5])
        reducer.drain()

    return staged_call("attn_backward_last", body, ins, outs, sum(groups, []), 3)


def block_forward(stream, params, weights, length, head_dim, bridge=None):
    (gain, shift, head_bias, output_bias, feed_gain, feed_shift, up_bias, down_bias) = params
    attn, up, down = weights
    zeros = jnp.zeros_like(head_bias[0])
    bias = jnp.concatenate([head_bias[0], zeros, head_bias[1]], -1)[:, None]
    normed, triple, attended, logsum, middle = run_attn_forward(
        stream, attn, (gain[None], shift[None], bias, output_bias[None]), length, head_dim
    )
    feed_input, hidden, slope, *results = run_feed_forward(
        middle, up, down, (up_bias[:, None], feed_gain[None], feed_shift[None], down_bias[None]), bridge
    )
    return results, (
        (hidden, slope, feed_input, middle),
        (attended, triple, logsum, normed, stream),
    )


def shards(sizes, *inputs):
    patches, lengths = inputs[:2]
    cotangent = inputs[28]
    planes, groups = sizes["mp"], sizes["dp"]
    mp = lax.axis_index("mp")
    length = lax.dynamic_slice_in_dim(lengths, mp, 1)

    def block_of(at):
        (gain, shift, proj, head_bias, out, out_bias, f_gain, f_shift, up, up_bias, down, d_bias) = (
            inputs[at : at + 12]
        )
        packed = jnp.concatenate([proj[0], proj[1], proj[2], out.T], -1)
        vectors = (gain, shift, out_bias, f_gain, f_shift, d_bias)
        return (packed, up, down), vectors, (head_bias, up_bias)

    enc_shards, enc_vectors, enc_split = block_of(2)
    bridge_weight, bridge_bias = inputs[14:16]
    dec_shards, dec_vectors, dec_split = block_of(16)
    small = jnp.concatenate([v.reshape(-1) for v in enc_split + dec_split])
    *wholes, small = spread(enc_shards + dec_shards, small, sizes)
    small = small.reshape(planes, -1)

    def params_of(vectors, split, at):
        gain, shift, out_bias, f_gain, f_shift, d_bias = vectors
        width, hidden = split[0].shape[1], split[1].shape[0]
        head_bias = small[:, at : at + 2 * width].reshape(planes, 2, width).transpose(1, 0, 2)
        up_bias = small[:, at + 2 * width : at + 2 * width + hidden]
        return (gain, shift, head_bias, out_bias, f_gain, f_shift, up_bias, d_bias)

    encoder = params_of(enc_vectors, enc_split, 0)
    decoder = params_of(dec_vectors, dec_split, 2 * enc_split[0].shape[1] + enc_split[1].shape[0])

    rows = patches.shape[0]
    padded = -(-rows // 32) * 32
    stream = jnp.pad(patches, ((0, padded - rows), (0, 0)))
    upstream = jnp.pad(cotangent, ((0, padded - rows), (0, 0)))

    (bridge_input, bridged), enc_stored = block_forward(
        stream, encoder, wholes[:3], length, HEAD, (bridge_weight, bridge_bias[None])
    )
    (decoded,), dec_stored = block_forward(bridged, decoder, wholes[3:], length, DHEAD)
    fast = groups == 8 and planes == 4
    dec_attn, dec_up, dec_down = wholes[3:]
    enc_attn, enc_up, enc_down = wholes[:3]
    down_part, up_part, up_sums, middle_grad, down_sums, f_gain_sums, f_shift_sums = (
        run_feed_backward(upstream, dec_stored[0], (dec_up, dec_down), decoder[4][None])
    )
    head_sums, bridge_rows, out_sums, gain_sums, shift_sums, attn_part, *dec_sums = run_attn_backward(
        middle_grad,
        dec_stored[1],
        dec_attn,
        decoder[0][None],
        length,
        DHEAD,
        (down_part, up_part) if fast else None,
    )
    dec_vectors = (
        gain_sums,
        shift_sums,
        out_sums,
        head_sums,
        f_gain_sums,
        f_shift_sums,
        down_sums,
        up_sums,
    )
    dec_parts = (attn_part, up_part, down_part)
    down_part, up_part, up_sums, middle_grad, down_sums, f_gain_sums, f_shift_sums, *more = (
        run_bridge_feed_backward(
            (bridge_rows, bridge_input, bridge_weight),
            enc_stored[0],
            (enc_up, enc_down),
            encoder[4][None],
            attn_part if fast else None,
        )
    )
    bridge_sums, *more = more
    feed_vectors = (f_gain_sums, f_shift_sums, down_sums, up_sums)
    deep = bridge_weight.shape[0] // planes // groups
    if fast:
        dec_attn_sum, bridge_sum = more
        dec_grads = (dec_attn_sum, dec_sums[1], dec_sums[0])
        bridge_out = bridge_sum[:deep]
        patches_grad, down_sum, up_sum, attn_sum, early, late = run_last_backward(
            middle_grad,
            enc_stored[1],
            enc_attn,
            encoder[0][None],
            length,
            HEAD,
            (down_part, up_part),
            feed_vectors,
            dec_vectors,
            bridge_sums,
        )
        enc_grads = (attn_sum, up_sum, down_sum)
    else:
        head_sums, patches_grad, out_sums, gain_sums, shift_sums, attn_part = run_attn_backward(
            middle_grad, enc_stored[1], enc_attn, encoder[0][None], length, HEAD
        )
        wide = patches.shape[1]
        early = stack_rows(early_rows(feed_vectors, dec_vectors, bridge_sums), wide)
        late = stack_rows(late_rows(gain_sums, shift_sums, out_sums, head_sums), wide)
        early, late = lax.psum(early, ("dp", "mp")), lax.psum(late, ("dp", "mp"))

        def in_groups(grad):
            return collect(grad.reshape(planes, groups, -1, grad.shape[-1]), sizes)

        dec_grads = tuple(in_groups(g) for g in dec_parts)
        enc_grads = tuple(in_groups(g) for g in (attn_part, up_part, down_part))
        bridge_part = more[0].reshape(groups, planes, deep, -1).transpose(1, 0, 2, 3)
        bridge_out = collect(bridge_part, sizes)

    dp = lax.axis_index("dp")

    def shared(row):
        row = row[: patches.shape[1]]
        size = row.shape[0] // groups // planes
        return lax.dynamic_slice_in_dim(row, (dp * planes + mp) * size, size)

    def split(rows):
        size = rows.shape[1] // groups
        return lax.dynamic_slice(rows, (mp, dp * size), (1, size))[0]

    def block_out(mats, shared_rows, head, up_bias, wide):
        attn, up, down = mats
        width = attn.shape[1] // 4
        proj = attn[:, : 3 * width].reshape(-1, 3, width).transpose(1, 0, 2)
        gain, shift, out_bias, f_gain, f_shift, d_bias = (shared(v[:wide]) for v in shared_rows)
        head_bias = jnp.stack([split(head[:, :width]), split(head[:, 2 * width : 3 * width])])
        up_out = split(up_bias[:, : up.shape[1]])
        out = attn[:, 3 * width :].T
        return (gain, shift, proj, head_bias, out, out_bias, f_gain, f_shift, up, up_out, down.T, d_bias)

    at = 3 + planes
    wide, narrow = patches.shape[1], cotangent.shape[1]
    enc_out = block_out(
        enc_grads,
        (late[0], late[1], late[2], early[0], early[1], early[2]),
        late[3 : 3 + planes],
        early[3:at],
        wide,
    )
    dec_out = block_out(
        dec_grads,
        [early[at + k] for k in range(6)],
        early[at + 6 + planes : at + 6 + 2 * planes],
        early[at + 6 : at + 6 + planes],
        narrow,
    )
    bridge_bias_out = shared(early[at + 6 + 2 * planes, :narrow])
    return (
        (decoded[:rows], patches_grad[:rows])
        + enc_out
        + (bridge_out, bridge_bias_out)
        + dec_out
    )


def solution(mesh):
    block_in = (
        P(),
        P(),
        P(None, None, "mp"),
        P(None, "mp"),
        P("mp", None),
        P(),
        P(),
        P(),
        P(None, "mp"),
        P("mp"),
        P("mp", None),
        P(),
    )
    both = P(("dp", "mp"))
    block_out = (
        both,
        both,
        P(None, "dp", "mp"),
        P(None, ("mp", "dp")),
        P("mp", "dp"),
        both,
        both,
        both,
        P("dp", "mp"),
        P(("mp", "dp")),
        P("mp", "dp"),
        both,
    )
    rows = P(("dp", "mp"), None)
    return jax.shard_map(
        partial(shards, dict(mesh.shape)),
        mesh=mesh,
        in_specs=(rows, P("dp")) + block_in + (P(), P()) + block_in + (rows,),
        out_specs=(rows, rows) + block_out + (rows, both) + block_out,
        check_vma=False,
    )
```

```python
from functools import partial

import jax
import jax.numpy as jnp
from jax import lax
from jax.experimental import pallas as pl
from jax.experimental.pallas import tpu as pltpu
from jax.sharding import PartitionSpec as P

HEAD = 64
DHEAD = 32
EPSILON = 1e-06
MESH = pl.DeviceIdType.MESH
F32 = jnp.float32
BF16 = jnp.bfloat16
VMEM_BYTES = 60 * 1024 * 1024


def neighbours():
    dp, mp = lax.axis_index("dp"), lax.axis_index("mp")
    core, x, y = dp % 2, (dp // 2) % 2, dp // 4
    across_core = dp + 1 - 2 * core
    across_x = dp + 2 - 4 * x
    across_y = dp + 4 - 8 * y
    return dp, mp, core, x, y, across_core, across_x, across_y


def entry_barrier(parts):
    mp, across_core, across_x, across_y = parts
    dp = lax.axis_index("dp")
    barrier = pltpu.get_barrier_semaphore()
    planes = lax.axis_size("mp")
    for other in (across_core, across_x, across_y):
        pl.semaphore_signal(barrier, inc=1, device_id=(other, mp), device_id_type=MESH)
    for step in range(1, planes):
        pl.semaphore_signal(
            barrier, inc=1, device_id=(dp, (mp + step) % planes), device_id_type=MESH
        )
    pl.semaphore_wait(barrier, 3 + planes - 1)


def plane_order(mp, planes):
    if planes != 4:
        return [(mp + step) % planes for step in range(1, planes)]
    upper = mp // 2
    place = mp + upper * (3 - 2 * mp)
    return [o + upper * (3 - 2 * o) for o in (place + 1, 2 - 2 * place, 3)]


def order_of(k, mp):
    upper = mp // 2
    place = mp + upper * (3 - 2 * mp)
    plane = (k + place) % 3 * (1 - k // 3) + 3 * (k // 3)
    return plane + upper * (3 - 2 * plane)


class Gatherer:
    A, X, Y, S, DY, DX, SX, SY, SDY, SDX = range(10)
    kinds = 10

    def __init__(self, planes, shards, placed, wholes, targets, smalls, sems):
        self.planes, self.count, self.placed = planes, len(shards), placed
        self.shards, self.wholes, self.targets = shards, wholes, targets
        self.small, self.smalls = smalls.at[lax.axis_index("mp")], smalls
        self.local_sem, self.flush_sem, self.send_sem, self.recv_sem = sems
        self.dp, self.mp, core, x, y, *across = neighbours()
        self.across_core, self.across_x, self.across_y = across
        self.others = plane_order(self.mp, planes)
        corner = self.across_x + self.across_y - self.dp
        shift = self.across_core - self.dp
        self.arrivals = {
            self.A: (self.dp, None),
            self.X: (self.across_x, None),
            self.Y: (self.across_y, None),
            self.S: (self.across_core, None),
            self.DY: (corner, 0),
            self.DX: (corner, 1),
            self.SX: (self.across_x + shift, None),
            self.SY: (self.across_y + shift, None),
            self.SDY: (corner + shift, 0),
            self.SDX: (corner + shift, 1),
        }
        self.onward = {
            self.X: (self.dp, None, self.across_x),
            self.Y: (self.dp, None, self.across_y),
            self.S: (self.dp, None, self.across_core),
            self.DY: (self.across_x, 0, self.across_y),
            self.DX: (self.across_y, 1, self.across_x),
            self.SX: (self.across_x, None, self.across_core),
            self.SY: (self.across_y, None, self.across_core),
            self.SDY: (corner, 0, self.across_core),
            self.SDX: (corner, 1, self.across_core),
        }

    @staticmethod
    def sems(count, planes):
        return [
            pltpu.SemaphoreType.DMA((count,)),
            pltpu.SemaphoreType.DMA((count, planes)),
            pltpu.SemaphoreType.DMA((count + 1, planes, Gatherer.kinds)),
            pltpu.SemaphoreType.DMA((count + 1, planes, Gatherer.kinds)),
        ]

    def rows_of(self, m, owner, half):
        piece = self.shards[m].shape[0] // 8
        if half is None:
            return pl.ds(owner * piece, piece)
        return pl.ds(owner * piece + half * (piece // 2), piece // 2)

    def remote(self, m, kind, src, dst, send_plane, recv_plane, target):
        return pltpu.make_async_remote_copy(
            src_ref=src,
            dst_ref=dst,
            send_sem=self.send_sem.at[m, send_plane, kind],
            recv_sem=self.recv_sem.at[m, recv_plane, kind],
            device_id=target,
            device_id_type=MESH,
        )

    def send(self, m, i, kind):
        plane = self.others[i]
        if kind == self.A:
            own = self.rows_of(m, self.dp, None)
            src, dst = self.shards[m].at[own], self.wholes[m].at[self.mp, own]
            return self.remote(m, kind, src, dst, plane, self.mp, (self.dp, plane))
        owner, half, target = self.onward[kind]
        part = self.wholes[m].at[plane, self.rows_of(m, owner, half)]
        return self.remote(m, kind, part, part, plane, plane, (target, self.mp))

    def send_small(self, i):
        plane = self.others[i]
        return self.remote(
            self.count,
            self.A,
            self.small,
            self.smalls.at[self.mp],
            plane,
            self.mp,
            (self.dp, plane),
        )

    def arrived(self, m, i, kind):
        plane = self.others[i]
        owner, half = self.arrivals[kind]
        part = self.wholes[m].at[plane, self.rows_of(m, owner, half)]
        self.remote(m, kind, part, part, plane, plane, (self.across_core, self.mp)).wait_recv()

    def along_z(self, m, i):
        self.send(m, i, self.A).start()

    def to_plane(self, m, i):
        self.arrived(m, i, self.A)
        for kind in (self.X, self.Y, self.S):
            self.send(m, i, kind).start()

    def to_corner(self, m, i):
        self.arrived(m, i, self.X)
        self.send(m, i, self.DY).start()
        self.send(m, i, self.SX).start()
        self.arrived(m, i, self.Y)
        self.send(m, i, self.DX).start()
        self.send(m, i, self.SY).start()

    def to_core(self, m, i):
        self.arrived(m, i, self.DY)
        self.send(m, i, self.SDY).start()
        self.arrived(m, i, self.DX)
        self.send(m, i, self.SDX).start()

    def flush(self, m, plane):
        return pltpu.make_async_copy(
            self.wholes[m].at[plane], self.targets[m].at[plane], self.flush_sem.at[m, plane]
        )

    def whole(self, m, i):
        for kind in (self.S, self.SX, self.SY, self.SDY, self.SDX):
            self.arrived(m, i, kind)
        self.flush(m, self.others[i]).start()

    def own(self, m):
        return pltpu.make_async_copy(
            self.shards[m], self.wholes[m].at[self.mp], self.local_sem.at[m]
        )

    def begin(self):
        for m in range(self.count):
            if m not in self.placed:
                self.own(m).start()

    def begin_small(self):
        for i in range(self.planes - 1):
            self.send_small(i).start()

    def have_own(self, m):
        if m not in self.placed:
            self.own(m).wait()
        self.flush(m, self.mp).start()

    def have_small(self):
        for i in range(self.planes - 1):
            part = self.smalls.at[self.others[i]]
            self.remote(
                self.count,
                self.A,
                part,
                part,
                self.others[i],
                self.others[i],
                (self.across_core, self.mp),
            ).wait_recv()

    def drain(self):
        for m in range(self.count):
            for i in range(self.planes - 1):
                for kind in range(self.kinds):
                    self.send(m, i, kind).wait_send()
            for p in range(self.planes):
                self.flush(m, p).wait()
        for i in range(self.planes - 1):
            self.send_small(i).wait_send()


class Reducer:
    def __init__(self, shapes, planes, refs):
        self.planes, self.count = planes, len(shapes)
        refs = list(refs)
        take = lambda: [refs.pop(0) for _ in range(self.count)]
        self.mine, self.from_core, self.from_x, self.from_y = take(), take(), take(), take()
        self.then_y, self.then_x, self.from_z = take(), take(), take()
        self.local_sem, self.send_sem, self.recv_sem = refs
        self.dp, self.mp, self.core_id, self.x, self.y, *across = neighbours()
        self.across_core, self.across_x, self.across_y = across
        self.halves = [rows // 2 for rows, columns in shapes]
        self.parts = [None] * self.count

    @staticmethod
    def scratch(shapes, planes, resident=()):
        count = len(shapes)

        def buffers(*lead, halves=False, skip=()):
            return [
                pltpu.VMEM((1, 16, 128), BF16)
                if m in skip
                else pltpu.VMEM(lead + (r // 2 if halves else r, c), BF16)
                for m, (r, c) in enumerate(shapes)
            ]

        return (
            buffers(planes, 2, 2, skip=resident)
            + buffers(planes, 2, 2)
            + buffers(planes, 2, halves=True)
            + buffers(planes, 2, halves=True)
            + buffers(planes, halves=True)
            + buffers(planes, halves=True)
            + buffers(planes)
            + [
                pltpu.SemaphoreType.DMA((count, planes)),
                pltpu.SemaphoreType.DMA((count, planes, 6)),
                pltpu.SemaphoreType.DMA((count, planes, 6)),
            ]
        )

    def remote(self, m, p, kind, src, dst, target, recv_plane=None):
        return pltpu.make_async_remote_copy(
            src_ref=src,
            dst_ref=dst,
            send_sem=self.send_sem.at[m, p, kind],
            recv_sem=self.recv_sem.at[m, p if recv_plane is None else recv_plane, kind],
            device_id=target,
            device_id_type=MESH,
        )

    def own(self, m, p, b, a):
        if self.resident(m):
            return self.parts[m].at[p, b, a, self.core_id]
        return self.mine[m].at[p, b, a]

    def owned(self, m, p, b, a, rows):
        if self.resident(m):
            return self.parts[m].at[p, b, a, self.core_id, rows]
        return self.mine[m].at[p, b, a, rows]

    def resident(self, m):
        return self.mine[m].shape[0] == 1

    def begin(self, m, p):
        if not self.resident(m):
            pltpu.make_async_copy(
                self.parts[m].at[p, :, :, self.core_id], self.mine[m].at[p], self.local_sem.at[m, p]
            ).start()
        self.to_core(m, p).start()

    def to_core(self, m, p):
        return self.remote(
            m,
            p,
            0,
            self.parts[m].at[p, :, :, 1 - self.core_id],
            self.from_core[m].at[p],
            (self.across_core, self.mp),
        )

    def to_x(self, m, p):
        src = self.owned(m, p, slice(None), 1 - self.x, pl.ds(0, self.halves[m]))
        return self.remote(m, p, 1, src, self.from_x[m].at[p], (self.across_x, self.mp))

    def to_y(self, m, p):
        half = self.halves[m]
        src = self.owned(m, p, 1 - self.y, slice(None), pl.ds(half, half))
        return self.remote(m, p, 2, src, self.from_y[m].at[p], (self.across_y, self.mp))

    def x_to_y(self, m, p):
        src = self.owned(m, p, 1 - self.y, self.x, pl.ds(0, self.halves[m]))
        return self.remote(m, p, 3, src, self.then_y[m].at[p], (self.across_y, self.mp))

    def y_to_x(self, m, p):
        half = self.halves[m]
        src = self.owned(m, p, self.y, 1 - self.x, pl.ds(half, half))
        return self.remote(m, p, 4, src, self.then_x[m].at[p], (self.across_x, self.mp))

    def to_z(self, m, p):
        src = self.own(m, p, self.y, self.x)
        return self.remote(m, p, 5, src, self.from_z[m].at[self.mp], (self.dp, p), self.mp)

    def core(self, m, p):
        if not self.resident(m):
            pltpu.make_async_copy(
                self.parts[m].at[p, :, :, self.core_id], self.mine[m].at[p], self.local_sem.at[m, p]
            ).wait()
        self.to_core(m, p).wait_recv()
        for b in range(2):
            for a in range(2):
                ref = self.own(m, p, b, a)
                ref[...] = ref[...] + self.from_core[m][p, b, a]
        self.to_x(m, p).start()
        self.to_y(m, p).start()

    def plane(self, m, p):
        half = self.halves[m]
        self.to_x(m, p).wait_recv()
        for b in range(2):
            ref = self.owned(m, p, b, self.x, pl.ds(0, half))
            ref[...] = ref[...] + self.from_x[m][p, b]
        self.x_to_y(m, p).start()
        self.to_y(m, p).wait_recv()
        for a in range(2):
            ref = self.owned(m, p, self.y, a, pl.ds(half, half))
            ref[...] = ref[...] + self.from_y[m][p, a]
        self.y_to_x(m, p).start()

    def corner(self, m, p):
        half = self.halves[m]
        self.x_to_y(m, p).wait_recv()
        self.y_to_x(m, p).wait_recv()
        ref = self.owned(m, p, self.y, self.x, pl.ds(0, half))
        ref[...] = ref[...] + self.then_y[m][p]
        ref = self.owned(m, p, self.y, self.x, pl.ds(half, half))
        ref[...] = ref[...] + self.then_x[m][p]

        @pl.when(p != self.mp)
        def _():
            self.to_z(m, p).start()

    def finish(self, m, out):
        total = self.own(m, self.mp, self.y, self.x)[...].astype(F32)
        for step in range(1, self.planes):
            plane = (self.mp + step) % self.planes
            src = self.from_z[m].at[plane]
            self.remote(m, plane, 5, src, src, (self.dp, plane)).wait_recv()
            total = total + src[...].astype(F32)
        out[...] = total

    def drain(self):
        @pl.loop(0, self.planes)
        def _(p):
            for m in range(self.count):
                for copy in (self.to_core, self.to_x, self.to_y, self.x_to_y, self.y_to_x):
                    copy(m, p).wait_send()

                @pl.when(p != self.mp)
                def _():
                    self.to_z(m, p).wait_send()


def collect(part, sizes):
    part = lax.psum_scatter(part, "mp", scatter_dimension=0, tiled=False)
    return lax.psum_scatter(part.astype(F32), "dp", scatter_dimension=0, tiled=False)


LOG2E = 1.4426950408889634
ROW_BLOCK = 32
NT = (((1,), (1,)), ((), ()))


def dot(left, right, dims=(((1,), (0,)), ((), ()))):
    return lax.dot_general(left, right, dims, preferred_element_type=F32)


def standardize(x):
    centered = x - jnp.mean(x, -1, keepdims=True)
    scale = lax.rsqrt(jnp.mean(centered * centered, -1, keepdims=True) + EPSILON)
    return centered * scale, scale


def gelu_and_slope(b):
    cdf = 0.5 * (1.0 + lax.erf(b * 0.7071067811865476))
    density = jnp.exp(-0.5 * b * b) * 0.3989422804014327
    return b * cdf, cdf + b * density


def fold_rows(x):
    return jnp.sum(x.reshape(x.shape[0] // 8, 8, x.shape[1]), 0)


def row_blocks(rows):
    return pl.loop(0, rows // ROW_BLOCK)


def block_at(i):
    return pl.ds(pl.multiple_of(i * ROW_BLOCK, ROW_BLOCK), ROW_BLOCK)


def whole_lanes(columns):
    return -(-columns // 128) * 128


def strip_forward(head_dim, width, length, p, triple, attended, logsum):
    rows = triple.shape[1]
    visible = lax.broadcasted_iota(jnp.int32, (rows, 1), 0) < length
    factor = head_dim**-0.5 * LOG2E
    outs = []
    for head in range(width // head_dim):
        low = head * head_dim
        query = triple[p, :, low : low + head_dim]
        key = triple[p, :, width + low : width + low + head_dim]
        value = triple[p, :, 2 * width + low : 2 * width + low + head_dim]
        scores = jnp.where(visible, dot(key, query, NT) * factor, -1e30)
        ceiling = jnp.max(scores, 0, keepdims=True)
        exponent = jnp.exp2(scores - ceiling)
        denominator = jnp.sum(exponent, 0, keepdims=True)
        outs.append(dot(value.T, exponent.astype(BF16)) * (1.0 / denominator))
        logsum[p, head : head + 1, :] = ceiling + jnp.log2(denominator)
    attended[p, :, :width] = jnp.concatenate(outs, 0).T.astype(BF16)


def strip_backward(head_dim, width, length, p, triple, attended, mixed, logsum, out):
    rows = triple.shape[1]
    visible = lax.broadcasted_iota(jnp.int32, (rows, 1), 0) < length
    factor = head_dim**-0.5
    products = (mixed.astype(F32) * attended[p, :, :width].astype(F32)).T
    query_grads = []
    for head in range(width // head_dim):
        low = head * head_dim
        query = triple[p, :, low : low + head_dim]
        key = triple[p, :, width + low : width + low + head_dim]
        value = triple[p, :, 2 * width + low : 2 * width + low + head_dim]
        mixed_head = mixed[:, low : low + head_dim]
        row_sums = jnp.sum(products[low : low + head_dim], 0, keepdims=True)
        scores = dot(key, query, NT) * (factor * LOG2E) - logsum[p, head : head + 1, :]
        chances = jnp.exp2(jnp.where(visible, scores, -1e30))
        chance_grad = dot(value, mixed_head, NT)
        score_grad = (chances * (chance_grad - row_sums)).astype(BF16)
        key_grad = dot(score_grad, query) * factor
        value_grad = dot(chances.astype(BF16), mixed_head)
        query_grads.append(dot(key.T, score_grad) * factor)
        out[:, width + low : width + low + head_dim] = key_grad.astype(BF16)
        out[:, 2 * width + low : 2 * width + low + head_dim] = value_grad.astype(BF16)
    out[:, :width] = jnp.concatenate(query_grads, 0).T.astype(BF16)


def attn_forward(head_dim, length, stream, weight, vectors, bias_of, outs, order, before):
    gain, shift, out_bias = [as_row(v) for v in vectors]
    normed, triple, attended, logsum, middle = outs
    planes, rows = triple.shape[:2]
    width = weight.shape[2] // 4

    @row_blocks(rows)
    def _(i):
        x = stream[block_at(i), :].astype(F32)
        normed[block_at(i), :] = (standardize(x)[0] * gain + shift).astype(BF16)
        middle[block_at(i), :] = x + out_bias

    @pl.loop(0, planes)
    def _(k):
        before(k)
        p = order(k)
        projected = dot(normed[...], weight[p, :, : 3 * width]) + bias_of(p)
        triple[p, :, : 3 * width] = projected.astype(BF16)
        strip_forward(head_dim, width, length, p, triple, attended, logsum)
        middle[...] += dot(attended[p, :, :width], weight[p, :, 3 * width :], NT)


def feed_forward(middle, up, down, vectors, bias_of, outs, total, order, before):
    gain, shift, down_bias = [as_row(v) for v in vectors]
    feed_input, hidden, slope = outs
    planes, rows, width = hidden.shape

    @row_blocks(rows)
    def _(i):
        x = middle[block_at(i), :]
        feed_input[block_at(i), :] = (standardize(x)[0] * gain + shift).astype(BF16)
        total[block_at(i), :] = x + down_bias

    @pl.loop(0, planes)
    def _(k):
        before(k)
        p = order(k)
        bias = bias_of(p)
        for low in range(0, width, 256):
            part = slice(low, low + 256)
            activated, rise = gelu_and_slope(dot(feed_input[...], up[p, :, part]) + bias[:, part])
            hidden[p, :, part] = activated.astype(BF16)
            slope[p, :, part] = rise.astype(BF16)
        total[...] += dot(hidden[p], down[p])


def as_row(vector):
    return vector[...].reshape(1, -1)


def layer_backward(stream, gain, upstream, spare, gain_sums, shift_sums):
    gain_sums[...] = jnp.zeros_like(gain_sums)
    shift_sums[...] = jnp.zeros_like(shift_sums)
    gain = as_row(gain)

    @row_blocks(stream.shape[0])
    def _(i):
        hat, scale = standardize(stream[block_at(i), :].astype(F32))
        grad = spare[block_at(i), :]
        gain_sums[...] += fold_rows(grad * hat)
        shift_sums[...] += fold_rows(grad)
        grad = grad * gain
        part = grad - jnp.mean(grad, -1, keepdims=True)
        part = part - hat * jnp.mean(grad * hat, -1, keepdims=True)
        spare[block_at(i), :] = upstream[block_at(i), :].astype(F32) + part * scale


def put_transposed(values, turned):
    columns = values.shape[1]
    turned[:columns, :] = values.T
    turned[columns:, :] = jnp.ones((16, values.shape[0]), BF16)


def start_branch(upstream, branch, turned, sums, total):
    rows, wide = branch.shape
    sums[...] = jnp.zeros_like(sums)

    @row_blocks(rows)
    def _(i):
        rounded = upstream[block_at(i), :].astype(BF16)
        branch[block_at(i), :] = rounded
        sums[...] += fold_rows(rounded.astype(F32))
        total[block_at(i), :] = jnp.zeros((ROW_BLOCK, wide), F32)

    turned[...] = branch[...].T


def matrix(ref, p):
    values = ref[p]
    return values.reshape(8 * values.shape[3], values.shape[4])


def put_matrix(ref, p, value):
    ref[p] = value.reshape(ref.shape[1:])


def feed_backward(upstream, saved, weights, scratch, sums, total, hook):
    hidden, slope, feed_input = saved
    up, down = weights
    branch, branch_turned, feed_turned = scratch
    branch_sums, up_sums = sums
    planes = hidden.shape[0]
    wide = branch.shape[1]
    start_branch(upstream, branch, branch_turned, branch_sums, total)
    put_transposed(feed_input[...], feed_turned)

    @pl.loop(0, planes)
    def _(p):
        down_grad = dot(branch_turned[...], hidden[p]).astype(BF16)
        hidden_grad = dot(branch[...], matrix(down, p), NT)
        put_matrix(down, p, down_grad)
        before_grad = (hidden_grad * slope[p].astype(F32)).astype(BF16)
        total[...] += dot(before_grad, matrix(up, p), NT)
        both = dot(feed_turned[...], before_grad)
        put_matrix(up, p, both[:wide].astype(BF16))
        up_sums[p] = both[wide : wide + 8]
        hook(p)


def attn_backward(head_dim, length, upstream, saved, weight, scratch, sums, total, hook):
    attended, triple, logsum, normed = saved
    branch, branch_turned, normed_turned, triple_grad = scratch
    branch_sums, head_sums = sums
    planes, width = attended.shape[0], weight.shape[5] // 4
    wide = branch.shape[1]
    start_branch(upstream, branch, branch_turned, branch_sums, total)
    put_transposed(normed[...], normed_turned)

    @pl.loop(0, planes)
    def _(p):
        own = matrix(weight, p)
        mixed = dot(branch[...], own[:, 3 * width :]).astype(BF16)
        strip_backward(head_dim, width, length, p, triple, attended, mixed, logsum, triple_grad)
        total[...] += dot(triple_grad[...], own[:, : 3 * width], NT)
        both = dot(normed_turned[...], triple_grad[...])
        out_grad = dot(branch_turned[...], attended[p, :, :width])
        grad = jnp.concatenate([both[:wide].astype(BF16), out_grad.astype(BF16)], -1)
        put_matrix(weight, p, grad)
        head_sums[p] = both[wide : wide + 8]
        hook(p)


IN_VMEM = pl.BlockSpec(memory_space=pltpu.VMEM)
IN_SMEM = pl.BlockSpec(memory_space=pltpu.SMEM)


class Load:
    def __init__(self, source, ref, sem):
        self.ref, self.copy, self.waits = ref, pltpu.make_async_copy(source, ref, sem), True
        self.copy.start()

    def use(self):
        if self.waits:
            self.copy.wait()
            self.waits = False
        return self.ref


class Store:
    def __init__(self, ref, target, sems):
        self.ref, self.target, self.sems, self.by_plane = ref, target, sems, False

    def flush(self, p=None):
        if p is None:
            pltpu.make_async_copy(self.ref, self.target, self.sems.at[0]).start()
        else:
            self.by_plane = True
            pltpu.make_async_copy(self.ref.at[p], self.target.at[p], self.sems.at[p]).start()

    def finish(self):
        if not self.by_plane:
            pltpu.make_async_copy(self.ref, self.target, self.sems.at[0]).wait()
            return
        for p in range(self.ref.shape[0]):
            pltpu.make_async_copy(self.ref.at[p], self.target.at[p], self.sems.at[p]).wait()


def staged_call(name, body, ins, outs, scratch=(), collective_id=None):
    any_spec = pl.BlockSpec(memory_space=pl.ANY)
    near = lambda v: IN_SMEM if v.dtype == jnp.int32 else IN_VMEM
    loads = [v for mode, v in ins if mode == "load"]
    stores = [(shape, dtype) for mode, shape, dtype in outs if mode == "store"]
    scratch = list(scratch)

    def kernel(*refs):
        refs = list(refs)
        take = lambda n: [refs.pop(0) for _ in range(n)]
        in_refs, out_refs = take(len(ins)), take(len(outs))
        load_refs, store_refs, rest = take(len(loads)), take(len(stores)), take(len(scratch))
        load_sem, store_sem = refs
        given, load_at = [], 0
        for (mode, _), ref in zip(ins, in_refs):
            if mode == "load":
                given.append(Load(ref, load_refs[load_at], load_sem.at[load_at]))
                load_at += 1
            else:
                given.append(ref)
        results, store_at = [], 0
        for (mode, _, _), ref in zip(outs, out_refs):
            if mode == "store":
                results.append(Store(store_refs[store_at], ref, store_sem.at[store_at]))
                store_at += 1
            else:
                results.append(ref)
        body(given, results, rest)
        for item in given:
            if isinstance(item, Load):
                item.use()
        for item in results:
            if isinstance(item, Store):
                item.finish()

    params = {"vmem_limit_bytes": VMEM_BYTES}
    if collective_id is not None:
        params.update(collective_id=collective_id, has_side_effects=True)
    return pl.pallas_call(
        kernel,
        out_shape=[jax.ShapeDtypeStruct(shape, dtype) for _, shape, dtype in outs],
        in_specs=[near(v) if mode == "near" else any_spec for mode, v in ins],
        out_specs=[IN_VMEM if mode == "near" else any_spec for mode, _, _ in outs],
        scratch_shapes=[pltpu.VMEM(v.shape, v.dtype) for v in loads]
        + [pltpu.VMEM(shape, dtype) for shape, dtype in stores]
        + scratch
        + [pltpu.SemaphoreType.DMA((max(len(loads), 1),))]
        + [pltpu.SemaphoreType.DMA((max(len(stores), 1), 4))],
        compiler_params=pltpu.CompilerParams(**params),
        name=name,
    )(*[v for _, v in ins])


def nothing(p):
    pass


def at_planes(schedule):
    def hook(p):
        for k, work in enumerate(schedule):

            @pl.when(p == k)
            def _():
                for step in work:
                    step()

    return hook


def six_deep(grad):
    planes, rows, columns = grad.shape
    return grad.reshape(planes, 2, 2, 2, rows // 8, columns)


class VectorSum:
    def __init__(self, refs):
        self.levels, self.came, self.from_z, self.send_sem, self.recv_sem = refs
        self.dp, self.mp, core, x, y, *across = neighbours()
        self.across = across

    @staticmethod
    def scratch(rows, columns, planes):
        return [
            pltpu.VMEM((4, rows, columns), F32),
            pltpu.VMEM((3, rows, columns), F32),
            pltpu.VMEM((planes, rows, columns), F32),
            pltpu.SemaphoreType.DMA((3 + planes,)),
            pltpu.SemaphoreType.DMA((3 + planes,)),
        ]

    def hop(self, level):
        return pltpu.make_async_remote_copy(
            src_ref=self.levels.at[level],
            dst_ref=self.came.at[level],
            send_sem=self.send_sem.at[level],
            recv_sem=self.recv_sem.at[level],
            device_id=(self.across[level], self.mp),
            device_id_type=MESH,
        )

    def along(self, plane, receiving=False):
        slot = plane if receiving else self.mp
        return pltpu.make_async_remote_copy(
            src_ref=self.levels.at[3],
            dst_ref=self.from_z.at[slot],
            send_sem=self.send_sem.at[3 + plane],
            recv_sem=self.recv_sem.at[3 + slot],
            device_id=(self.dp, plane),
            device_id_type=MESH,
        )

    def begin(self):
        self.hop(0).start()

    def others(self):
        planes = self.from_z.shape[0]
        return [(self.mp + step) % planes for step in range(1, planes)]

    def advance(self, level):
        self.hop(level).wait_recv()
        self.levels[level + 1] = self.levels[level] + self.came[level]
        if level < 2:
            self.hop(level + 1).start()
        else:
            for plane in self.others():
                self.along(plane).start()

    def finish(self, out):
        total = self.levels[3]
        for plane in self.others():
            self.along(plane, receiving=True).wait_recv()
            total = total + self.from_z[plane]
        out[...] = total
        for level in range(3):
            self.hop(level).wait_send()
        for plane in self.others():
            self.along(plane).wait_send()


def stack_rows(rows, columns):
    wide = [
        row
        if row.shape[1] == columns
        else jnp.concatenate([row, jnp.zeros((1, columns - row.shape[1]), F32)], -1)
        for row in rows
    ]
    spare = -len(wide) % 8
    if spare:
        wide.append(jnp.zeros((spare, columns), F32))
    return jnp.concatenate(wide, 0)


def folded(sums):
    return jnp.sum(sums[...], 0, keepdims=True)


def first_rows(sums):
    return [sums[p, 0:1] for p in range(sums.shape[0])]


EARLY_DEC = 8
EARLY_ROWS = 24


def early_rows(feed_sums, dec_sums, bridge_sums):
    f_gain, f_shift, down_bias, up_bias = feed_sums
    rows = [folded(f_gain), folded(f_shift), folded(down_bias)] + first_rows(up_bias)
    empty = [jnp.zeros_like(rows[0])]
    gain, shift, out_bias, head, f_gain, f_shift, down_bias, up_bias = dec_sums
    rows += empty + [folded(v) for v in (gain, shift, out_bias)] + first_rows(up_bias) + empty
    rows += [folded(v) for v in (f_gain, f_shift, down_bias)] + first_rows(head)
    return rows + [bridge_sums[0:1]]


def late_rows(gain, shift, out_bias, head):
    return [folded(gain), folded(shift), folded(out_bias)] + first_rows(head)


def named_call(name, body, ins, outs, scratch, collective_id=None):
    flat, counts = [], {}
    for key, item in scratch.items():
        items = item if isinstance(item, list) else [item]
        counts[key] = len(items)
        flat += items

    def inner(in_refs, out_refs, refs):
        buffers, at = {}, 0
        for key, count in counts.items():
            part = refs[at : at + count]
            buffers[key] = part if isinstance(scratch[key], list) else part[0]
            at += count
        body(dict(zip(ins, in_refs)), dict(zip(outs, out_refs)), buffers)

    results = staged_call(name, inner, list(ins.values()), list(outs.values()), flat, collective_id)
    return dict(zip(outs, results))


SUM_NAMES = ("gain", "shift", "out_bias", "head", "f_gain", "f_shift", "down_bias", "up_bias")


def run_backward(fast, top, saved, weights, gains, lengths, head_dim, carry=None, dec_sums=None):
    (hidden, slope, feed_input, middle), (attended, triple, logsum, normed, stream) = saved
    attn, up, down = weights
    planes, rows, hidden_width = hidden.shape
    wide, width = attn.shape[1], attn.shape[2] // 4
    encoder = len(top) == 3
    last = fast and encoder
    narrow = top[0].shape[1]
    strip = top[0].shape[0]
    deep = wide // 8 // planes
    tall = -(-deep // 32) * 32

    ins = {"lengths": ("near", lengths)}
    for key, value in zip(("rows", "input", "weight") if encoder else ("cotangent",), top):
        ins[key] = ("load" if encoder else "near", value)
    loads = {"feed_input": feed_input, "hidden": hidden, "slope": slope}
    loads.update(down=six_deep(down), up=six_deep(up), middle=middle)
    loads.update(attn=six_deep(attn), logsum=logsum, stream=stream)
    ins.update((key, ("load", value)) for key, value in loads.items())
    late_loads = {"triple": triple, "attended": attended, "normed": normed}
    ins.update((key, ("raw", value)) for key, value in late_loads.items())
    ins.update(attn_gain=("near", gains[0]), feed_gain=("near", gains[1]))

    sum_shapes = {key: (8, wide) for key in SUM_NAMES}
    sum_shapes.update(head=(planes, 8, 3 * width), up_bias=(planes, 8, hidden_width))
    if encoder:
        sum_shapes["bridge"] = (8, narrow)
    outs = {"input_grad": ("store", (rows, wide), BF16)}
    scratch = {
        "upstream": pltpu.VMEM((rows, wide), F32 if encoder else BF16),
        "middle_grad": pltpu.VMEM((rows, wide), F32),
        "branch": pltpu.VMEM((rows, wide), BF16),
        "branch_turned": pltpu.VMEM((wide, rows), BF16),
        "turned": pltpu.VMEM((wide + 16, rows), BF16),
        "triple_grad": pltpu.VMEM((rows, 3 * width), BF16),
        "late_sem": pltpu.SemaphoreType.DMA((3,)),
        "flush_sem": pltpu.SemaphoreType.DMA((3, planes)),
    }
    if encoder:
        scratch["total"] = pltpu.VMEM((rows, wide), F32)
    else:
        scratch["total"] = pltpu.VMEM((rows, wide), F32)
    if last:
        scratch.update((key, pltpu.VMEM(shape, F32)) for key, shape in sum_shapes.items())
    else:
        outs.update((key, ("near", shape, F32)) for key, shape in sum_shapes.items())
    feed_shape, attn_shape = (wide // 8, hidden_width), (wide // 8, 4 * width)
    flushed = () if last else ("attn",) if fast else ("attn", "up", "down")
    for key in flushed:
        outs[key + "_part"] = ("raw", loads[key].shape, BF16)
    shapes, names, resident = (), (), ()
    if fast:
        shapes, names, resident = (feed_shape, feed_shape), ("down", "up"), (0, 1)
    if last:
        shapes = (carry.shape[4:], (tall, narrow), feed_shape, feed_shape, attn_shape)
        names, resident = ("carry", "bridge_grad", "down", "up", "attn"), (1, 2, 3, 4)
        ins["carry"] = ("raw", carry)
        ins.update(("dec_" + key, ("near", dec_sums[key])) for key in SUM_NAMES)
        scratch["bridge_grad"] = pltpu.VMEM((planes, 2, 2, 2, tall, narrow), BF16)
        scratch["early"] = VectorSum.scratch(EARLY_ROWS, wide, planes)
        scratch["late"] = VectorSum.scratch(8, wide, planes)
        outs["early"] = ("near", (EARLY_ROWS, wide), F32)
        outs["late"] = ("near", (8, wide), F32)
    elif encoder:
        outs["bridge_grad"] = ("near", (wide, narrow), F32)
    if fast:
        scratch["reducer"] = Reducer.scratch(shapes, planes, resident)
        outs.update((key + "_sum", ("near", shape, F32)) for key, shape in zip(names, shapes))

    def body(ins, outs, buffers):
        length = ins["lengths"][lax.axis_index("mp")]
        sums = {key: (buffers if last else outs)[key] for key in sum_shapes}
        turned, total, middle_grad = buffers["turned"], buffers["total"], buffers["middle_grad"]
        upstream = buffers["upstream"]
        up, down, attn = (ins[key].ref for key in ("up", "down", "attn"))
        schedules = [[[] for _ in range(planes)] for _ in range(2)]
        if fast:
            reducer = Reducer(shapes, planes, buffers["reducer"])
            entry_barrier((reducer.mp, reducer.across_core, reducer.across_x, reducer.across_y))
            where = {"up": up, "down": down, "attn": attn}
            if last:
                where.update(carry=ins["carry"], bridge_grad=buffers["bridge_grad"])
            reducer.parts = [where[key] for key in names]
            at = {key: m for m, key in enumerate(names)}

            def todo(schedule, step, keys, ps):
                schedule += [partial(step, at[key], p) for p in ps for key in keys]

            feed, both = schedules[0], ("down", "up")
            core, plane, corner = reducer.core, reducer.plane, reducer.corner
            if last:
                for p in range(planes):
                    reducer.begin(at["carry"], p)
                others = ("carry", "bridge_grad")
                todo(feed[0], core, others, range(4))
                todo(feed[1], plane, others, range(4))
                todo(feed[1], core, both, (0,))
                todo(feed[2], corner, others, range(4))
                todo(feed[2], core, both, (1,))
                todo(feed[2], plane, both, (0,))
                todo(feed[3], core, both, (2,))
                todo(feed[3], plane, both, (1,))
                rest = schedules[1]
                todo(rest[0], plane, both, (2,))
                todo(rest[0], corner, both, (0,))
                todo(rest[1], plane, both, (3,))
                todo(rest[1], corner, both, (1,))
                todo(rest[1], core, ("attn",), (0,))
                todo(rest[2], corner, both, (2,))
                todo(rest[2], core, ("attn",), (1,))
                todo(rest[2], plane, ("attn",), (0,))
                todo(rest[3], corner, both, (3,))
                todo(rest[3], core, ("attn",), (2,))
                todo(rest[3], plane, ("attn",), (1,))
            else:
                todo(feed[1], core, both, (0,))
                todo(feed[2], core, both, (1,))
                todo(feed[2], plane, both, (0,))
                todo(feed[3], core, both, (2,))
                todo(feed[3], plane, both, (1,))
                todo(feed[3], corner, both, (0,))
                rest = schedules[1]
                todo(rest[0], plane, both, (2, 3))
                todo(rest[0], corner, both, (1,))
                todo(rest[1], corner, both, (2, 3))

        def flush(key, p):
            part = ins[key].ref.at[p]
            target = outs[key + "_part"].at[p]
            sem = buffers["flush_sem"].at[("attn", "up", "down").index(key), p]
            return pltpu.make_async_copy(part, target, sem)

        def leave(keys):
            def act(p):
                for key in keys:
                    if key in names:
                        reducer.begin(at[key], p)
                    if key in flushed:
                        flush(key, p).start()

            return act

        if encoder:
            put_transposed(ins["input"].use()[...], turned)
            both_grads = dot(turned[...], ins["rows"].use()[...])
            sums["bridge"][...] = both_grads[wide : wide + 8]
            if last:
                for g in range(8):
                    for p in range(planes):
                        low = (g * planes + p) * deep
                        part = both_grads[low : low + deep]
                        part = jnp.concatenate([part, jnp.zeros((tall - deep, narrow), F32)], 0)
                        grads = buffers["bridge_grad"]
                        grads[p, g // 4, g // 2 % 2, g % 2] = part.astype(BF16)
                for p in range(planes):
                    reducer.begin(at["bridge_grad"], p)
            else:
                outs["bridge_grad"][...] = both_grads[:wide]
            upstream[...] = dot(ins["rows"].use()[...], ins["weight"].use()[...], NT)
        else:
            upstream[rows - 32 :, :] = jnp.zeros((32, wide), BF16)
            upstream[:strip, :] = ins["cotangent"][...]

        def hook_of(schedule, keys):
            first, then = leave(keys), at_planes(schedule)

            def hook(p):
                first(p)
                then(p)

            return hook

        branches = [buffers[key] for key in ("branch", "branch_turned", "turned")]
        feed_saved = [ins[key].use() for key in ("hidden", "slope", "feed_input")]
        for key in ("down", "up"):
            ins[key].use()
        feed_backward(
            upstream,
            feed_saved,
            (up, down),
            branches,
            (sums["down_bias"], sums["up_bias"]),
            middle_grad,
            hook_of(schedules[0], ("down", "up")),
        )
        hidden, slope, feed_input = feed_saved
        spots = {
            "triple": hidden.at[:, :, : triple.shape[2]],
            "attended": slope.at[:, :, : attended.shape[2]],
            "normed": feed_input,
        }
        late = {
            key: Load(ins[key], spot, buffers["late_sem"].at[k])
            for k, (key, spot) in enumerate(spots.items())
        }
        layer_backward(
            ins["middle"].use(),
            ins["feed_gain"],
            upstream,
            middle_grad,
            sums["f_gain"],
            sums["f_shift"],
        )
        if fast:
            for key in ("down", "up"):
                reducer.core(at[key], 3)
        if last:
            early, late_sum = VectorSum(buffers["early"]), VectorSum(buffers["late"])
            feed_sums = [sums[key] for key in ("f_gain", "f_shift", "down_bias", "up_bias")]
            dec_sums = [ins["dec_" + key] for key in SUM_NAMES]
            early.levels[0] = stack_rows(early_rows(feed_sums, dec_sums, sums["bridge"]), wide)
            early.begin()
            for level in range(3):
                schedules[1][level].append(partial(early.advance, level))
        attn_saved = [late["attended"].use(), late["triple"].use(), ins["logsum"].use()]
        attn_saved.append(late["normed"].use())
        ins["attn"].use()
        attn_backward(
            head_dim,
            length,
            middle_grad,
            attn_saved,
            attn,
            branches + [buffers["triple_grad"]],
            (sums["out_bias"], sums["head"]),
            total,
            hook_of(schedules[1], ("attn",)),
        )
        if last:
            reducer.core(at["attn"], 3)
            reducer.plane(at["attn"], 2)
        layer_backward(
            ins["stream"].use(),
            ins["attn_gain"],
            middle_grad,
            total,
            sums["gain"],
            sums["shift"],
        )
        if last:
            late_sum.levels[0] = stack_rows(
                late_rows(*(sums[key] for key in ("gain", "shift", "out_bias", "head"))), wide
            )
            late_sum.begin()
        grad = outs["input_grad"]

        @row_blocks(rows)
        def _(i):
            grad.ref[block_at(i), :] = total[block_at(i), :].astype(BF16)

        grad.flush()
        if last:
            m = at["attn"]
            reducer.corner(m, 0)
            late_sum.advance(0)
            reducer.plane(m, 3)
            late_sum.advance(1)
            reducer.corner(m, 1)
            reducer.corner(m, 2)
            late_sum.advance(2)
            for key in ("carry", "bridge_grad", "down", "up"):
                reducer.finish(at[key], outs[key + "_sum"])
            reducer.corner(m, 3)
            early.finish(outs["early"])
            late_sum.finish(outs["late"])
            reducer.finish(m, outs["attn_sum"])
        elif fast:
            for key in names:
                reducer.finish(at[key], outs[key + "_sum"])
        if fast:
            reducer.drain()
        for key in flushed:
            for p in range(planes):
                flush(key, p).wait()

    name = "backward_encoder" if encoder else "backward_decoder"
    barrier = (2 if encoder else 1) if fast else None
    return named_call(name, body, ins, outs, scratch, barrier)


def pack_attention(proj, out, turned=False):
    if turned:
        return jnp.concatenate([proj[0], proj[1], proj[2], out], 0).T
    return jnp.concatenate([proj[0], proj[1], proj[2], out.T], -1)


def bias_rows(head_bias, up_bias):
    return [
        jnp.concatenate(
            [head_bias[0:1], jnp.zeros((1, head_bias.shape[1]), F32), head_bias[1:2]], -1
        ),
        up_bias.reshape(1, -1),
    ]


def run_forward(patches, lengths, enc, dec, vectors, bridge, fast):
    enc_vectors, dec_vectors = vectors
    bridge_weight, bridge_bias = bridge
    planes = lengths.shape[0]
    strip, wide = patches.shape
    narrow = bridge_weight.shape[1]
    rows = -(-strip // 32) * 32
    attns, heads, feeds = [], [], []
    for block in (enc, dec):
        _, _, proj, head_bias, out, _, _, _, up, up_bias, down, _ = block
        attns.append((proj, out))
        heads.append((head_bias, up_bias))
        feeds.append((up, down))
    small_shape = (8, feeds[0][0].shape[1])
    packed = [(proj.shape[1], 4 * proj.shape[2]) for proj, _ in attns]
    kinds = [packed[0][1], feeds[0][0].shape[1], None, packed[1][1], feeds[1][0].shape[1], None]
    mat_shapes = [packed[0], feeds[0][0].shape, feeds[0][1].shape]
    mat_shapes += [packed[1], feeds[1][0].shape, feeds[1][1].shape]
    count = len(mat_shapes)
    small_whole = wholes = None
    if not fast:
        mats = [m for attn, feed in zip(attns, feeds) for m in (pack_attention(*attn),) + feed]
        wholes = [lax.all_gather(m, "mp", axis=0) for m in mats]
        small = stack_rows([r for pair in heads for r in bias_rows(*pair)], small_shape[1])
        small_whole = lax.all_gather(small, "mp", axis=0)

    def block_outs(columns, width, hidden, head_dim):
        return [
            ("store", (rows, columns), BF16),
            ("store", (planes, rows, whole_lanes(3 * width)), BF16),
            ("store", (planes, rows, whole_lanes(width)), BF16),
            ("store", (planes, width // head_dim, rows), F32),
            ("store", (rows, columns), F32),
            ("store", (rows, columns), BF16),
            ("store", (planes, rows, hidden), BF16),
            ("store", (planes, rows, hidden), BF16),
        ]

    outs = block_outs(wide, kinds[0] // 4, kinds[1], HEAD)
    outs += block_outs(narrow, kinds[3] // 4, kinds[4], DHEAD)
    outs += [
        ("store", (rows, wide), BF16),
        ("store", (rows, wide), BF16),
        ("store", (rows, narrow), F32),
        ("near", (strip, narrow), BF16),
    ]
    ins = [("near", lengths), ("near", patches)]
    ins += [("near", v) for v in enc_vectors + dec_vectors + (bridge_bias,)]
    ins += [("load", bridge_weight)]
    first = len(ins)
    scratch = [pltpu.VMEM((rows, wide), F32), pltpu.VMEM((rows, narrow), F32)]
    if fast:
        turned = [stands(*proj.shape[1:]) for proj, _ in attns]
        for (proj, out), turn in zip(attns, turned):
            ins += [("near", jnp.swapaxes(proj, 1, 2) if turn else proj), ("near", out)]
        ins += [("near", v) for pair in heads for v in pair]
        ins += [("raw", v) for pair in feeds for v in pair]
        outs += [("raw", (planes,) + shape, BF16) for shape in mat_shapes]
        scratch += [pltpu.VMEM((planes,) + shape, BF16) for shape in mat_shapes]
        scratch += [pltpu.VMEM((planes,) + small_shape, F32)]
        scratch += Gatherer.sems(count, planes)
    else:
        ins += [("load", w) for w in wholes] + [("near", small_whole)]

    def body(ins, outs, scratch):
        mp = lax.axis_index("mp")
        lengths, patches = ins[:2]
        enc, dec, bridge_bias = ins[2:8], ins[8:14], ins[14]
        enc_outs, dec_outs = outs[:8], outs[8:16]
        stream, bridge_input, bridged, decoded = outs[16:20]
        totals = scratch[:2]
        length = lengths[mp]
        if fast:
            weights, smalls = scratch[2 : 2 + count], scratch[2 + count]
            attn_refs, head_refs = ins[first : first + 4], ins[first + 4 : first + 8]
            up_down = ins[first + 8 : first + 12]
            sources = [weights[0].at[mp], *up_down[:2], weights[3].at[mp], *up_down[2:]]
            gatherer = Gatherer(
                planes, sources, (0, 3), weights, outs[20:], smalls, scratch[3 + count :]
            )
            gatherer.begin()
            weights[0][mp] = pack_attention(attn_refs[0][...], attn_refs[1][...], turned[0])
            weights[3][mp] = pack_attention(attn_refs[2][...], attn_refs[3][...], turned[1])
            heads = [ref[...] for ref in head_refs]
            small_rows = bias_rows(*heads[:2]) + bias_rows(*heads[2:])
            smalls[mp] = stack_rows(small_rows, small_shape[1])
            entry_barrier(
                (mp, gatherer.across_core, gatherer.across_x, gatherer.across_y)
            )
            units = [(0, i) for i in range(3)] + [(m, i) for i in range(3) for m in (1, 2)]
            units += [(3, i) for i in range(3)] + [(m, i) for i in range(3) for m in (4, 5)]
            lag, ahead = 2, 6
            stages = (
                (0, gatherer.along_z),
                (ahead, gatherer.to_plane),
                (ahead + lag, gatherer.to_corner),
                (ahead + 2 * lag, gatherer.to_core),
                (ahead + 3 * lag, gatherer.whole),
            )

            def ticks(start, stop):
                for tick in range(start, stop):
                    for late, stage in stages:
                        if 0 <= tick - late < len(units):
                            stage(*units[tick - late])

            def before_steps(own, cuts):
                def before(k):
                    for step in range(planes):

                        @pl.when(k == step)
                        def _():
                            if step == 0:
                                for m in own:
                                    gatherer.have_own(m)
                            ticks(cuts[step], cuts[step + 1])

                return before

            depth = ahead + 3 * lag
            befores = (
                before_steps((0,), (ahead, ahead, depth + 1, depth + 2, depth + 3)),
                before_steps((1, 2), (depth + 3, depth + 3, depth + 5, depth + 7, depth + 9)),
                before_steps((3,), (depth + 9, depth + 9, depth + 10, depth + 11, depth + 12)),
                before_steps((4, 5), (depth + 12, depth + 12, depth + 14, depth + 16, depth + 18)),
            )
            order = lambda k: order_of(k, mp)
            gatherer.begin_small()
            ticks(0, ahead)
        else:
            weights, smalls = [w.use() for w in ins[first : first + count]], ins[first + count]
            order = lambda k: k
            befores = (nothing,) * 4

        tail = slice(rows - 32, rows)
        stream.ref[tail, :] = jnp.zeros((32, wide), BF16)
        stream.ref[:strip, :] = patches[...]
        stream.flush()
        if fast:
            gatherer.have_small()

        def bias(row, columns):
            return lambda p: smalls[p, row : row + 1, :columns]

        def block(source, vectors, weights, row, outs, head_dim, total, befores):
            gain, shift, out_bias, feed_gain, feed_shift, down_bias = vectors
            attn, up, down = weights
            refs = [out.ref for out in outs]
            attn_forward(
                head_dim,
                length,
                source,
                attn,
                (gain, shift, out_bias),
                bias(row, attn.shape[2] // 4 * 3),
                refs[:5],
                order,
                befores[0],
            )
            for out in outs[:5]:
                out.flush()
            feed_forward(
                refs[4],
                up,
                down,
                (feed_gain, feed_shift, down_bias),
                bias(row + 1, refs[6].shape[2]),
                refs[5:8],
                total,
                order,
                befores[1],
            )
            for out in outs[5:8]:
                out.flush()

        block(stream.ref, enc, weights[:3], 0, enc_outs, HEAD, totals[0], befores[:2])
        bridge_input.ref[...] = totals[0][...].astype(BF16)
        bridge_input.flush()
        bridged.ref[...] = dot(bridge_input.ref[...], ins[first - 1].use()[...]) + as_row(bridge_bias)
        bridged.flush()
        block(bridged.ref, dec, weights[3:], 2, dec_outs, DHEAD, totals[1], befores[2:])
        decoded[...] = totals[1][:strip, :].astype(BF16)
        if fast:
            gatherer.drain()

    results = staged_call("forward", body, ins, outs, scratch, 0 if fast else None)

    def stored(outs, source):
        normed, triple, attended, logsum, middle, feed_input, hidden, slope = outs
        return (
            (hidden, slope, feed_input, middle),
            (attended, triple, logsum, normed, source),
        )

    stream, bridge_input, bridged, decoded, *gathered = results[16:]
    return (
        stored(results[:8], stream),
        stored(results[8:16], bridged),
        bridge_input,
        decoded,
        gathered if fast else wholes,
    )


def stands(tall, flat):
    return tall % 128 == 0 and flat % 128 != 0


def run_outputs(rows, early, late, enc_sums, dec_sums, bridge_sum, sizes, bridge_shape):
    planes, groups = sizes["mp"], sizes["dp"]
    decoded, patches_grad = rows
    strip = decoded.shape[0]
    wide, narrow = bridge_shape
    deep = wide // groups // planes

    def block_shapes(columns, mats):
        width, hidden = mats[0].shape[1] // 4, mats[1].shape[1]
        each, piece = columns // groups // planes, columns // groups
        return [
            (each,),
            (each,),
            (3, piece, width),
            (2, width // groups),
            (piece, width) if stands(width, piece) else (width, piece),
            (each,),
            (each,),
            (each,),
            (piece, hidden),
            (hidden // groups,),
            (piece, hidden) if stands(hidden, piece) else (hidden, piece),
            (each,),
        ]

    shapes = block_shapes(wide, enc_sums) + [(deep, narrow), (narrow // groups // planes,)]
    shapes += block_shapes(narrow, dec_sums)
    ins = [decoded, patches_grad, early, late, *enc_sums, *dec_sums, bridge_sum]

    def kernel(*refs):
        decoded, patches_grad, early, late = refs[:4]
        enc, dec, bridge_sum = refs[4:7], refs[7:10], refs[10]
        decoded_out, patches_out, *outs = refs[11:]
        decoded_out[...] = decoded[...]
        patches_out[...] = patches_grad[:strip, :]
        dp, mp = lax.axis_index("dp"), lax.axis_index("mp")
        lanes = early.shape[1]

        def cut(values, low, size):
            values = pltpu.roll(values, lax.rem(lanes - low, lanes), 1)
            return values[:, :size]

        def put_rows(values, targets):
            for k, target in enumerate(targets):
                target[...] = values[k]

        def block(mats, outs, columns, first, row, second, up_row, head_row):
            attn, up, down = mats
            width, hidden = attn.shape[1] // 4, up.shape[1]
            gain, shift, proj, head, out, out_bias, f_gain, f_shift, up_out, up_bias, down_out, d_bias = outs
            for j in range(3):
                proj[j] = attn[:, j * width : (j + 1) * width]
            out_grad = attn[:, 3 * width :]
            out[...] = out_grad if out.shape == out_grad.shape else out_grad.T
            up_out[...] = up[...]
            down_out[...] = down[...] if down_out.shape == down.shape else down[...].T
            each = columns // groups // planes
            low = (dp * planes + mp) * each
            put_rows(cut(first[row : row + 8, :], low, each), (gain, shift, out_bias))
            lane, ref = second
            put_rows(cut(ref[lane : lane + 8, :], low, each), (f_gain, f_shift, d_bias))
            line = up_row[0][pl.ds(up_row[1] + mp, 1), :]
            put_rows(cut(line, dp * (hidden // groups), hidden // groups), (up_bias,))
            line = head_row[0][pl.ds(head_row[1] + mp, 1), :]
            piece = width // groups
            head[0:1, :] = cut(line, dp * piece, piece)
            head[1:2, :] = cut(line, 2 * width + dp * piece, piece)

        at = EARLY_DEC
        block(enc, outs[:12], wide, late, 0, (0, early), (early, 3), (late, 3))
        block(dec, outs[14:], narrow, early, at, (at + 8, early), (early, at + 3), (early, at + 11))
        outs[12][...] = bridge_sum[:deep, :]
        each = narrow // groups // planes
        line = cut(early[at + 15 : at + 16, :], (dp * planes + mp) * each, each)
        put_rows(line, (outs[13],))

    results = pl.pallas_call(
        kernel,
        out_shape=[
            jax.ShapeDtypeStruct(decoded.shape, BF16),
            jax.ShapeDtypeStruct((strip, wide), BF16),
        ]
        + [jax.ShapeDtypeStruct(shape, F32) for shape in shapes],
        in_specs=[IN_VMEM] * len(ins),
        out_specs=[IN_VMEM] * (2 + len(shapes)),
        compiler_params=pltpu.CompilerParams(vmem_limit_bytes=VMEM_BYTES),
        name="outputs",
    )(*ins)
    first, second = list(results[2:14]), list(results[16:28])
    for block, mats in ((first, enc_sums), (second, dec_sums)):
        for at, (tall, flat) in ((4, (mats[0].shape[1] // 4, mats[0].shape[0])), (10, mats[2].shape[::-1])):
            block[at] = block[at] if block[at].shape == (tall, flat) else block[at].T
    return (*results[:2], *first, *results[14:16], *second)


def shards(sizes, *inputs):
    patches, lengths = inputs[:2]
    cotangent = inputs[28]
    planes, groups = sizes["mp"], sizes["dp"]
    fast = groups == 8 and planes == 4
    strip, wide = patches.shape
    enc, (bridge_weight, bridge_bias), dec = inputs[2:14], inputs[14:16], inputs[16:28]

    def vectors_of(block):
        gain, shift, _, _, _, out_bias, f_gain, f_shift, _, _, _, d_bias = block
        return (gain, shift, out_bias, f_gain, f_shift, d_bias)

    enc_vectors, dec_vectors = vectors_of(enc), vectors_of(dec)
    enc_stored, dec_stored, bridge_input, decoded, wholes = run_forward(
        patches, lengths, enc, dec, (enc_vectors, dec_vectors), (bridge_weight, bridge_bias), fast
    )
    dec_gains, enc_gains = (dec[0], dec[6]), (enc[0], enc[6])
    down = run_backward(
        fast, (cotangent,), dec_stored, wholes[3:], dec_gains, lengths, DHEAD
    )
    dec_sums = {key: down[key] for key in SUM_NAMES}
    bridge = (down["input_grad"], bridge_input, bridge_weight)
    on = run_backward(
        fast,
        bridge,
        enc_stored,
        wholes[:3],
        enc_gains,
        lengths,
        HEAD,
        down["attn_part"] if fast else None,
        dec_sums,
    )
    if fast:
        enc_grads = (on["attn_sum"], on["up_sum"], on["down_sum"])
        dec_grads = (on["carry_sum"], down["up_sum"], down["down_sum"])
        early, late, bridge_sum = on["early"], on["late"], on["bridge_grad_sum"]
    else:
        feed_sums = [on[key] for key in ("f_gain", "f_shift", "down_bias", "up_bias")]
        rows = early_rows(feed_sums, [dec_sums[key] for key in SUM_NAMES], on["bridge"])
        early = stack_rows(rows, wide)
        late = stack_rows(late_rows(*(on[key] for key in SUM_NAMES[:4])), wide)
        early, late = lax.psum(early, ("dp", "mp")), lax.psum(late, ("dp", "mp"))

        def in_groups(grad):
            return collect(grad.reshape(planes, groups, -1, grad.shape[-1]), sizes)

        keys = ("attn_part", "up_part", "down_part")
        dec_grads = tuple(in_groups(down[key]) for key in keys)
        enc_grads = tuple(in_groups(on[key]) for key in keys)
        deep = wide // planes // groups
        bridge_part = on["bridge_grad"].reshape(groups, planes, deep, -1).transpose(1, 0, 2, 3)
        bridge_sum = collect(bridge_part, sizes)
    patches_grad = on["input_grad"]
    return run_outputs(
        (decoded, patches_grad),
        early,
        late,
        enc_grads,
        dec_grads,
        bridge_sum,
        sizes,
        bridge_weight.shape,
    )


def solution(mesh):
    block_in = (
        P(),
        P(),
        P(None, None, "mp"),
        P(None, "mp"),
        P("mp", None),
        P(),
        P(),
        P(),
        P(None, "mp"),
        P("mp"),
        P("mp", None),
        P(),
    )
    both = P(("dp", "mp"))
    block_out = (
        both,
        both,
        P(None, "dp", "mp"),
        P(None, ("mp", "dp")),
        P("mp", "dp"),
        both,
        both,
        both,
        P("dp", "mp"),
        P(("mp", "dp")),
        P("mp", "dp"),
        both,
    )
    rows = P(("dp", "mp"), None)
    return jax.shard_map(
        partial(shards, dict(mesh.shape)),
        mesh=mesh,
        in_specs=(rows, P("dp")) + block_in + (P(), P()) + block_in + (rows,),
        out_specs=(rows, rows) + block_out + (rows, both) + block_out,
        check_vma=False,
    )
```

```python
from functools import partial

import jax
import jax.numpy as jnp
from jax import lax
from jax.experimental import pallas as pl
from jax.experimental.pallas import tpu as pltpu
from jax.sharding import PartitionSpec as P

HEAD = 64
DHEAD = 32
EPSILON = 1e-06
MESH = pl.DeviceIdType.MESH
F32 = jnp.float32
BF16 = jnp.bfloat16
VMEM_BYTES = 60 * 1024 * 1024


def neighbours():
    dp, mp = lax.axis_index("dp"), lax.axis_index("mp")
    core, x, y = dp % 2, (dp // 2) % 2, dp // 4
    across_core = dp + 1 - 2 * core
    across_x = dp + 2 - 4 * x
    across_y = dp + 4 - 8 * y
    return dp, mp, core, x, y, across_core, across_x, across_y


def entry_barrier(parts):
    mp, across_core, across_x, across_y = parts
    dp = lax.axis_index("dp")
    barrier = pltpu.get_barrier_semaphore()
    planes = lax.axis_size("mp")
    for other in (across_core, across_x, across_y):
        pl.semaphore_signal(barrier, inc=1, device_id=(other, mp), device_id_type=MESH)
    for step in range(1, planes):
        pl.semaphore_signal(
            barrier, inc=1, device_id=(dp, (mp + step) % planes), device_id_type=MESH
        )
    pl.semaphore_wait(barrier, 3 + planes - 1)


def plane_order(mp, planes):
    if planes != 4:
        return [(mp + step) % planes for step in range(1, planes)]
    upper = mp // 2
    place = mp + upper * (3 - 2 * mp)
    return [o + upper * (3 - 2 * o) for o in (place + 1, 2 - 2 * place, 3)]


def order_of(k, mp):
    upper = mp // 2
    place = mp + upper * (3 - 2 * mp)
    plane = (k + place) % 3 * (1 - k // 3) + 3 * (k // 3)
    return plane + upper * (3 - 2 * plane)


class Layout:
    def __init__(self, pair):
        self.pair = pair

    def block(self, ref, p, y, x, core):
        return ref.at[p, :, y, x, core] if self.pair else ref.at[p, y, x, core]

    def half(self, ref, p, y, x, core, h):
        return ref.at[p, h, y, x, core] if self.pair else ref.at[p, y, x, core, h]

    def matrices(self, ref, p):
        if self.pair:
            return ref[p, 0].reshape(-1, ref.shape[-1]), ref[p, 1].reshape(-1, ref.shape[-1])
        return (ref[p].reshape(-1, ref.shape[-1]),)

    def in_core(self, ref, p, y, x):
        return ref.at[p, :, y, x] if self.pair else ref.at[p, y, x]


PAIR, ONE = Layout(True), Layout(False)
ALL = slice(None)


def as_pair(first, second):
    both = jnp.stack([first, second], 1)
    planes, _, rows, columns = both.shape
    return both.reshape(planes, 2, 2, 2, 2, rows // 8, columns)


def as_one(array):
    planes, rows, columns = array.shape
    return array.reshape(planes, 2, 2, 2, 2, rows // 16, columns)


class Gatherer:
    A, X, Y, DY, DX, S = range(6)
    kinds = 6

    def __init__(self, planes, layouts, wholes, targets, smalls, sems):
        self.planes, self.count, self.layouts = planes, len(wholes), layouts
        self.wholes, self.targets, self.smalls = wholes, targets, smalls
        self.flush_sem, self.send_sem, self.recv_sem = sems
        self.dp, self.mp, self.core, self.x, self.y, *across = neighbours()
        self.across_core, self.across_x, self.across_y = across
        self.others = plane_order(self.mp, planes)

    @staticmethod
    def sems(count, planes):
        return [
            pltpu.SemaphoreType.DMA((count, planes)),
            pltpu.SemaphoreType.DMA((count + 1, planes, Gatherer.kinds)),
            pltpu.SemaphoreType.DMA((count + 1, planes, Gatherer.kinds)),
        ]

    def remote(self, m, kind, src, dst, send_plane, recv_plane, target):
        return pltpu.make_async_remote_copy(
            src_ref=src,
            dst_ref=dst,
            send_sem=self.send_sem.at[m, send_plane, kind],
            recv_sem=self.recv_sem.at[m, recv_plane, kind],
            device_id=target,
            device_id_type=MESH,
        )

    def piece(self, m, plane, y, x, core, half=None):
        layout, ref = self.layouts[m], self.wholes[m]
        if half is None:
            return layout.block(ref, plane, y, x, core)
        return layout.half(ref, plane, y, x, core, half)

    def send(self, m, i, kind):
        plane = self.others[i]
        x, y, core = self.x, self.y, self.core
        if kind == self.A:
            below = (self.mp - plane + self.planes - 1) // self.planes
            part = self.piece(m, plane, y, x, core)
            target = (self.dp, self.clamped(self.mp - 1 + 2 * below))
            return self.remote(m, kind, part, part, plane, plane, target)
        part, target = {
            self.X: (self.piece(m, plane, y, x, core), self.across_x),
            self.Y: (self.piece(m, plane, y, x, core), self.across_y),
            self.DY: (self.piece(m, plane, y, 1 - x, core, 0), self.across_y),
            self.DX: (self.piece(m, plane, 1 - y, x, core, 1), self.across_x),
            self.S: (self.piece(m, plane, ALL, ALL, core), self.across_core),
        }[kind]
        return self.remote(m, kind, part, part, plane, plane, (target, self.mp))

    def arrived(self, m, i, kind):
        plane = self.others[i]
        x, y, core = self.x, self.y, self.core
        part = {
            self.A: self.piece(m, plane, y, x, core),
            self.X: self.piece(m, plane, y, 1 - x, core),
            self.Y: self.piece(m, plane, 1 - y, x, core),
            self.DY: self.piece(m, plane, 1 - y, 1 - x, core, 0),
            self.DX: self.piece(m, plane, 1 - y, 1 - x, core, 1),
            self.S: self.piece(m, plane, ALL, ALL, 1 - core),
        }[kind]
        self.remote(m, kind, part, part, plane, plane, (self.across_core, self.mp)).wait_recv()

    def clamped(self, plane):
        return jnp.clip(plane, 0, self.planes - 1)

    def goes_on(self, i):
        below = (self.mp - self.others[i] + self.planes - 1) // self.planes
        target = self.mp - 1 + 2 * below
        return (target >= 0) & (target < self.planes)

    def outward(self, m, up):
        part = self.piece(m, self.mp, self.y, self.x, self.core)
        copy = pltpu.make_async_remote_copy(
            src_ref=part,
            dst_ref=part,
            send_sem=self.send_sem.at[m, self.mp, self.X if up else self.Y],
            recv_sem=self.recv_sem.at[m, self.mp, self.A],
            device_id=(self.dp, self.clamped(self.mp + (1 if up else -1))),
            device_id_type=MESH,
        )
        return copy, self.mp < self.planes - 1 if up else self.mp > 0

    def along_z(self, m):
        for up in (True, False):
            copy, there = self.outward(m, up)
            pl.when(there)(copy.start)

    def to_plane(self, m, i):
        self.arrived(m, i, self.A)
        pl.when(self.goes_on(i))(self.send(m, i, self.A).start)
        self.send(m, i, self.X).start()
        self.send(m, i, self.Y).start()

    def to_corner(self, m, i):
        self.arrived(m, i, self.X)
        self.send(m, i, self.DY).start()
        self.arrived(m, i, self.Y)
        self.send(m, i, self.DX).start()

    def to_core(self, m, i):
        self.arrived(m, i, self.DY)
        self.arrived(m, i, self.DX)
        self.send(m, i, self.S).start()

    def flush(self, m, plane):
        return pltpu.make_async_copy(
            self.wholes[m].at[plane], self.targets[m].at[plane], self.flush_sem.at[m, plane]
        )

    def whole(self, m, i):
        self.arrived(m, i, self.S)
        self.flush(m, self.others[i]).start()

    def send_small(self, i):
        plane = self.others[i]
        part = self.smalls.at[self.mp]
        return self.remote(self.count, self.A, part, part, plane, self.mp, (self.dp, plane))

    def begin_small(self):
        for i in range(self.planes - 1):
            self.send_small(i).start()

    def have_small(self):
        for plane in self.others:
            part = self.smalls.at[plane]
            target = (self.across_core, self.mp)
            self.remote(self.count, self.A, part, part, plane, plane, target).wait_recv()

    def drain(self):
        for m in range(self.count):
            for up in (True, False):
                copy, there = self.outward(m, up)
                pl.when(there)(copy.wait_send)
            for i in range(self.planes - 1):
                for kind in range(1, self.kinds):
                    self.send(m, i, kind).wait_send()
                pl.when(self.goes_on(i))(self.send(m, i, self.A).wait_send)
            for p in range(self.planes):
                self.flush(m, p).wait()
        for i in range(self.planes - 1):
            self.send_small(i).wait_send()


class Reducer:
    def __init__(self, kinds, planes, turns, refs):
        self.planes, self.count, self.kinds, self.turns = planes, len(kinds), kinds, turns
        refs = list(refs)
        take = lambda: [refs.pop(0) for _ in range(self.count)]
        self.mine, self.from_core, self.from_x, self.from_y = take(), take(), take(), take()
        self.then_y, self.then_x, self.from_z = take(), take(), take()
        self.local_sem, self.send_sem, self.recv_sem = refs
        self.dp, self.mp, self.core_id, self.x, self.y, *across = neighbours()
        self.across_core, self.across_x, self.across_y = across
        self.parts = [None] * self.count

    @staticmethod
    def scratch(kinds, planes):
        count = len(kinds)

        def buffers(*lead, skip=False):
            return [
                pltpu.VMEM((1, 16, 128) if skip and resident else (planes,) + lead + half, BF16)
                for _, half, resident, _ in kinds
            ]

        return (
            buffers(2, 2, 2, skip=True)
            + buffers(2, 2, 2)
            + buffers(2)
            + buffers(2)
            + buffers()
            + buffers()
            + buffers(2)
            + [
                pltpu.SemaphoreType.DMA((count, planes)),
                pltpu.SemaphoreType.DMA((count, planes, 6)),
                pltpu.SemaphoreType.DMA((count, planes, 6)),
            ]
        )

    def remote(self, m, p, kind, src, dst, target, recv_plane=None):
        return pltpu.make_async_remote_copy(
            src_ref=src,
            dst_ref=dst,
            send_sem=self.send_sem.at[m, p, kind],
            recv_sem=self.recv_sem.at[m, p if recv_plane is None else recv_plane, kind],
            device_id=target,
            device_id_type=MESH,
        )

    def piece(self, m, p, y, x, half=None):
        layout, _, resident, _ = self.kinds[m]
        if not resident:
            ref = layout.in_core(self.mine[m], p, y, x)
            if half is None:
                return ref
            return self.mine[m].at[p, half, y, x] if layout.pair else self.mine[m].at[p, y, x, half]
        if half is None:
            return layout.block(self.parts[m], p, y, x, self.core_id)
        return layout.half(self.parts[m], p, y, x, self.core_id, half)

    def fetch(self, m, p):
        src = self.kinds[m][0].block(self.parts[m], p, ALL, ALL, self.core_id)
        return pltpu.make_async_copy(src, self.mine[m].at[p], self.local_sem.at[m, p])

    def begin(self, m, p):
        if not self.kinds[m][2]:
            self.fetch(m, p).start()
        self.to_core(m, p).start()

    def to_core(self, m, p):
        src = self.kinds[m][0].block(self.parts[m], p, ALL, ALL, 1 - self.core_id)
        return self.remote(m, p, 0, src, self.from_core[m].at[p], (self.across_core, self.mp))

    def to_x(self, m, p):
        src = self.piece(m, p, ALL, 1 - self.x, 0)
        return self.remote(m, p, 1, src, self.from_x[m].at[p], (self.across_x, self.mp))

    def to_y(self, m, p):
        src = self.piece(m, p, 1 - self.y, ALL, 1)
        return self.remote(m, p, 2, src, self.from_y[m].at[p], (self.across_y, self.mp))

    def x_to_y(self, m, p):
        src = self.piece(m, p, 1 - self.y, self.x, 0)
        return self.remote(m, p, 3, src, self.then_y[m].at[p], (self.across_y, self.mp))

    def y_to_x(self, m, p):
        src = self.piece(m, p, self.y, 1 - self.x, 1)
        return self.remote(m, p, 4, src, self.then_x[m].at[p], (self.across_x, self.mp))

    def to_z(self, m, p):
        src = self.piece(m, p, self.y, self.x)
        return self.remote(m, p, 5, src, self.from_z[m].at[self.mp], (self.dp, p), self.mp)

    def core(self, m, p):
        layout = self.kinds[m][0]
        if not self.kinds[m][2]:
            self.fetch(m, p).wait()
        self.to_core(m, p).wait_recv()

        def add(y, x):
            ref = self.piece(m, p, y, x)
            ref[...] = ref[...] + layout.in_core(self.from_core[m], p, y, x)[...]

        for y in range(2):
            add(y, 1 - self.x)
        self.to_x(m, p).start()
        add(1 - self.y, self.x)
        self.to_y(m, p).start()
        add(self.y, self.x)

    def plane(self, m, p):
        self.to_x(m, p).wait_recv()
        for y in (1 - self.y, self.y):
            ref = self.piece(m, p, y, self.x, 0)
            ref[...] = ref[...] + self.from_x[m][p, y]
        self.x_to_y(m, p).start()
        self.to_y(m, p).wait_recv()
        for x in (1 - self.x, self.x):
            ref = self.piece(m, p, self.y, x, 1)
            ref[...] = ref[...] + self.from_y[m][p, x]
        self.y_to_x(m, p).start()

    def corner(self, m, p):
        self.x_to_y(m, p).wait_recv()
        self.y_to_x(m, p).wait_recv()
        for half, came in enumerate((self.then_y, self.then_x)):
            ref = self.piece(m, p, self.y, self.x, half)
            ref[...] = ref[...] + came[m][p]

        if p is not self.turns[-1]:
            self.to_z(m, p).start()

    def finish(self, m, out, partial_sum=None):
        ks = self.kinds[m][3]
        total = 0.0 if partial_sum is None else partial_sum[...]
        if self.planes - 1 in ks:
            total = total + self.piece(m, self.mp, self.y, self.x)[...].astype(F32)
        if 0 in ks:
            for step in range(1, self.planes):
                plane = (self.mp + step) % self.planes
                src = self.from_z[m].at[plane]
                self.remote(m, plane, 5, src, src, (self.dp, plane)).wait_recv()
                total = total + src[...].astype(F32)
        out[...] = total

    def drain(self):
        for m in range(self.count):
            for k in self.kinds[m][3]:
                p = self.turns[k]
                for copy in (self.to_core, self.to_x, self.to_y, self.x_to_y, self.y_to_x):
                    copy(m, p).wait_send()
                if k < self.planes - 1:
                    self.to_z(m, p).wait_send()


def collect(part, sizes):
    part = lax.psum_scatter(part, "mp", scatter_dimension=0, tiled=False)
    return lax.psum_scatter(part.astype(F32), "dp", scatter_dimension=0, tiled=False)


LOG2E = 1.4426950408889634
AG_LAG = 1
ROW_BLOCK = 32
NT = (((1,), (1,)), ((), ()))


def dot(left, right, dims=(((1,), (0,)), ((), ()))):
    return lax.dot_general(left, right, dims, preferred_element_type=F32)


def standardize(x):
    centered = x - jnp.mean(x, -1, keepdims=True)
    scale = lax.rsqrt(jnp.mean(centered * centered, -1, keepdims=True) + EPSILON)
    return centered * scale, scale


def gelu_and_slope(b):
    cdf = 0.5 * (1.0 + lax.erf(b * 0.7071067811865476))
    density = jnp.exp(-0.5 * b * b) * 0.3989422804014327
    return b * cdf, cdf + b * density


def fold_rows(x):
    return jnp.sum(x.reshape(x.shape[0] // 8, 8, x.shape[1]), 0)


def row_blocks(rows):
    return pl.loop(0, rows // ROW_BLOCK, unroll=rows // ROW_BLOCK)


def block_at(i):
    return pl.ds(pl.multiple_of(i * ROW_BLOCK, ROW_BLOCK), ROW_BLOCK)


def whole_lanes(columns):
    return -(-columns // 128) * 128


def strip_forward(head_dim, width, length, p, triple, attended, logsum):
    rows = triple.shape[1]
    visible = lax.broadcasted_iota(jnp.int32, (rows, 1), 0) < length
    factor = head_dim**-0.5 * LOG2E
    outs = []
    for head in range(width // head_dim):
        low = head * head_dim
        query = triple[p, :, low : low + head_dim]
        key = triple[p, :, width + low : width + low + head_dim]
        value = triple[p, :, 2 * width + low : 2 * width + low + head_dim]
        scores = jnp.where(visible, dot(key, query, NT) * factor, -1e30)
        ceiling = jnp.max(scores, 0, keepdims=True)
        exponent = jnp.exp2(scores - ceiling)
        denominator = jnp.sum(exponent, 0, keepdims=True)
        outs.append(dot(value.T, exponent.astype(BF16)) * (1.0 / denominator))
        logsum[p, head : head + 1, :] = ceiling + jnp.log2(denominator)
    attended[p, :, :width] = jnp.concatenate(outs, 0).T.astype(BF16)


def strip_backward(head_dim, width, length, p, triple, attended, mixed, logsum, out):
    rows = triple.shape[1]
    visible = lax.broadcasted_iota(jnp.int32, (rows, 1), 0) < length
    factor = head_dim**-0.5
    products = (mixed.astype(F32) * attended[p, :, :width].astype(F32)).T
    query_grads = []
    for head in range(width // head_dim):
        low = head * head_dim
        query = triple[p, :, low : low + head_dim]
        key = triple[p, :, width + low : width + low + head_dim]
        value = triple[p, :, 2 * width + low : 2 * width + low + head_dim]
        mixed_head = mixed[:, low : low + head_dim]
        row_sums = jnp.sum(products[low : low + head_dim], 0, keepdims=True)
        scores = dot(key, query, NT) * (factor * LOG2E) - logsum[p, head : head + 1, :]
        chances = jnp.exp2(jnp.where(visible, scores, -1e30))
        chance_grad = dot(value, mixed_head, NT)
        score_grad = (chances * (chance_grad - row_sums)).astype(BF16)
        key_grad = dot(score_grad, query) * factor
        value_grad = dot(chances.astype(BF16), mixed_head)
        query_grads.append(dot(key.T, score_grad) * factor)
        out[:, width + low : width + low + head_dim] = key_grad.astype(BF16)
        out[:, 2 * width + low : 2 * width + low + head_dim] = value_grad.astype(BF16)
    out[:, :width] = jnp.concatenate(query_grads, 0).T.astype(BF16)


def attn_forward(head_dim, length, stream, weight, vectors, bias_of, outs, order, before):
    gain, shift, out_bias = [as_row(v) for v in vectors]
    normed, triple, attended, logsum, middle = outs
    planes, rows = triple.shape[:2]
    width = weight.shape[-1] // 4

    @row_blocks(rows)
    def _(i):
        x = stream[block_at(i), :].astype(F32)
        normed[block_at(i), :] = (standardize(x)[0] * gain + shift).astype(BF16)
        middle[block_at(i), :] = x + out_bias

    @pl.loop(0, planes)
    def _(k):
        before(k)
        p = order(k)
        (own,) = ONE.matrices(weight, p)
        projected = dot(normed[...], own[:, : 3 * width]) + bias_of(p)
        triple[p, :, : 3 * width] = projected.astype(BF16)
        strip_forward(head_dim, width, length, p, triple, attended, logsum)
        middle[...] += dot(attended[p, :, :width], own[:, 3 * width :], NT)


def feed_forward(middle, weights, vectors, bias_of, outs, total, order, before):
    gain, shift, down_bias = [as_row(v) for v in vectors]
    feed_input, hidden, slope = outs
    planes, rows, width = hidden.shape

    @row_blocks(rows)
    def _(i):
        x = middle[block_at(i), :]
        feed_input[block_at(i), :] = (standardize(x)[0] * gain + shift).astype(BF16)
        total[block_at(i), :] = x + down_bias

    @pl.loop(0, planes)
    def _(k):
        before(k)
        p = order(k)
        bias = bias_of(p)
        up, down = PAIR.matrices(weights, p)
        for low in range(0, width, 256):
            part = slice(low, low + 256)
            activated, rise = gelu_and_slope(dot(feed_input[...], up[:, part]) + bias[:, part])
            hidden[p, :, part] = activated.astype(BF16)
            slope[p, :, part] = rise.astype(BF16)
        total[...] += dot(hidden[p], down)


def as_row(vector):
    return vector[...].reshape(1, -1)


def layer_backward(stream, gain, upstream, spare, gain_sums, shift_sums):
    gain_sums[...] = jnp.zeros_like(gain_sums)
    shift_sums[...] = jnp.zeros_like(shift_sums)
    gain = as_row(gain)

    @row_blocks(stream.shape[0])
    def _(i):
        hat, scale = standardize(stream[block_at(i), :].astype(F32))
        grad = spare[block_at(i), :]
        gain_sums[...] += fold_rows(grad * hat)
        shift_sums[...] += fold_rows(grad)
        grad = grad * gain
        part = grad - jnp.mean(grad, -1, keepdims=True)
        part = part - hat * jnp.mean(grad * hat, -1, keepdims=True)
        spare[block_at(i), :] = upstream[block_at(i), :].astype(F32) + part * scale


def put_transposed(values, turned):
    columns = values.shape[1]
    turned[:columns, :] = values.T
    turned[columns:, :] = jnp.ones((16, values.shape[0]), BF16)


def start_branch(upstream, branch, turned, sums, total):
    rows, wide = branch.shape
    sums[...] = jnp.zeros_like(sums)

    @row_blocks(rows)
    def _(i):
        rounded = upstream[block_at(i), :].astype(BF16)
        branch[block_at(i), :] = rounded
        sums[...] += fold_rows(rounded.astype(F32))
        total[block_at(i), :] = jnp.zeros((ROW_BLOCK, wide), F32)

    turned[...] = branch[...].T


def feed_backward(upstream, saved, weights, scratch, sums, total, order, ready, hook):
    hidden, slope, feed_input = saved
    branch, branch_turned, feed_turned = scratch
    branch_sums, up_sums = sums
    planes = hidden.shape[0]
    wide = branch.shape[1]
    start_branch(upstream, branch, branch_turned, branch_sums, total)
    put_transposed(feed_input[...], feed_turned)

    @pl.loop(0, planes)
    def _(k):
        p = order(k)
        ready(p)
        up, down = PAIR.matrices(weights, p)
        hidden_grad = dot(branch[...], down, NT)
        before_grad = (hidden_grad * slope[p].astype(F32)).astype(BF16)
        total[...] += dot(before_grad, up, NT)
        spot = weights.shape[2:]
        weights[p, 1] = dot(branch_turned[...], hidden[p]).astype(BF16).reshape(spot)
        both = dot(feed_turned[...], before_grad)
        weights[p, 0] = both[:wide].astype(BF16).reshape(spot)
        up_sums[p] = both[wide : wide + 8]
        hook(k, p)


def attn_backward(
    head_dim, length, upstream, saved, weight, scratch, sums, total, order, ready, hook
):
    attended, triple, logsum, normed = saved
    branch, branch_turned, normed_turned, triple_grad = scratch
    branch_sums, head_sums = sums
    planes, width = attended.shape[0], weight.shape[-1] // 4
    wide = branch.shape[1]
    start_branch(upstream, branch, branch_turned, branch_sums, total)
    put_transposed(normed[...], normed_turned)

    @pl.loop(0, planes)
    def _(k):
        p = order(k)
        ready(p)
        (own,) = ONE.matrices(weight, p)
        out_weight = weight[p, :, :, :, :, :, 3 * width :].reshape(wide, width)
        mixed = dot(branch[...], out_weight).astype(BF16)
        strip_backward(head_dim, width, length, p, triple, attended, mixed, logsum, triple_grad)
        total[...] += dot(triple_grad[...], own[:, : 3 * width], NT)
        both = dot(normed_turned[...], triple_grad[...])
        out_grad = dot(branch_turned[...], attended[p, :, :width])
        grad = jnp.concatenate([both[:wide].astype(BF16), out_grad.astype(BF16)], -1)
        weight[p] = grad.reshape(weight.shape[1:])
        head_sums[p] = both[wide : wide + 8]
        hook(k, p)


IN_VMEM = pl.BlockSpec(memory_space=pltpu.VMEM)
IN_SMEM = pl.BlockSpec(memory_space=pltpu.SMEM)


class Load:
    def __init__(self, source, ref, sems):
        self.source, self.ref, self.sems, self.waits = source, ref, sems, False

    def copy(self, p=None):
        if p is None:
            return pltpu.make_async_copy(self.source, self.ref, self.sems.at[0])
        return pltpu.make_async_copy(self.source.at[p], self.ref.at[p], self.sems.at[p])

    def begin(self):
        self.copy().start()
        self.waits = True

    def begin_plane(self, p):
        self.copy(p).start()

    def use(self):
        if self.waits:
            self.copy().wait()
            self.waits = False
        return self.ref

    def ready(self, p):
        self.copy(p).wait()


class Store:
    def __init__(self, ref, target, sems):
        self.ref, self.target, self.sems, self.by_plane = ref, target, sems, False

    def flush(self, p=None):
        if p is None:
            pltpu.make_async_copy(self.ref, self.target, self.sems.at[0]).start()
        else:
            self.by_plane = True
            pltpu.make_async_copy(self.ref.at[p], self.target.at[p], self.sems.at[p]).start()

    def finish(self):
        if not self.by_plane:
            pltpu.make_async_copy(self.ref, self.target, self.sems.at[0]).wait()
            return
        for p in range(self.ref.shape[0]):
            pltpu.make_async_copy(self.ref.at[p], self.target.at[p], self.sems.at[p]).wait()


def staged_call(name, body, ins, outs, scratch=(), collective_id=None):
    any_spec = pl.BlockSpec(memory_space=pl.ANY)
    near = lambda v: IN_SMEM if v.dtype == jnp.int32 else IN_VMEM
    loads = [v for mode, v in ins if mode in ("load", "planes")]
    stores = [(shape, dtype) for mode, shape, dtype in outs if mode == "store"]
    scratch = list(scratch)

    def kernel(*refs):
        refs = list(refs)
        take = lambda n: [refs.pop(0) for _ in range(n)]
        in_refs, out_refs = take(len(ins)), take(len(outs))
        load_refs, store_refs, rest = take(len(loads)), take(len(stores)), take(len(scratch))
        load_sem, store_sem = refs
        given, load_at = [], 0
        for (mode, _), ref in zip(ins, in_refs):
            if mode in ("load", "planes"):
                given.append(Load(ref, load_refs[load_at], load_sem.at[load_at]))
                load_at += 1
                if mode == "load":
                    given[-1].begin()
            else:
                given.append(ref)
        results, store_at = [], 0
        for (mode, _, _), ref in zip(outs, out_refs):
            if mode == "store":
                results.append(Store(store_refs[store_at], ref, store_sem.at[store_at]))
                store_at += 1
            else:
                results.append(ref)
        body(given, results, rest)
        for item in given:
            if isinstance(item, Load):
                item.use()
        for item in results:
            if isinstance(item, Store):
                item.finish()

    params = {"vmem_limit_bytes": VMEM_BYTES}
    if collective_id is not None:
        params.update(collective_id=collective_id, has_side_effects=True)
    return pl.pallas_call(
        kernel,
        out_shape=[jax.ShapeDtypeStruct(shape, dtype) for _, shape, dtype in outs],
        in_specs=[near(v) if mode == "near" else any_spec for mode, v in ins],
        out_specs=[IN_VMEM if mode == "near" else any_spec for mode, _, _ in outs],
        scratch_shapes=[pltpu.VMEM(v.shape, v.dtype) for v in loads]
        + [pltpu.VMEM(shape, dtype) for shape, dtype in stores]
        + scratch
        + [pltpu.SemaphoreType.DMA((max(len(loads), 1), 4))]
        + [pltpu.SemaphoreType.DMA((max(len(stores), 1), 4))],
        compiler_params=pltpu.CompilerParams(**params),
        name=name,
    )(*[v for _, v in ins])


def nothing(p):
    pass


def at_planes(schedule):
    def hook(k):
        for step_at, work in enumerate(schedule):

            @pl.when(k == step_at)
            def _():
                for step in work:
                    step()

    return hook


class VectorSum:
    def __init__(self, refs):
        self.levels, self.came, self.from_z, self.send_sem, self.recv_sem = refs
        self.dp, self.mp, core, x, y, *across = neighbours()
        self.across = across

    @staticmethod
    def scratch(rows, columns, planes):
        return [
            pltpu.VMEM((4, rows, columns), F32),
            pltpu.VMEM((3, rows, columns), F32),
            pltpu.VMEM((planes, rows, columns), F32),
            pltpu.SemaphoreType.DMA((3 + planes,)),
            pltpu.SemaphoreType.DMA((3 + planes,)),
        ]

    def hop(self, level):
        return pltpu.make_async_remote_copy(
            src_ref=self.levels.at[level],
            dst_ref=self.came.at[level],
            send_sem=self.send_sem.at[level],
            recv_sem=self.recv_sem.at[level],
            device_id=(self.across[level], self.mp),
            device_id_type=MESH,
        )

    def along(self, plane, receiving=False):
        slot = plane if receiving else self.mp
        return pltpu.make_async_remote_copy(
            src_ref=self.levels.at[3],
            dst_ref=self.from_z.at[slot],
            send_sem=self.send_sem.at[3 + plane],
            recv_sem=self.recv_sem.at[3 + slot],
            device_id=(self.dp, plane),
            device_id_type=MESH,
        )

    def begin(self):
        self.hop(0).start()

    def others(self):
        planes = self.from_z.shape[0]
        return [(self.mp + step) % planes for step in range(1, planes)]

    def advance(self, level):
        self.hop(level).wait_recv()
        self.levels[level + 1] = self.levels[level] + self.came[level]
        if level < 2:
            self.hop(level + 1).start()
        else:
            for plane in self.others():
                self.along(plane).start()

    def finish(self, out):
        total = self.levels[3]
        for plane in self.others():
            self.along(plane, receiving=True).wait_recv()
            total = total + self.from_z[plane]
        out[...] = total
        for level in range(3):
            self.hop(level).wait_send()
        for plane in self.others():
            self.along(plane).wait_send()


def stack_rows(rows, columns):
    wide = [
        row
        if row.shape[1] == columns
        else jnp.concatenate([row, jnp.zeros((1, columns - row.shape[1]), F32)], -1)
        for row in rows
    ]
    spare = -len(wide) % 8
    if spare:
        wide.append(jnp.zeros((spare, columns), F32))
    return jnp.concatenate(wide, 0)


def folded(sums):
    return jnp.sum(sums[...], 0, keepdims=True)


def first_rows(sums):
    return [sums[p, 0:1] for p in range(sums.shape[0])]


EARLY_DEC = 8
EARLY_ROWS = 24


def early_rows(feed_sums, dec_sums, bridge_sums):
    f_gain, f_shift, down_bias, up_bias = feed_sums
    rows = [folded(f_gain), folded(f_shift), folded(down_bias)] + first_rows(up_bias)
    empty = [jnp.zeros_like(rows[0])]
    gain, shift, out_bias, head, f_gain, f_shift, down_bias, up_bias = dec_sums
    rows += empty + [folded(v) for v in (gain, shift, out_bias)] + first_rows(up_bias) + empty
    rows += [folded(v) for v in (f_gain, f_shift, down_bias)] + first_rows(head)
    return rows + [bridge_sums[0:1]]


def late_rows(gain, shift, out_bias, head):
    return [folded(gain), folded(shift), folded(out_bias)] + first_rows(head)


def named_call(name, body, ins, outs, scratch, collective_id=None):
    flat, counts = [], {}
    for key, item in scratch.items():
        items = item if isinstance(item, list) else [item]
        counts[key] = len(items)
        flat += items

    def inner(in_refs, out_refs, refs):
        buffers, at = {}, 0
        for key, count in counts.items():
            part = refs[at : at + count]
            buffers[key] = part if isinstance(scratch[key], list) else part[0]
            at += count
        body(dict(zip(ins, in_refs)), dict(zip(outs, out_refs)), buffers)

    results = staged_call(name, inner, list(ins.values()), list(outs.values()), flat, collective_id)
    return dict(zip(outs, results))


SUM_NAMES = ("gain", "shift", "out_bias", "head", "f_gain", "f_shift", "down_bias", "up_bias")


def run_backward(
    fast, top, saved, weights, gains, lengths, head_dim, carry=None, dec_sums=None
):
    (hidden, slope, feed_input, middle), (attended, triple, logsum, normed, stream) = saved
    attn, feed = weights
    planes, rows, hidden_width = hidden.shape
    width, wide = attn.shape[-1] // 4, feed_input.shape[1]
    encoder = len(top) == 3
    last = fast and encoder
    strip, narrow = top[0].shape
    deep = wide // 8 // planes
    tall = -(-deep // 32) * 32

    ins = {"lengths": ("near", lengths)}
    for key, value in zip(("rows", "input", "weight") if encoder else ("cotangent",), top):
        ins[key] = ("load" if encoder else "near", value)
    ins.update(feed_input=("load", feed_input))
    ins.update((key, ("planes", v)) for key, v in (("hidden", hidden), ("slope", slope)))
    ins.update(feed=("planes", feed), attn=("planes", attn))
    ins.update(middle=("planes", middle))
    ins.update(stream=("raw" if encoder else "planes", stream))
    ins.update(logsum=("planes", logsum))
    late_loads = {"triple": triple, "attended": attended, "normed": normed}
    ins.update((key, ("raw", value)) for key, value in late_loads.items())
    ins.update(attn_gain=("near", gains[0]), feed_gain=("near", gains[1]))

    sum_shapes = {key: (8, wide) for key in SUM_NAMES}
    sum_shapes.update(head=(planes, 8, 3 * width), up_bias=(planes, 8, hidden_width))
    if encoder:
        sum_shapes["bridge"] = (8, narrow)
    outs = {"input_grad": ("raw", (rows, wide), BF16)}
    scratch = {
        "grad_sem": pltpu.SemaphoreType.DMA((1,)),
        "stream_sem": pltpu.SemaphoreType.DMA((1,)),
        "upstream": pltpu.VMEM((rows, wide), F32 if encoder else BF16),
        "middle_grad": pltpu.VMEM((rows, wide), F32),
        "branch": pltpu.VMEM((rows, wide), BF16),
        "branch_turned": pltpu.VMEM((wide, rows), BF16),
        "turned": pltpu.VMEM((wide + 16, rows), BF16),
        "triple_grad": pltpu.VMEM((rows, 3 * width), BF16),
        "late_sem": pltpu.SemaphoreType.DMA((3, planes)),
        "flush_sem": pltpu.SemaphoreType.DMA((2, planes)),
    }
    if not encoder:
        scratch["total"] = pltpu.VMEM((rows, wide), F32)
    if last:
        scratch.update((key, pltpu.VMEM(shape, F32)) for key, shape in sum_shapes.items())
    else:
        outs.update((key, ("near", shape, F32)) for key, shape in sum_shapes.items())
    flushed = () if last else ("attn",) if fast else ("attn", "feed")
    for key, value in (("attn", attn), ("feed", feed)):
        if key in flushed:
            outs[key + "_part"] = ("raw", value.shape, BF16)
    names, kinds = (), ()
    every = range(planes)
    if fast:
        names, kinds = ("feed",), ((PAIR, feed.shape[5:], True, every),)
    if last:
        names, kinds = names + ("attn",), kinds + ((ONE, attn.shape[5:], True, every),)
    if last:
        names += ("carry", "bridge_grad")
        kinds += (
            (ONE, carry.shape[5:], False, every),
            (ONE, (tall // 2, narrow), True, every),
        )
        ins["carry"] = ("raw", carry)
        ins.update(("dec_" + key, ("near", dec_sums[key])) for key in SUM_NAMES)
        scratch["bridge_grad"] = pltpu.VMEM((planes, 2, 2, 2, 2, tall // 2, narrow), BF16)
        scratch["early"] = VectorSum.scratch(EARLY_ROWS, wide, planes)
        scratch["late"] = VectorSum.scratch(8, wide, planes)
        outs["early"] = ("near", (EARLY_ROWS, wide), F32)
        outs["late"] = ("near", (8, wide), F32)
    elif encoder:
        outs["bridge_grad"] = ("near", (wide, narrow), F32)
    if fast:
        scratch["reducer"] = Reducer.scratch(kinds, planes)
        outs.update(
            (key + "_sum", ("near", (2,) + kind[1], F32)) for key, kind in zip(names, kinds)
        )

    def body(ins, outs, buffers):
        mp = lax.axis_index("mp")
        order = (lambda k: order_of(planes - 1 - k, mp)) if fast else (lambda k: k)
        turns = [order(k) for k in range(planes)]
        for p in turns:
            for key in ("feed", "hidden", "slope"):
                ins[key].begin_plane(p)
        for key in ("middle", "logsum") if encoder else ("middle", "logsum", "stream"):
            ins[key].begin()
        for p in turns:
            ins["attn"].begin_plane(p)
        length = ins["lengths"][mp]
        sums = {key: (buffers if last else outs)[key] for key in sum_shapes}
        turned, middle_grad = buffers["turned"], buffers["middle_grad"]
        upstream = buffers["upstream"]
        feed, attn = ins["feed"].ref, ins["attn"].ref
        feed_todo, attn_todo = [[[] for _ in range(planes)] for _ in range(2)]
        after_feed, before_end, at_end = [], [], []
        if fast:
            reducer = Reducer(kinds, planes, turns, buffers["reducer"])
            where = {"feed": feed, "attn": attn}
            if last:
                where.update(carry=ins["carry"], bridge_grad=buffers["bridge_grad"])
            reducer.parts = [where[key] for key in names]
            at = {key: m for m, key in enumerate(names)}

            def todo(schedule, step, keys, ks):
                schedule += [partial(step, at[key], turns[k]) for k in ks for key in keys]

            core, plane, corner = reducer.core, reducer.plane, reducer.corner
            f, a, c, b = ("feed",), ("attn",), ("carry",), ("bridge_grad",)
            k0, k1, k2, k3 = feed_todo
            if last:
                todo(k0, core, c, every)
                todo(k0, core, b, every)
            if last:
                todo(k1, core, f, (0,))
                todo(k1, plane, c, every)
                todo(k2, core, f, (1,))
                todo(k2, plane, b, every)
                todo(k2, corner, c, every)
                todo(k3, core, f, (2,))
                todo(k3, plane, f, (0,))
                todo(k3, corner, b, every)
                todo(after_feed, core, f, (3,))
                todo(after_feed, plane, f, (1,))
                todo(after_feed, corner, f, (0,))
                k0, k1, k2, k3 = attn_todo
                todo(k0, plane, f, (2,))
                todo(k0, corner, f, (1,))
                todo(k1, core, a, (0,))
                todo(k1, plane, f, (3,))
                todo(k1, corner, f, (2,))
                todo(k2, core, a, (1,))
                todo(k2, plane, a, (0,))
                todo(k2, corner, f, (3,))
                todo(k3, core, a, (2,))
                todo(k3, plane, a, (1,))
                todo(k3, corner, a, (0,))
                todo(before_end, core, a, (3,))
                todo(before_end, plane, a, (2,))
                todo(before_end, corner, a, (1,))
                todo(at_end, plane, a, (3,))
                todo(at_end, corner, a, (2, 3))
            else:
                todo(k2, core, f, (0,))
                todo(k3, core, f, (1,))
                todo(after_feed, core, f, (2,))
                todo(after_feed, core, f, (3,))
                k0, k1, k2, k3 = attn_todo
                todo(k0, plane, f, (0, 1))
                todo(k1, plane, f, (2, 3))
                todo(k1, corner, f, (0,))
                todo(k2, corner, f, (1, 2, 3))
            entry_barrier((reducer.mp, reducer.across_core, reducer.across_x, reducer.across_y))
            if last:
                for p in turns:
                    reducer.begin(at["carry"], p)

        def run(steps):
            for step in steps:
                step()

        def flush(key, p):
            sem = buffers["flush_sem"].at[("attn", "feed").index(key), p]
            return pltpu.make_async_copy(ins[key].ref.at[p], outs[key + "_part"].at[p], sem)

        def hook_of(schedule, key):
            then = at_planes(schedule)

            def hook(k, p):
                if key in names:
                    reducer.begin(at[key], p)
                if key in flushed:
                    flush(key, p).start()
                then(k)

            return hook

        if encoder:
            put_transposed(ins["input"].use()[...], turned)
            both_grads = dot(turned[...], ins["rows"].use()[...])
            sums["bridge"][...] = both_grads[wide : wide + 8]
            if last:
                for g in range(8):
                    for p in range(planes):
                        low = (g * planes + p) * deep
                        part = both_grads[low : low + deep]
                        part = jnp.concatenate([part, jnp.zeros((tall - deep, narrow), F32)], 0)
                        part = part.astype(BF16).reshape(2, tall // 2, narrow)
                        buffers["bridge_grad"][p, g // 4, g // 2 % 2, g % 2] = part
                for p in turns:
                    reducer.begin(at["bridge_grad"], p)
            else:
                outs["bridge_grad"][...] = both_grads[:wide]
            upstream[...] = dot(ins["rows"].use()[...], ins["weight"].use()[...], NT)
            stream = Load(ins["stream"], ins["input"].ref, buffers["stream_sem"])
            stream.begin()
        else:
            stream = ins["stream"]
            upstream[rows - 32 :, :] = jnp.zeros((32, wide), BF16)
            upstream[:strip, :] = ins["cotangent"][...]

        def feed_ready(p):
            for key in ("feed", "hidden", "slope"):
                ins[key].ready(p)

        branches = [buffers[key] for key in ("branch", "branch_turned", "turned")]
        hidden, slope, feed_input = ins["hidden"].ref, ins["slope"].ref, ins["feed_input"].use()
        feed_backward(
            upstream,
            (hidden, slope, feed_input),
            feed,
            branches,
            (sums["down_bias"], sums["up_bias"]),
            middle_grad,
            order,
            feed_ready,
            hook_of(feed_todo, "feed"),
        )
        late = {}
        for k, (key, spot) in enumerate(
            (
                ("normed", feed_input),
                ("attended", slope.at[:, :, : attended.shape[2]]),
                ("triple", hidden.at[:, :, : triple.shape[2]]),
            )
        ):
            late[key] = Load(ins[key], spot, buffers["late_sem"].at[k])
            if key == "normed":
                late[key].begin()
        for p in turns:
            late["attended"].begin_plane(p)
            late["triple"].begin_plane(p)
        run(after_feed[:1])
        layer_backward(
            ins["middle"].use(),
            ins["feed_gain"],
            upstream,
            middle_grad,
            sums["f_gain"],
            sums["f_shift"],
        )
        run(after_feed[1:])
        if last:
            early, late_sum = VectorSum(buffers["early"]), VectorSum(buffers["late"])
            feed_sums = [sums[key] for key in ("f_gain", "f_shift", "down_bias", "up_bias")]
            dec_sums = [ins["dec_" + key] for key in SUM_NAMES]
            early.levels[0] = stack_rows(early_rows(feed_sums, dec_sums, sums["bridge"]), wide)
            early.begin()
            for level in range(3):
                attn_todo[level].append(partial(early.advance, level))
        ins["logsum"].use()
        total = upstream if encoder else buffers["total"]

        def attn_ready(p):
            ins["attn"].ready(p)
            late["attended"].ready(p)
            late["triple"].ready(p)

        attn_backward(
            head_dim,
            length,
            middle_grad,
            (late["attended"].ref, late["triple"].ref, ins["logsum"].ref, late["normed"].use()),
            attn,
            branches + [buffers["triple_grad"]],
            (sums["out_bias"], sums["head"]),
            total,
            order,
            attn_ready,
            hook_of(attn_todo, "attn"),
        )
        layer_backward(
            stream.use(),
            ins["attn_gain"],
            middle_grad,
            total,
            sums["gain"],
            sums["shift"],
        )
        if last:
            late_sum.levels[0] = stack_rows(
                late_rows(*(sums[key] for key in ("gain", "shift", "out_bias", "head"))), wide
            )
            late_sum.begin()
        run(before_end[:1])
        grad = Store(buffers["branch"], outs["input_grad"], buffers["grad_sem"])

        @row_blocks(rows)
        def _(i):
            grad.ref[block_at(i), :] = total[block_at(i), :].astype(BF16)

        grad.flush()
        if last:
            late_sum.advance(0)
            run(before_end[1:2])
            late_sum.advance(1)
            run(before_end[2:])
            run(at_end[:1])
            late_sum.advance(2)
            run(at_end[1:])
            early.finish(outs["early"])
            reducer.finish(at["carry"], outs["carry_sum"])
            for key in ("bridge_grad", "feed"):
                reducer.finish(at[key], outs[key + "_sum"])
            late_sum.finish(outs["late"])
            reducer.finish(at["attn"], outs["attn_sum"])
        elif fast:
            run(at_end)
            for key in names:
                reducer.finish(at[key], outs[key + "_sum"])
        grad.finish()
        if fast:
            reducer.drain()
        for key in flushed:
            for k in every:
                flush(key, turns[k]).wait()

    name = "backward_encoder" if encoder else "backward_decoder"
    barrier = (2 if encoder else 1) if fast else None
    return named_call(name, body, ins, outs, scratch, barrier)


def pack_attention(proj, out, turned=False):
    if turned:
        return jnp.concatenate([proj[0], proj[1], proj[2], out], 0).T
    return jnp.concatenate([proj[0], proj[1], proj[2], out.T], -1)


def bias_rows(head_bias, up_bias):
    return [
        jnp.concatenate(
            [head_bias[0:1], jnp.zeros((1, head_bias.shape[1]), F32), head_bias[1:2]], -1
        ),
        up_bias.reshape(1, -1),
    ]


def run_forward(patches, lengths, enc, dec, vectors, bridge, fast):
    enc_vectors, dec_vectors = vectors
    bridge_weight, bridge_bias = bridge
    planes = lengths.shape[0]
    strip, wide = patches.shape
    narrow = bridge_weight.shape[1]
    rows = -(-strip // 32) * 32
    attns, heads, feeds = [], [], []
    for block in (enc, dec):
        _, _, proj, head_bias, out, _, _, _, up, up_bias, down, _ = block
        attns.append((proj, out))
        heads.append((head_bias, up_bias))
        feeds.append((up, down))
    small_shape = (8, feeds[0][0].shape[1])
    packed = [(proj.shape[1], 4 * proj.shape[2]) for proj, _ in attns]
    mat_shapes = []
    for (tall, columns), (up, _) in zip(packed, feeds):
        mat_shapes += [(2, 2, 2, 2, tall // 16, columns), (2, 2, 2, 2, up.shape[0] // 8, up.shape[1])]
    layouts = [ONE, PAIR] * 2
    count = len(mat_shapes)
    small_whole = wholes = None
    if not fast:
        spread = lambda m: lax.all_gather(m, "mp", axis=0)
        wholes = []
        for attn, (up, down) in zip(attns, feeds):
            wholes += [as_one(spread(pack_attention(*attn))), as_pair(spread(up), spread(down))]
        small = stack_rows([r for pair in heads for r in bias_rows(*pair)], small_shape[1])
        small_whole = spread(small)

    def block_outs(columns, width, hidden, head_dim):
        return [
            ("store", (rows, columns), BF16),
            ("store", (planes, rows, whole_lanes(3 * width)), BF16),
            ("store", (planes, rows, whole_lanes(width)), BF16),
            ("store", (planes, width // head_dim, rows), F32),
            ("store", (rows, columns), F32),
            ("store", (rows, columns), BF16),
            ("store", (planes, rows, hidden), BF16),
            ("store", (planes, rows, hidden), BF16),
        ]

    outs = block_outs(wide, packed[0][1] // 4, mat_shapes[1][-1], HEAD)
    outs += block_outs(narrow, packed[1][1] // 4, mat_shapes[3][-1], DHEAD)
    outs += [
        ("store", (rows, wide), BF16),
        ("store", (rows, wide), BF16),
        ("store", (rows, narrow), F32),
        ("near", (strip, narrow), BF16),
    ]
    ins = [("near", lengths), ("near", patches)]
    ins += [("near", v) for v in enc_vectors + dec_vectors + (bridge_bias,)]
    ins += [("load", bridge_weight)]
    first = len(ins)
    scratch = [pltpu.VMEM((rows, wide), F32), pltpu.VMEM((rows, narrow), F32)]
    if fast:
        turned = [stands(*proj.shape[1:]) for proj, _ in attns]
        for (proj, out), turn in zip(attns, turned):
            ins += [("near", jnp.swapaxes(proj, 1, 2) if turn else proj), ("near", out)]
        ins += [("near", v) for pair in heads for v in pair]
        cut = lambda v: v.reshape(2, 2, 2, v.shape[0] // 8, v.shape[1])
        ins += [("raw", cut(v)) for pair in feeds for v in pair]
        outs += [("raw", (planes,) + shape, BF16) for shape in mat_shapes]
        scratch += [pltpu.VMEM((planes,) + shape, BF16) for shape in mat_shapes]
        scratch += [pltpu.VMEM((planes,) + small_shape, F32)]
        scratch += [pltpu.SemaphoreType.DMA((4,))]
        scratch += Gatherer.sems(count, planes)
    else:
        ins += [("load", w) for w in wholes] + [("near", small_whole)]

    def body(ins, outs, scratch):
        mp = lax.axis_index("mp")
        lengths, patches = ins[:2]
        enc, dec, bridge_bias = ins[2:8], ins[8:14], ins[14]
        enc_outs, dec_outs = outs[:8], outs[8:16]
        stream, bridge_input, bridged, decoded = outs[16:20]
        totals = scratch[:2]
        length = lengths[mp]
        if fast:
            weights, smalls = scratch[2 : 2 + count], scratch[2 + count]
            attn_refs, head_refs = ins[first : first + 4], ins[first + 4 : first + 8]
            gatherer = Gatherer(planes, layouts, weights, outs[20:], smalls, scratch[4 + count :])
            own_copies = []
            for k, ref in enumerate(ins[first + 8 : first + 12]):
                target = weights[1 + k // 2 * 2].at[mp, k % 2]
                own_copies.append(pltpu.make_async_copy(ref, target, scratch[3 + count].at[k]))
                own_copies[-1].start()
            entry_barrier(
                (mp, gatherer.across_core, gatherer.across_x, gatherer.across_y)
            )
            for m, k in ((0, 0), (2, 2)):
                own = pack_attention(attn_refs[k][...], attn_refs[k + 1][...], turned[k // 2])
                weights[m][mp] = own.reshape(weights[m].shape[1:])
                if m == 0:
                    gatherer.along_z(0)
                    head_values = [ref[...] for ref in head_refs]
                    small_rows = bias_rows(*head_values[:2]) + bias_rows(*head_values[2:])
                    smalls[mp] = stack_rows(small_rows, small_shape[1])
                    gatherer.begin_small()
            for copy in own_copies:
                copy.wait()
            for m in range(count):
                gatherer.flush(m, mp).start()
            gatherer.along_z(1)
            units = [(m, i) for m in range(count) for i in range(3)]
            lag = AG_LAG
            stages = (
                (0, gatherer.to_plane),
                (lag, gatherer.to_corner),
                (2 * lag, gatherer.to_core),
                (3 * lag, gatherer.whole),
            )

            def ticks(start, stop):
                for tick in range(start, stop):
                    for late, stage in stages:
                        if 0 <= tick - late < len(units):
                            stage(*units[tick - late])
                    if tick % 3 == 0 and 2 + tick // 3 < count:
                        gatherer.along_z(2 + tick // 3)

            def before_steps(cuts):
                def before(k):
                    for step in range(planes):

                        @pl.when(k == step)
                        def _():
                            ticks(cuts[step], cuts[step + 1])

                return before

            depth = 3 * lag + 1
            befores = []
            for m in range(count):
                done = depth + 3 * m
                first_cut = 0 if m == 0 else done - 1
                befores.append(before_steps((first_cut, first_cut, done, done + 1, done + 2)))
            order = lambda k: order_of(k, mp)
        else:
            weights, smalls = [w.use() for w in ins[first : first + count]], ins[first + count]
            order = lambda k: k
            befores = (nothing,) * 4

        tail = slice(rows - 32, rows)
        stream.ref[tail, :] = jnp.zeros((32, wide), BF16)
        stream.ref[:strip, :] = patches[...]
        stream.flush()
        if fast:
            gatherer.have_small()

        def bias(row, columns):
            return lambda p: smalls[p, row : row + 1, :columns]

        def block(source, vectors, weights, row, outs, head_dim, total, befores):
            gain, shift, out_bias, feed_gain, feed_shift, down_bias = vectors
            attn, feed = weights
            refs = [out.ref for out in outs]
            attn_forward(
                head_dim,
                length,
                source,
                attn,
                (gain, shift, out_bias),
                bias(row, attn.shape[-1] // 4 * 3),
                refs[:5],
                order,
                befores[0],
            )
            for out in outs[:5]:
                out.flush()
            feed_forward(
                refs[4],
                feed,
                (feed_gain, feed_shift, down_bias),
                bias(row + 1, refs[6].shape[2]),
                refs[5:8],
                total,
                order,
                befores[1],
            )
            for out in outs[5:8]:
                out.flush()

        block(stream.ref, enc, weights[:2], 0, enc_outs, HEAD, totals[0], befores[:2])
        bridge_input.ref[...] = totals[0][...].astype(BF16)
        bridge_input.flush()
        bridged.ref[...] = dot(bridge_input.ref[...], ins[first - 1].use()[...]) + as_row(bridge_bias)
        bridged.flush()
        block(bridged.ref, dec, weights[2:], 2, dec_outs, DHEAD, totals[1], befores[2:])
        decoded[...] = totals[1][:strip, :].astype(BF16)
        if fast:
            gatherer.drain()

    results = staged_call("forward", body, ins, outs, scratch, 0 if fast else None)

    def stored(outs, source):
        normed, triple, attended, logsum, middle, feed_input, hidden, slope = outs
        return (
            (hidden, slope, feed_input, middle),
            (attended, triple, logsum, normed, source),
        )

    stream, bridge_input, bridged, decoded, *gathered = results[16:]
    return (
        stored(results[:8], stream),
        stored(results[8:16], bridged),
        bridge_input,
        decoded,
        gathered if fast else wholes,
    )


def stands(tall, flat):
    return tall % 128 == 0 and flat % 128 != 0


def run_outputs(rows, early, late, enc_sums, dec_sums, bridge_sum, sizes, bridge_shape):
    planes, groups = sizes["mp"], sizes["dp"]
    decoded, patches_grad = rows
    strip = decoded.shape[0]
    wide, narrow = bridge_shape
    deep = wide // groups // planes

    def block_shapes(columns, mats):
        width, hidden = mats[0].shape[1] // 4, mats[1].shape[2]
        each, piece = columns // groups // planes, columns // groups
        return [
            (each,),
            (each,),
            (3, piece, width),
            (2, width // groups),
            (piece, width) if stands(width, piece) else (width, piece),
            (each,),
            (each,),
            (each,),
            (piece, hidden),
            (hidden // groups,),
            (piece, hidden) if stands(hidden, piece) else (hidden, piece),
            (each,),
        ]

    shapes = block_shapes(wide, enc_sums) + [(deep, narrow), (narrow // groups // planes,)]
    shapes += block_shapes(narrow, dec_sums)
    ins = [decoded, patches_grad, early, late, *enc_sums, *dec_sums, bridge_sum]

    def kernel(*refs):
        decoded, patches_grad, early, late = refs[:4]
        enc, dec, bridge_sum = refs[4:6], refs[6:8], refs[8]
        decoded_out, patches_out, *outs = refs[9:]
        decoded_out[...] = decoded[...]
        patches_out[...] = patches_grad[:strip, :]
        dp, mp = lax.axis_index("dp"), lax.axis_index("mp")
        lanes = early.shape[1]

        def cut(values, low, size):
            values = pltpu.roll(values, lax.rem(lanes - low, lanes), 1)
            return values[:, :size]

        def put_rows(values, targets):
            for k, target in enumerate(targets):
                target[...] = values[k]

        def block(mats, outs, columns, first, row, second, up_row, head_row):
            attn, (up, down) = mats[0], (mats[1].at[0], mats[1].at[1])
            width, hidden = attn.shape[1] // 4, up.shape[1]
            gain, shift, proj, head, out, out_bias, f_gain, f_shift, up_out, up_bias, down_out, d_bias = outs
            for j in range(3):
                proj[j] = attn[:, j * width : (j + 1) * width]
            out_grad = attn[:, 3 * width :]
            out[...] = out_grad if out.shape == out_grad.shape else out_grad.T
            up_out[...] = up[...]
            down_out[...] = down[...] if down_out.shape == down.shape else down[...].T
            each = columns // groups // planes
            low = (dp * planes + mp) * each
            put_rows(cut(first[row : row + 8, :], low, each), (gain, shift, out_bias))
            lane, ref = second
            put_rows(cut(ref[lane : lane + 8, :], low, each), (f_gain, f_shift, d_bias))
            line = up_row[0][pl.ds(up_row[1] + mp, 1), :]
            put_rows(cut(line, dp * (hidden // groups), hidden // groups), (up_bias,))
            line = head_row[0][pl.ds(head_row[1] + mp, 1), :]
            piece = width // groups
            head[0:1, :] = cut(line, dp * piece, piece)
            head[1:2, :] = cut(line, 2 * width + dp * piece, piece)

        at = EARLY_DEC
        block(enc, outs[:12], wide, late, 0, (0, early), (early, 3), (late, 3))
        block(dec, outs[14:], narrow, early, at, (at + 8, early), (early, at + 3), (early, at + 11))
        outs[12][...] = bridge_sum[:deep, :]
        each = narrow // groups // planes
        line = cut(early[at + 15 : at + 16, :], (dp * planes + mp) * each, each)
        put_rows(line, (outs[13],))

    results = pl.pallas_call(
        kernel,
        out_shape=[
            jax.ShapeDtypeStruct(decoded.shape, BF16),
            jax.ShapeDtypeStruct((strip, wide), BF16),
        ]
        + [jax.ShapeDtypeStruct(shape, F32) for shape in shapes],
        in_specs=[IN_VMEM] * len(ins),
        out_specs=[IN_VMEM] * (2 + len(shapes)),
        compiler_params=pltpu.CompilerParams(vmem_limit_bytes=VMEM_BYTES),
        name="outputs",
    )(*ins)
    first, second = list(results[2:14]), list(results[16:28])
    for block, mats in ((first, enc_sums), (second, dec_sums)):
        for at, (tall, flat) in ((4, (mats[0].shape[1] // 4, mats[0].shape[0])), (10, mats[1].shape[:0:-1])):
            block[at] = block[at] if block[at].shape == (tall, flat) else block[at].T
    return (*results[:2], *first, *results[14:16], *second)


def shards(sizes, *inputs):
    patches, lengths = inputs[:2]
    cotangent = inputs[28]
    planes, groups = sizes["mp"], sizes["dp"]
    fast = groups == 8 and planes == 4
    strip, wide = patches.shape
    enc, (bridge_weight, bridge_bias), dec = inputs[2:14], inputs[14:16], inputs[16:28]

    def vectors_of(block):
        gain, shift, _, _, _, out_bias, f_gain, f_shift, _, _, _, d_bias = block
        return (gain, shift, out_bias, f_gain, f_shift, d_bias)

    enc_vectors, dec_vectors = vectors_of(enc), vectors_of(dec)
    enc_stored, dec_stored, bridge_input, decoded, wholes = run_forward(
        patches, lengths, enc, dec, (enc_vectors, dec_vectors), (bridge_weight, bridge_bias), fast
    )
    dec_gains, enc_gains = (dec[0], dec[6]), (enc[0], enc[6])
    down = run_backward(
        fast, (cotangent,), dec_stored, wholes[2:], dec_gains, lengths, DHEAD
    )
    dec_sums = {key: down[key] for key in SUM_NAMES}
    bridge = (down["input_grad"], bridge_input, bridge_weight)
    on = run_backward(
        fast,
        bridge,
        enc_stored,
        wholes[:2],
        enc_gains,
        lengths,
        HEAD,
        down["attn_part"] if fast else None,
        dec_sums,
    )
    if fast:
        rows_of = lambda v: v.reshape(-1, v.shape[-1])
        enc_grads = (rows_of(on["attn_sum"]), on["feed_sum"])
        dec_grads = (rows_of(on["carry_sum"]), down["feed_sum"])
        early, late, bridge_sum = on["early"], on["late"], rows_of(on["bridge_grad_sum"])
    else:
        feed_sums = [on[key] for key in ("f_gain", "f_shift", "down_bias", "up_bias")]
        rows = early_rows(feed_sums, [dec_sums[key] for key in SUM_NAMES], on["bridge"])
        early = stack_rows(rows, wide)
        late = stack_rows(late_rows(*(on[key] for key in SUM_NAMES[:4])), wide)
        early, late = lax.psum(early, ("dp", "mp")), lax.psum(late, ("dp", "mp"))

        def in_groups(grad):
            return collect(grad.reshape(planes, groups, -1, grad.shape[-1]), sizes)

        def block_grads(result):
            attn, feed = result["attn_part"], result["feed_part"]
            return in_groups(attn), jnp.stack([in_groups(feed[:, 0]), in_groups(feed[:, 1])])

        dec_grads, enc_grads = block_grads(down), block_grads(on)
        deep = wide // planes // groups
        bridge_part = on["bridge_grad"].reshape(groups, planes, deep, -1).transpose(1, 0, 2, 3)
        bridge_sum = collect(bridge_part, sizes)
    patches_grad = on["input_grad"]
    return run_outputs(
        (decoded, patches_grad),
        early,
        late,
        enc_grads,
        dec_grads,
        bridge_sum,
        sizes,
        bridge_weight.shape,
    )


def solution(mesh):
    block_in = (
        P(),
        P(),
        P(None, None, "mp"),
        P(None, "mp"),
        P("mp", None),
        P(),
        P(),
        P(),
        P(None, "mp"),
        P("mp"),
        P("mp", None),
        P(),
    )
    both = P(("dp", "mp"))
    block_out = (
        both,
        both,
        P(None, "dp", "mp"),
        P(None, ("mp", "dp")),
        P("mp", "dp"),
        both,
        both,
        both,
        P("dp", "mp"),
        P(("mp", "dp")),
        P("mp", "dp"),
        both,
    )
    rows = P(("dp", "mp"), None)
    return jax.shard_map(
        partial(shards, dict(mesh.shape)),
        mesh=mesh,
        in_specs=(rows, P("dp")) + block_in + (P(), P()) + block_in + (rows,),
        out_specs=(rows, rows) + block_out + (rows, both) + block_out,
        check_vma=False,
    )
```

```python
from functools import partial

import jax
import jax.numpy as jnp
from jax import lax
from jax.experimental import pallas as pl
from jax.experimental.pallas import tpu as pltpu
from jax.sharding import PartitionSpec as P

HEAD = 64
DHEAD = 32
EPSILON = 1e-06
MESH = pl.DeviceIdType.MESH
F32 = jnp.float32
BF16 = jnp.bfloat16
VMEM_BYTES = 60 * 1024 * 1024


def neighbours():
    dp, mp = lax.axis_index("dp"), lax.axis_index("mp")
    core, x, y = dp % 2, (dp // 2) % 2, dp // 4
    across_core = dp + 1 - 2 * core
    across_x = dp + 2 - 4 * x
    across_y = dp + 4 - 8 * y
    return dp, mp, core, x, y, across_core, across_x, across_y


def entry_barrier(parts):
    mp, across_core, across_x, across_y = parts
    dp = lax.axis_index("dp")
    barrier = pltpu.get_barrier_semaphore()
    planes = lax.axis_size("mp")
    for other in (across_core, across_x, across_y):
        pl.semaphore_signal(barrier, inc=1, device_id=(other, mp), device_id_type=MESH)
    for step in range(1, planes):
        pl.semaphore_signal(
            barrier, inc=1, device_id=(dp, (mp + step) % planes), device_id_type=MESH
        )
    pl.semaphore_wait(barrier, 3 + planes - 1)


def plane_order(mp, planes):
    if planes != 4:
        return [(mp + step) % planes for step in range(1, planes)]
    upper = mp // 2
    place = mp + upper * (3 - 2 * mp)
    return [o + upper * (3 - 2 * o) for o in (place + 1, 2 - 2 * place, 3)]


def order_of(k, mp):
    upper = mp // 2
    place = mp + upper * (3 - 2 * mp)
    plane = (k + place) % 3 * (1 - k // 3) + 3 * (k // 3)
    return plane + upper * (3 - 2 * plane)


class Layout:
    def __init__(self, pair):
        self.pair = pair

    def block(self, ref, p, y, x, core):
        return ref.at[p, :, y, x, core] if self.pair else ref.at[p, y, x, core]

    def half(self, ref, p, y, x, core, h):
        return ref.at[p, h, y, x, core] if self.pair else ref.at[p, y, x, core, h]

    def matrices(self, ref, p):
        if self.pair:
            return ref[p, 0].reshape(-1, ref.shape[-1]), ref[p, 1].reshape(-1, ref.shape[-1])
        return (ref[p].reshape(-1, ref.shape[-1]),)

    def in_core(self, ref, p, y, x):
        return ref.at[p, :, y, x] if self.pair else ref.at[p, y, x]


PAIR, ONE = Layout(True), Layout(False)
ALL = slice(None)


def as_pair(first, second):
    both = jnp.stack([first, second], 1)
    planes, _, rows, columns = both.shape
    return both.reshape(planes, 2, 2, 2, 2, rows // 8, columns)


def as_one(array):
    planes, rows, columns = array.shape
    return array.reshape(planes, 2, 2, 2, 2, rows // 16, columns)


class Gatherer:
    A, X, Y, DY, DX, S = range(6)
    kinds = 6

    def __init__(self, planes, layouts, wholes, targets, smalls, sems):
        self.planes, self.count, self.layouts = planes, len(wholes), layouts
        self.wholes, self.targets, self.smalls = wholes, targets, smalls
        self.flush_sem, self.send_sem, self.recv_sem = sems
        self.dp, self.mp, self.core, self.x, self.y, *across = neighbours()
        self.across_core, self.across_x, self.across_y = across
        self.others = plane_order(self.mp, planes)

    @staticmethod
    def sems(count, planes):
        return [
            pltpu.SemaphoreType.DMA((count, planes)),
            pltpu.SemaphoreType.DMA((count + 1, planes, Gatherer.kinds)),
            pltpu.SemaphoreType.DMA((count + 1, planes, Gatherer.kinds)),
        ]

    def remote(self, m, kind, src, dst, send_plane, recv_plane, target):
        return pltpu.make_async_remote_copy(
            src_ref=src,
            dst_ref=dst,
            send_sem=self.send_sem.at[m, send_plane, kind],
            recv_sem=self.recv_sem.at[m, recv_plane, kind],
            device_id=target,
            device_id_type=MESH,
        )

    def piece(self, m, plane, y, x, core, half=None):
        layout, ref = self.layouts[m], self.wholes[m]
        if half is None:
            return layout.block(ref, plane, y, x, core)
        return layout.half(ref, plane, y, x, core, half)

    def send(self, m, i, kind):
        plane = self.others[i]
        x, y, core = self.x, self.y, self.core
        if kind == self.A:
            below = (self.mp - plane + self.planes - 1) // self.planes
            part = self.piece(m, plane, y, x, core)
            target = (self.dp, self.clamped(self.mp - 1 + 2 * below))
            return self.remote(m, kind, part, part, plane, plane, target)
        part, target = {
            self.X: (self.piece(m, plane, y, x, core), self.across_x),
            self.Y: (self.piece(m, plane, y, x, core), self.across_y),
            self.DY: (self.piece(m, plane, y, 1 - x, core, 0), self.across_y),
            self.DX: (self.piece(m, plane, 1 - y, x, core, 1), self.across_x),
            self.S: (self.piece(m, plane, ALL, ALL, core), self.across_core),
        }[kind]
        return self.remote(m, kind, part, part, plane, plane, (target, self.mp))

    def arrived(self, m, i, kind):
        plane = self.others[i]
        x, y, core = self.x, self.y, self.core
        part = {
            self.A: self.piece(m, plane, y, x, core),
            self.X: self.piece(m, plane, y, 1 - x, core),
            self.Y: self.piece(m, plane, 1 - y, x, core),
            self.DY: self.piece(m, plane, 1 - y, 1 - x, core, 0),
            self.DX: self.piece(m, plane, 1 - y, 1 - x, core, 1),
            self.S: self.piece(m, plane, ALL, ALL, 1 - core),
        }[kind]
        self.remote(m, kind, part, part, plane, plane, (self.across_core, self.mp)).wait_recv()

    def clamped(self, plane):
        return jnp.clip(plane, 0, self.planes - 1)

    def goes_on(self, i):
        below = (self.mp - self.others[i] + self.planes - 1) // self.planes
        target = self.mp - 1 + 2 * below
        return (target >= 0) & (target < self.planes)

    def outward(self, m, up):
        part = self.piece(m, self.mp, self.y, self.x, self.core)
        copy = pltpu.make_async_remote_copy(
            src_ref=part,
            dst_ref=part,
            send_sem=self.send_sem.at[m, self.mp, self.X if up else self.Y],
            recv_sem=self.recv_sem.at[m, self.mp, self.A],
            device_id=(self.dp, self.clamped(self.mp + (1 if up else -1))),
            device_id_type=MESH,
        )
        return copy, self.mp < self.planes - 1 if up else self.mp > 0

    def along_z(self, m):
        for up in (True, False):
            copy, there = self.outward(m, up)
            pl.when(there)(copy.start)

    def to_plane(self, m, i):
        self.arrived(m, i, self.A)
        pl.when(self.goes_on(i))(self.send(m, i, self.A).start)
        self.send(m, i, self.X).start()
        self.send(m, i, self.Y).start()

    def to_corner(self, m, i):
        self.arrived(m, i, self.X)
        self.send(m, i, self.DY).start()
        self.arrived(m, i, self.Y)
        self.send(m, i, self.DX).start()

    def to_core(self, m, i):
        self.arrived(m, i, self.DY)
        self.arrived(m, i, self.DX)
        self.send(m, i, self.S).start()

    def flush(self, m, plane):
        return pltpu.make_async_copy(
            self.wholes[m].at[plane], self.targets[m].at[plane], self.flush_sem.at[m, plane]
        )

    def whole(self, m, i):
        self.arrived(m, i, self.S)
        self.flush(m, self.others[i]).start()

    def send_small(self, i):
        plane = self.others[i]
        part = self.smalls.at[self.mp]
        return self.remote(self.count, self.A, part, part, plane, self.mp, (self.dp, plane))

    def begin_small(self):
        for i in range(self.planes - 1):
            self.send_small(i).start()

    def have_small(self):
        for plane in self.others:
            part = self.smalls.at[plane]
            target = (self.across_core, self.mp)
            self.remote(self.count, self.A, part, part, plane, plane, target).wait_recv()

    def drain(self):
        for m in range(self.count):
            for up in (True, False):
                copy, there = self.outward(m, up)
                pl.when(there)(copy.wait_send)
            for i in range(self.planes - 1):
                for kind in range(1, self.kinds):
                    self.send(m, i, kind).wait_send()
                pl.when(self.goes_on(i))(self.send(m, i, self.A).wait_send)
            for p in range(self.planes):
                self.flush(m, p).wait()
        for i in range(self.planes - 1):
            self.send_small(i).wait_send()


class Reducer:
    def __init__(self, kinds, planes, turns, refs):
        self.planes, self.count, self.kinds, self.turns = planes, len(kinds), kinds, turns
        refs = list(refs)
        take = lambda: [refs.pop(0) for _ in range(self.count)]
        self.mine, self.from_core, self.from_x, self.from_y = take(), take(), take(), take()
        self.then_y, self.then_x, self.from_z = take(), take(), take()
        self.local_sem, self.send_sem, self.recv_sem = refs
        self.dp, self.mp, self.core_id, self.x, self.y, *across = neighbours()
        self.across_core, self.across_x, self.across_y = across
        self.parts = [None] * self.count

    @staticmethod
    def scratch(kinds, planes):
        count = len(kinds)

        def buffers(*lead, skip=False):
            return [
                pltpu.VMEM((1, 16, 128) if skip and resident else (planes,) + lead + half, BF16)
                for _, half, resident, _ in kinds
            ]

        return (
            buffers(2, 2, 2, skip=True)
            + buffers(2, 2, 2)
            + buffers(2)
            + buffers(2)
            + buffers()
            + buffers()
            + buffers(2)
            + [
                pltpu.SemaphoreType.DMA((count, planes)),
                pltpu.SemaphoreType.DMA((count, planes, 6)),
                pltpu.SemaphoreType.DMA((count, planes, 6)),
            ]
        )

    def remote(self, m, p, kind, src, dst, target, recv_plane=None):
        return pltpu.make_async_remote_copy(
            src_ref=src,
            dst_ref=dst,
            send_sem=self.send_sem.at[m, p, kind],
            recv_sem=self.recv_sem.at[m, p if recv_plane is None else recv_plane, kind],
            device_id=target,
            device_id_type=MESH,
        )

    def piece(self, m, p, y, x, half=None):
        layout, _, resident, _ = self.kinds[m]
        if not resident:
            ref = layout.in_core(self.mine[m], p, y, x)
            if half is None:
                return ref
            return self.mine[m].at[p, half, y, x] if layout.pair else self.mine[m].at[p, y, x, half]
        if half is None:
            return layout.block(self.parts[m], p, y, x, self.core_id)
        return layout.half(self.parts[m], p, y, x, self.core_id, half)

    def fetch(self, m, p):
        src = self.kinds[m][0].block(self.parts[m], p, ALL, ALL, self.core_id)
        return pltpu.make_async_copy(src, self.mine[m].at[p], self.local_sem.at[m, p])

    def begin(self, m, p):
        if not self.kinds[m][2]:
            self.fetch(m, p).start()
        self.to_core(m, p).start()

    def to_core(self, m, p):
        src = self.kinds[m][0].block(self.parts[m], p, ALL, ALL, 1 - self.core_id)
        return self.remote(m, p, 0, src, self.from_core[m].at[p], (self.across_core, self.mp))

    def to_x(self, m, p):
        src = self.piece(m, p, ALL, 1 - self.x, 0)
        return self.remote(m, p, 1, src, self.from_x[m].at[p], (self.across_x, self.mp))

    def to_y(self, m, p):
        src = self.piece(m, p, 1 - self.y, ALL, 1)
        return self.remote(m, p, 2, src, self.from_y[m].at[p], (self.across_y, self.mp))

    def x_to_y(self, m, p):
        src = self.piece(m, p, 1 - self.y, self.x, 0)
        return self.remote(m, p, 3, src, self.then_y[m].at[p], (self.across_y, self.mp))

    def y_to_x(self, m, p):
        src = self.piece(m, p, self.y, 1 - self.x, 1)
        return self.remote(m, p, 4, src, self.then_x[m].at[p], (self.across_x, self.mp))

    def to_z(self, m, p):
        src = self.piece(m, p, self.y, self.x)
        return self.remote(m, p, 5, src, self.from_z[m].at[self.mp], (self.dp, p), self.mp)

    def core(self, m, p):
        layout = self.kinds[m][0]
        if not self.kinds[m][2]:
            self.fetch(m, p).wait()
        self.to_core(m, p).wait_recv()

        def add(y, x):
            ref = self.piece(m, p, y, x)
            ref[...] = ref[...] + layout.in_core(self.from_core[m], p, y, x)[...]

        for y in range(2):
            add(y, 1 - self.x)
        self.to_x(m, p).start()
        add(1 - self.y, self.x)
        self.to_y(m, p).start()
        add(self.y, self.x)

    def plane(self, m, p):
        self.to_x(m, p).wait_recv()
        for y in (1 - self.y, self.y):
            ref = self.piece(m, p, y, self.x, 0)
            ref[...] = ref[...] + self.from_x[m][p, y]
        self.x_to_y(m, p).start()
        self.to_y(m, p).wait_recv()
        for x in (1 - self.x, self.x):
            ref = self.piece(m, p, self.y, x, 1)
            ref[...] = ref[...] + self.from_y[m][p, x]
        self.y_to_x(m, p).start()

    def corner(self, m, p):
        self.x_to_y(m, p).wait_recv()
        self.y_to_x(m, p).wait_recv()
        for half, came in enumerate((self.then_y, self.then_x)):
            ref = self.piece(m, p, self.y, self.x, half)
            ref[...] = ref[...] + came[m][p]

        if p is not self.turns[-1]:
            self.to_z(m, p).start()

    def finish(self, m, out, partial_sum=None):
        ks = self.kinds[m][3]
        total = 0.0 if partial_sum is None else partial_sum[...]
        if self.planes - 1 in ks:
            total = total + self.piece(m, self.mp, self.y, self.x)[...].astype(F32)
        if 0 in ks:
            for step in range(1, self.planes):
                plane = (self.mp + step) % self.planes
                src = self.from_z[m].at[plane]
                self.remote(m, plane, 5, src, src, (self.dp, plane)).wait_recv()
                total = total + src[...].astype(F32)
        out[...] = total

    def drain(self):
        for m in range(self.count):
            for k in self.kinds[m][3]:
                p = self.turns[k]
                for copy in (self.to_core, self.to_x, self.to_y, self.x_to_y, self.y_to_x):
                    copy(m, p).wait_send()
                if k < self.planes - 1:
                    self.to_z(m, p).wait_send()


def collect(part, sizes):
    part = lax.psum_scatter(part, "mp", scatter_dimension=0, tiled=False)
    return lax.psum_scatter(part.astype(F32), "dp", scatter_dimension=0, tiled=False)


LOG2E = 1.4426950408889634
AG_LAG = 1
ROW_BLOCK = 32
NT = (((1,), (1,)), ((), ()))


def dot(left, right, dims=(((1,), (0,)), ((), ()))):
    return lax.dot_general(left, right, dims, preferred_element_type=F32)


def standardize(x):
    centered = x - jnp.mean(x, -1, keepdims=True)
    scale = lax.rsqrt(jnp.mean(centered * centered, -1, keepdims=True) + EPSILON)
    return centered * scale, scale


def gelu_and_slope(b):
    cdf = 0.5 * (1.0 + lax.erf(b * 0.7071067811865476))
    density = jnp.exp(-0.5 * b * b) * 0.3989422804014327
    return b * cdf, cdf + b * density


def fold_rows(x):
    return jnp.sum(x.reshape(x.shape[0] // 8, 8, x.shape[1]), 0)


def row_blocks(rows):
    return pl.loop(0, rows // ROW_BLOCK, unroll=rows // ROW_BLOCK)


def block_at(i):
    return pl.ds(pl.multiple_of(i * ROW_BLOCK, ROW_BLOCK), ROW_BLOCK)


def whole_lanes(columns):
    return -(-columns // 128) * 128


def strip_forward(head_dim, width, length, p, triple, attended, logsum):
    rows = triple.shape[1]
    visible = lax.broadcasted_iota(jnp.int32, (rows, 1), 0) < length
    factor = head_dim**-0.5 * LOG2E
    outs = []
    for head in range(width // head_dim):
        low = head * head_dim
        query = triple[p, :, low : low + head_dim]
        key = triple[p, :, width + low : width + low + head_dim]
        value = triple[p, :, 2 * width + low : 2 * width + low + head_dim]
        scores = jnp.where(visible, dot(key, query, NT) * factor, -1e30)
        ceiling = jnp.max(scores, 0, keepdims=True)
        exponent = jnp.exp2(scores - ceiling)
        denominator = jnp.sum(exponent, 0, keepdims=True)
        outs.append(dot(value.T, exponent.astype(BF16)) * (1.0 / denominator))
        logsum[p, head : head + 1, :] = ceiling + jnp.log2(denominator)
    attended[p, :, :width] = jnp.concatenate(outs, 0).T.astype(BF16)


def strip_backward(head_dim, width, length, p, triple, attended, mixed, logsum, out):
    rows = triple.shape[1]
    visible = lax.broadcasted_iota(jnp.int32, (rows, 1), 0) < length
    factor = head_dim**-0.5
    products = (mixed.astype(F32) * attended[p, :, :width].astype(F32)).T
    query_grads = []
    for head in range(width // head_dim):
        low = head * head_dim
        query = triple[p, :, low : low + head_dim]
        key = triple[p, :, width + low : width + low + head_dim]
        value = triple[p, :, 2 * width + low : 2 * width + low + head_dim]
        mixed_head = mixed[:, low : low + head_dim]
        row_sums = jnp.sum(products[low : low + head_dim], 0, keepdims=True)
        scores = dot(key, query, NT) * (factor * LOG2E) - logsum[p, head : head + 1, :]
        chances = jnp.exp2(jnp.where(visible, scores, -1e30))
        chance_grad = dot(value, mixed_head, NT)
        score_grad = (chances * (chance_grad - row_sums)).astype(BF16)
        key_grad = dot(score_grad, query) * factor
        value_grad = dot(chances.astype(BF16), mixed_head)
        query_grads.append(dot(key.T, score_grad) * factor)
        out[:, width + low : width + low + head_dim] = key_grad.astype(BF16)
        out[:, 2 * width + low : 2 * width + low + head_dim] = value_grad.astype(BF16)
    out[:, :width] = jnp.concatenate(query_grads, 0).T.astype(BF16)


def attn_forward(head_dim, length, stream, weight, vectors, bias_of, outs, order, before):
    gain, shift, out_bias = [as_row(v) for v in vectors]
    normed, triple, attended, logsum, middle = outs
    planes, rows = triple.shape[:2]
    width = weight.shape[-1] // 4

    @row_blocks(rows)
    def _(i):
        x = stream[block_at(i), :].astype(F32)
        normed[block_at(i), :] = (standardize(x)[0] * gain + shift).astype(BF16)
        middle[block_at(i), :] = x + out_bias

    @pl.loop(0, planes)
    def _(k):
        before(k)
        p = order(k)
        (own,) = ONE.matrices(weight, p)
        projected = dot(normed[...], own[:, : 3 * width]) + bias_of(p)
        triple[p, :, : 3 * width] = projected.astype(BF16)
        strip_forward(head_dim, width, length, p, triple, attended, logsum)
        middle[...] += dot(attended[p, :, :width], own[:, 3 * width :], NT)


def feed_forward(middle, weights, vectors, bias_of, outs, total, order, before):
    gain, shift, down_bias = [as_row(v) for v in vectors]
    feed_input, hidden, slope = outs
    planes, rows, width = hidden.shape

    @row_blocks(rows)
    def _(i):
        x = middle[block_at(i), :]
        feed_input[block_at(i), :] = (standardize(x)[0] * gain + shift).astype(BF16)
        total[block_at(i), :] = x + down_bias

    @pl.loop(0, planes)
    def _(k):
        before(k)
        p = order(k)
        bias = bias_of(p)
        up, down = PAIR.matrices(weights, p)
        for low in range(0, width, 256):
            part = slice(low, low + 256)
            activated, rise = gelu_and_slope(dot(feed_input[...], up[:, part]) + bias[:, part])
            hidden[p, :, part] = activated.astype(BF16)
            slope[p, :, part] = rise.astype(BF16)
        total[...] += dot(hidden[p], down)


def as_row(vector):
    return vector[...].reshape(1, -1)


def layer_backward(stream, gain, upstream, spare, gain_sums, shift_sums):
    gain_sums[...] = jnp.zeros_like(gain_sums)
    shift_sums[...] = jnp.zeros_like(shift_sums)
    gain = as_row(gain)

    @row_blocks(stream.shape[0])
    def _(i):
        hat, scale = standardize(stream[block_at(i), :].astype(F32))
        grad = spare[block_at(i), :]
        gain_sums[...] += fold_rows(grad * hat)
        shift_sums[...] += fold_rows(grad)
        grad = grad * gain
        part = grad - jnp.mean(grad, -1, keepdims=True)
        part = part - hat * jnp.mean(grad * hat, -1, keepdims=True)
        spare[block_at(i), :] = upstream[block_at(i), :].astype(F32) + part * scale


def put_transposed(values, turned):
    columns = values.shape[1]
    turned[:columns, :] = values.T
    turned[columns:, :] = jnp.ones((16, values.shape[0]), BF16)


def start_branch(upstream, branch, turned, sums, total):
    rows, wide = branch.shape
    sums[...] = jnp.zeros_like(sums)

    @row_blocks(rows)
    def _(i):
        rounded = upstream[block_at(i), :].astype(BF16)
        branch[block_at(i), :] = rounded
        sums[...] += fold_rows(rounded.astype(F32))
        total[block_at(i), :] = jnp.zeros((ROW_BLOCK, wide), F32)

    turned[...] = branch[...].T


def feed_backward(upstream, saved, weights, scratch, sums, total, order, ready, hook):
    hidden, slope, feed_input = saved
    branch, branch_turned, feed_turned = scratch
    branch_sums, up_sums = sums
    planes = hidden.shape[0]
    wide = branch.shape[1]
    start_branch(upstream, branch, branch_turned, branch_sums, total)
    put_transposed(feed_input[...], feed_turned)

    @pl.loop(0, planes)
    def _(k):
        p = order(k)
        ready(p)
        up, down = PAIR.matrices(weights, p)
        hidden_grad = dot(branch[...], down, NT)
        before_grad = (hidden_grad * slope[p].astype(F32)).astype(BF16)
        total[...] += dot(before_grad, up, NT)
        spot = weights.shape[2:]
        weights[p, 1] = dot(branch_turned[...], hidden[p]).astype(BF16).reshape(spot)
        both = dot(feed_turned[...], before_grad)
        weights[p, 0] = both[:wide].astype(BF16).reshape(spot)
        up_sums[p] = both[wide : wide + 8]
        hook(k, p)


def attn_backward(
    head_dim, length, upstream, saved, weight, scratch, sums, total, order, ready, hook
):
    attended, triple, logsum, normed = saved
    branch, branch_turned, normed_turned, triple_grad = scratch
    branch_sums, head_sums = sums
    planes, width = attended.shape[0], weight.shape[-1] // 4
    wide = branch.shape[1]
    start_branch(upstream, branch, branch_turned, branch_sums, total)
    put_transposed(normed[...], normed_turned)

    @pl.loop(0, planes)
    def _(k):
        p = order(k)
        ready(p)
        (own,) = ONE.matrices(weight, p)
        out_weight = weight[p, :, :, :, :, :, 3 * width :].reshape(wide, width)
        mixed = dot(branch[...], out_weight).astype(BF16)
        strip_backward(head_dim, width, length, p, triple, attended, mixed, logsum, triple_grad)
        total[...] += dot(triple_grad[...], own[:, : 3 * width], NT)
        both = dot(normed_turned[...], triple_grad[...])
        out_grad = dot(branch_turned[...], attended[p, :, :width])
        grad = jnp.concatenate([both[:wide].astype(BF16), out_grad.astype(BF16)], -1)
        weight[p] = grad.reshape(weight.shape[1:])
        head_sums[p] = both[wide : wide + 8]
        hook(k, p)


IN_VMEM = pl.BlockSpec(memory_space=pltpu.VMEM)
IN_SMEM = pl.BlockSpec(memory_space=pltpu.SMEM)


class Load:
    def __init__(self, source, ref, sems):
        self.source, self.ref, self.sems, self.waits = source, ref, sems, False

    def copy(self, p=None):
        if p is None:
            return pltpu.make_async_copy(self.source, self.ref, self.sems.at[0])
        return pltpu.make_async_copy(self.source.at[p], self.ref.at[p], self.sems.at[p])

    def begin(self):
        self.copy().start()
        self.waits = True

    def begin_plane(self, p):
        self.copy(p).start()

    def use(self):
        if self.waits:
            self.copy().wait()
            self.waits = False
        return self.ref

    def ready(self, p):
        self.copy(p).wait()


class Store:
    def __init__(self, ref, target, sems):
        self.ref, self.target, self.sems, self.by_plane = ref, target, sems, False

    def flush(self, p=None):
        if p is None:
            pltpu.make_async_copy(self.ref, self.target, self.sems.at[0]).start()
        else:
            self.by_plane = True
            pltpu.make_async_copy(self.ref.at[p], self.target.at[p], self.sems.at[p]).start()

    def finish(self):
        if not self.by_plane:
            pltpu.make_async_copy(self.ref, self.target, self.sems.at[0]).wait()
            return
        for p in range(self.ref.shape[0]):
            pltpu.make_async_copy(self.ref.at[p], self.target.at[p], self.sems.at[p]).wait()


def staged_call(name, body, ins, outs, scratch=(), collective_id=None):
    any_spec = pl.BlockSpec(memory_space=pl.ANY)
    near = lambda v: IN_SMEM if v.dtype == jnp.int32 else IN_VMEM
    loads = [v for mode, v in ins if mode in ("load", "planes")]
    stores = [(shape, dtype) for mode, shape, dtype in outs if mode == "store"]
    scratch = list(scratch)

    def kernel(*refs):
        refs = list(refs)
        take = lambda n: [refs.pop(0) for _ in range(n)]
        in_refs, out_refs = take(len(ins)), take(len(outs))
        load_refs, store_refs, rest = take(len(loads)), take(len(stores)), take(len(scratch))
        load_sem, store_sem = refs
        given, load_at = [], 0
        for (mode, _), ref in zip(ins, in_refs):
            if mode in ("load", "planes"):
                given.append(Load(ref, load_refs[load_at], load_sem.at[load_at]))
                load_at += 1
                if mode == "load":
                    given[-1].begin()
            else:
                given.append(ref)
        results, store_at = [], 0
        for (mode, _, _), ref in zip(outs, out_refs):
            if mode == "store":
                results.append(Store(store_refs[store_at], ref, store_sem.at[store_at]))
                store_at += 1
            else:
                results.append(ref)
        body(given, results, rest)
        for item in given:
            if isinstance(item, Load):
                item.use()
        for item in results:
            if isinstance(item, Store):
                item.finish()

    params = {"vmem_limit_bytes": VMEM_BYTES}
    if collective_id is not None:
        params.update(collective_id=collective_id, has_side_effects=True)
    return pl.pallas_call(
        kernel,
        out_shape=[jax.ShapeDtypeStruct(shape, dtype) for _, shape, dtype in outs],
        in_specs=[near(v) if mode == "near" else any_spec for mode, v in ins],
        out_specs=[IN_VMEM if mode == "near" else any_spec for mode, _, _ in outs],
        scratch_shapes=[pltpu.VMEM(v.shape, v.dtype) for v in loads]
        + [pltpu.VMEM(shape, dtype) for shape, dtype in stores]
        + scratch
        + [pltpu.SemaphoreType.DMA((max(len(loads), 1), 4))]
        + [pltpu.SemaphoreType.DMA((max(len(stores), 1), 4))],
        compiler_params=pltpu.CompilerParams(**params),
        name=name,
    )(*[v for _, v in ins])


def nothing(p):
    pass


def at_planes(schedule):
    def hook(k):
        for step_at, work in enumerate(schedule):

            @pl.when(k == step_at)
            def _():
                for step in work:
                    step()

    return hook


class VectorSum:
    def __init__(self, refs):
        self.levels, self.came, self.from_z, self.send_sem, self.recv_sem = refs
        self.dp, self.mp, core, x, y, *across = neighbours()
        self.across = across

    @staticmethod
    def scratch(rows, columns, planes):
        return [
            pltpu.VMEM((4, rows, columns), F32),
            pltpu.VMEM((3, rows, columns), F32),
            pltpu.VMEM((planes, rows, columns), F32),
            pltpu.SemaphoreType.DMA((3 + planes,)),
            pltpu.SemaphoreType.DMA((3 + planes,)),
        ]

    def hop(self, level):
        return pltpu.make_async_remote_copy(
            src_ref=self.levels.at[level],
            dst_ref=self.came.at[level],
            send_sem=self.send_sem.at[level],
            recv_sem=self.recv_sem.at[level],
            device_id=(self.across[level], self.mp),
            device_id_type=MESH,
        )

    def along(self, plane, receiving=False):
        slot = plane if receiving else self.mp
        return pltpu.make_async_remote_copy(
            src_ref=self.levels.at[3],
            dst_ref=self.from_z.at[slot],
            send_sem=self.send_sem.at[3 + plane],
            recv_sem=self.recv_sem.at[3 + slot],
            device_id=(self.dp, plane),
            device_id_type=MESH,
        )

    def begin(self):
        self.hop(0).start()

    def others(self):
        planes = self.from_z.shape[0]
        return [(self.mp + step) % planes for step in range(1, planes)]

    def advance(self, level):
        self.hop(level).wait_recv()
        self.levels[level + 1] = self.levels[level] + self.came[level]
        if level < 2:
            self.hop(level + 1).start()
        else:
            for plane in self.others():
                self.along(plane).start()

    def finish(self, out):
        total = self.levels[3]
        for plane in self.others():
            self.along(plane, receiving=True).wait_recv()
            total = total + self.from_z[plane]
        out[...] = total
        for level in range(3):
            self.hop(level).wait_send()
        for plane in self.others():
            self.along(plane).wait_send()


def stack_rows(rows, columns):
    wide = [
        row
        if row.shape[1] == columns
        else jnp.concatenate([row, jnp.zeros((1, columns - row.shape[1]), F32)], -1)
        for row in rows
    ]
    spare = -len(wide) % 8
    if spare:
        wide.append(jnp.zeros((spare, columns), F32))
    return jnp.concatenate(wide, 0)


def folded(sums):
    return jnp.sum(sums[...], 0, keepdims=True)


def first_rows(sums):
    return [sums[p, 0:1] for p in range(sums.shape[0])]


EARLY_DEC = 8
EARLY_ROWS = 24


def early_rows(feed_sums, dec_sums, bridge_sums):
    f_gain, f_shift, down_bias, up_bias = feed_sums
    rows = [folded(f_gain), folded(f_shift), folded(down_bias)] + first_rows(up_bias)
    empty = [jnp.zeros_like(rows[0])]
    gain, shift, out_bias, head, f_gain, f_shift, down_bias, up_bias = dec_sums
    rows += empty + [folded(v) for v in (gain, shift, out_bias)] + first_rows(up_bias) + empty
    rows += [folded(v) for v in (f_gain, f_shift, down_bias)] + first_rows(head)
    return rows + [bridge_sums[0:1]]


def late_rows(gain, shift, out_bias, head):
    return [folded(gain), folded(shift), folded(out_bias)] + first_rows(head)


def named_call(name, body, ins, outs, scratch, collective_id=None):
    flat, counts = [], {}
    for key, item in scratch.items():
        items = item if isinstance(item, list) else [item]
        counts[key] = len(items)
        flat += items

    def inner(in_refs, out_refs, refs):
        buffers, at = {}, 0
        for key, count in counts.items():
            part = refs[at : at + count]
            buffers[key] = part if isinstance(scratch[key], list) else part[0]
            at += count
        body(dict(zip(ins, in_refs)), dict(zip(outs, out_refs)), buffers)

    results = staged_call(name, inner, list(ins.values()), list(outs.values()), flat, collective_id)
    return dict(zip(outs, results))


SUM_NAMES = ("gain", "shift", "out_bias", "head", "f_gain", "f_shift", "down_bias", "up_bias")


def run_backward(
    fast, top, saved, weights, gains, lengths, head_dim, carry=None, dec_sums=None
):
    (hidden, slope, feed_input, middle), (attended, triple, logsum, normed, stream) = saved
    attn, feed = weights
    planes, rows, hidden_width = hidden.shape
    width, wide = attn.shape[-1] // 4, feed_input.shape[1]
    encoder = len(top) == 3
    last = fast and encoder
    strip, narrow = top[0].shape
    deep = wide // 8 // planes
    tall = -(-deep // 32) * 32

    ins = {"lengths": ("near", lengths)}
    for key, value in zip(("rows", "input", "weight") if encoder else ("cotangent",), top):
        ins[key] = ("load" if encoder else "near", value)
    ins.update(feed_input=("load", feed_input))
    ins.update((key, ("planes", v)) for key, v in (("hidden", hidden), ("slope", slope)))
    ins.update(feed=("planes", feed), attn=("planes", attn))
    ins.update(middle=("planes", middle))
    ins.update(stream=("raw" if encoder else "planes", stream))
    ins.update(logsum=("planes", logsum))
    late_loads = {"triple": triple, "attended": attended, "normed": normed}
    ins.update((key, ("raw", value)) for key, value in late_loads.items())
    ins.update(attn_gain=("near", gains[0]), feed_gain=("near", gains[1]))

    sum_shapes = {key: (8, wide) for key in SUM_NAMES}
    sum_shapes.update(head=(planes, 8, 3 * width), up_bias=(planes, 8, hidden_width))
    if encoder:
        sum_shapes["bridge"] = (8, narrow)
    outs = {"input_grad": ("raw", (rows, wide), BF16)}
    scratch = {
        "grad_sem": pltpu.SemaphoreType.DMA((1,)),
        "stream_sem": pltpu.SemaphoreType.DMA((1,)),
        "upstream": pltpu.VMEM((rows, wide), F32 if encoder else BF16),
        "middle_grad": pltpu.VMEM((rows, wide), F32),
        "branch": pltpu.VMEM((rows, wide), BF16),
        "branch_turned": pltpu.VMEM((wide, rows), BF16),
        "turned": pltpu.VMEM((wide + 16, rows), BF16),
        "triple_grad": pltpu.VMEM((rows, 3 * width), BF16),
        "late_sem": pltpu.SemaphoreType.DMA((3, planes)),
        "flush_sem": pltpu.SemaphoreType.DMA((2, planes)),
    }
    if not encoder:
        scratch["total"] = pltpu.VMEM((rows, wide), F32)
    if last:
        scratch.update((key, pltpu.VMEM(shape, F32)) for key, shape in sum_shapes.items())
    else:
        outs.update((key, ("near", shape, F32)) for key, shape in sum_shapes.items())
    flushed = () if last else ("attn",) if fast else ("attn", "feed")
    for key, value in (("attn", attn), ("feed", feed)):
        if key in flushed:
            outs[key + "_part"] = ("raw", value.shape, BF16)
    names, kinds = (), ()
    every = range(planes)
    if fast:
        names, kinds = ("feed",), ((PAIR, feed.shape[5:], True, every),)
    if last:
        names, kinds = names + ("attn",), kinds + ((ONE, attn.shape[5:], True, every),)
    if last:
        names += ("carry", "bridge_grad")
        kinds += (
            (ONE, carry.shape[5:], False, every),
            (ONE, (tall // 2, narrow), True, every),
        )
        ins["carry"] = ("raw", carry)
        ins.update(("dec_" + key, ("near", dec_sums[key])) for key in SUM_NAMES)
        scratch["bridge_grad"] = pltpu.VMEM((planes, 2, 2, 2, 2, tall // 2, narrow), BF16)
        scratch["early"] = VectorSum.scratch(EARLY_ROWS, wide, planes)
        scratch["late"] = VectorSum.scratch(8, wide, planes)
        outs["early"] = ("near", (EARLY_ROWS, wide), F32)
        outs["late"] = ("near", (8, wide), F32)
    elif encoder:
        outs["bridge_grad"] = ("near", (wide, narrow), F32)
    if fast:
        scratch["reducer"] = Reducer.scratch(kinds, planes)
        outs.update(
            (key + "_sum", ("near", (2,) + kind[1], F32)) for key, kind in zip(names, kinds)
        )

    def body(ins, outs, buffers):
        mp = lax.axis_index("mp")
        order = (lambda k: order_of(planes - 1 - k, mp)) if fast else (lambda k: k)
        turns = [order(k) for k in range(planes)]
        for p in turns:
            for key in ("feed", "hidden", "slope"):
                ins[key].begin_plane(p)
        for key in ("middle", "logsum") if encoder else ("middle", "logsum", "stream"):
            ins[key].begin()
        for p in turns:
            ins["attn"].begin_plane(p)
        length = ins["lengths"][mp]
        sums = {key: (buffers if last else outs)[key] for key in sum_shapes}
        turned, middle_grad = buffers["turned"], buffers["middle_grad"]
        upstream = buffers["upstream"]
        feed, attn = ins["feed"].ref, ins["attn"].ref
        feed_todo, attn_todo = [[[] for _ in range(planes)] for _ in range(2)]
        after_feed, before_end, at_end = [], [], []
        if fast:
            reducer = Reducer(kinds, planes, turns, buffers["reducer"])
            where = {"feed": feed, "attn": attn}
            if last:
                where.update(carry=ins["carry"], bridge_grad=buffers["bridge_grad"])
            reducer.parts = [where[key] for key in names]
            at = {key: m for m, key in enumerate(names)}

            def todo(schedule, step, keys, ks):
                schedule += [partial(step, at[key], turns[k]) for k in ks for key in keys]

            core, plane, corner = reducer.core, reducer.plane, reducer.corner
            f, a, c, b = ("feed",), ("attn",), ("carry",), ("bridge_grad",)
            k0, k1, k2, k3 = feed_todo
            if last:
                todo(k0, core, c, every)
                todo(k0, core, b, every)
            if last:
                todo(k1, core, f, (0,))
                todo(k1, plane, c, every)
                todo(k2, core, f, (1,))
                todo(k2, plane, b, every)
                todo(k2, corner, c, every)
                todo(k3, core, f, (2,))
                todo(k3, plane, f, (0,))
                todo(k3, corner, b, every)
                todo(after_feed, core, f, (3,))
                k0, k1, k2, k3 = attn_todo
                todo(k0, plane, f, (1,))
                todo(k0, corner, f, (0,))
                todo(k1, core, a, (0,))
                todo(k1, plane, f, (2,))
                todo(k1, corner, f, (1,))
                todo(k2, core, a, (1,))
                todo(k2, plane, f, (3,))
                todo(k2, corner, f, (2,))
                todo(k3, core, a, (2,))
                todo(k3, plane, a, (0,))
                todo(k3, corner, f, (3,))
                todo(before_end, core, a, (3,))
                todo(before_end, plane, a, (1,))
                todo(before_end, corner, a, (0,))
                todo(before_end, plane, a, (2,))
                todo(before_end, corner, a, (1,))
                todo(at_end, plane, a, (3,))
                todo(at_end, corner, a, (2, 3))
            else:
                todo(k2, core, f, (0,))
                todo(k3, core, f, (1,))
                todo(after_feed, core, f, (2,))
                todo(after_feed, core, f, (3,))
                k0, k1, k2, k3 = attn_todo
                todo(k0, plane, f, (0, 1))
                todo(k1, plane, f, (2, 3))
                todo(k1, corner, f, (0,))
                todo(k2, corner, f, (1, 2, 3))
            entry_barrier((reducer.mp, reducer.across_core, reducer.across_x, reducer.across_y))
            if last:
                for p in turns:
                    reducer.begin(at["carry"], p)

        def run(steps):
            for step in steps:
                step()

        def flush(key, p):
            sem = buffers["flush_sem"].at[("attn", "feed").index(key), p]
            return pltpu.make_async_copy(ins[key].ref.at[p], outs[key + "_part"].at[p], sem)

        def hook_of(schedule, key):
            then = at_planes(schedule)

            def hook(k, p):
                if key in names:
                    reducer.begin(at[key], p)
                if key in flushed:
                    flush(key, p).start()
                then(k)

            return hook

        if encoder:
            put_transposed(ins["input"].use()[...], turned)
            both_grads = dot(turned[...], ins["rows"].use()[...])
            sums["bridge"][...] = both_grads[wide : wide + 8]
            if last:
                for g in range(8):
                    for p in range(planes):
                        low = (g * planes + p) * deep
                        part = both_grads[low : low + deep]
                        part = jnp.concatenate([part, jnp.zeros((tall - deep, narrow), F32)], 0)
                        part = part.astype(BF16).reshape(2, tall // 2, narrow)
                        buffers["bridge_grad"][p, g // 4, g // 2 % 2, g % 2] = part
                for p in turns:
                    reducer.begin(at["bridge_grad"], p)
            else:
                outs["bridge_grad"][...] = both_grads[:wide]
            upstream[...] = dot(ins["rows"].use()[...], ins["weight"].use()[...], NT)
            stream = Load(ins["stream"], ins["input"].ref, buffers["stream_sem"])
            stream.begin()
        else:
            stream = ins["stream"]
            upstream[rows - 32 :, :] = jnp.zeros((32, wide), BF16)
            upstream[:strip, :] = ins["cotangent"][...]

        def feed_ready(p):
            for key in ("feed", "hidden", "slope"):
                ins[key].ready(p)

        branches = [buffers[key] for key in ("branch", "branch_turned", "turned")]
        hidden, slope, feed_input = ins["hidden"].ref, ins["slope"].ref, ins["feed_input"].use()
        feed_backward(
            upstream,
            (hidden, slope, feed_input),
            feed,
            branches,
            (sums["down_bias"], sums["up_bias"]),
            middle_grad,
            order,
            feed_ready,
            hook_of(feed_todo, "feed"),
        )
        late = {}
        for k, (key, spot) in enumerate(
            (
                ("normed", feed_input),
                ("attended", slope.at[:, :, : attended.shape[2]]),
                ("triple", hidden.at[:, :, : triple.shape[2]]),
            )
        ):
            late[key] = Load(ins[key], spot, buffers["late_sem"].at[k])
            if key == "normed":
                late[key].begin()
        for p in turns:
            late["attended"].begin_plane(p)
            late["triple"].begin_plane(p)
        run(after_feed[:1])
        layer_backward(
            ins["middle"].use(),
            ins["feed_gain"],
            upstream,
            middle_grad,
            sums["f_gain"],
            sums["f_shift"],
        )
        run(after_feed[1:])
        if last:
            early, late_sum = VectorSum(buffers["early"]), VectorSum(buffers["late"])
            feed_sums = [sums[key] for key in ("f_gain", "f_shift", "down_bias", "up_bias")]
            dec_sums = [ins["dec_" + key] for key in SUM_NAMES]
            early.levels[0] = stack_rows(early_rows(feed_sums, dec_sums, sums["bridge"]), wide)
            early.begin()
            for level in range(3):
                attn_todo[level].append(partial(early.advance, level))
        ins["logsum"].use()
        total = upstream if encoder else buffers["total"]

        def attn_ready(p):
            ins["attn"].ready(p)
            late["attended"].ready(p)
            late["triple"].ready(p)

        attn_backward(
            head_dim,
            length,
            middle_grad,
            (late["attended"].ref, late["triple"].ref, ins["logsum"].ref, late["normed"].use()),
            attn,
            branches + [buffers["triple_grad"]],
            (sums["out_bias"], sums["head"]),
            total,
            order,
            attn_ready,
            hook_of(attn_todo, "attn"),
        )
        layer_backward(
            stream.use(),
            ins["attn_gain"],
            middle_grad,
            total,
            sums["gain"],
            sums["shift"],
        )
        if last:
            late_sum.levels[0] = stack_rows(
                late_rows(*(sums[key] for key in ("gain", "shift", "out_bias", "head"))), wide
            )
            late_sum.begin()
        run(before_end[:1])
        grad = Store(buffers["branch"], outs["input_grad"], buffers["grad_sem"])

        @row_blocks(rows)
        def _(i):
            grad.ref[block_at(i), :] = total[block_at(i), :].astype(BF16)

        grad.flush()
        if last:
            late_sum.advance(0)
            run(before_end[1:2])
            late_sum.advance(1)
            run(before_end[2:])
            run(at_end[:1])
            late_sum.advance(2)
            run(at_end[1:])
            early.finish(outs["early"])
            reducer.finish(at["carry"], outs["carry_sum"])
            for key in ("bridge_grad", "feed"):
                reducer.finish(at[key], outs[key + "_sum"])
            late_sum.finish(outs["late"])
            reducer.finish(at["attn"], outs["attn_sum"])
        elif fast:
            run(at_end)
            for key in names:
                reducer.finish(at[key], outs[key + "_sum"])
        grad.finish()
        if fast:
            reducer.drain()
        for key in flushed:
            for k in every:
                flush(key, turns[k]).wait()

    name = "backward_encoder" if encoder else "backward_decoder"
    barrier = (2 if encoder else 1) if fast else None
    return named_call(name, body, ins, outs, scratch, barrier)


def pack_attention(proj, out, turned=False):
    if turned:
        return jnp.concatenate([proj[0], proj[1], proj[2], out], 0).T
    return jnp.concatenate([proj[0], proj[1], proj[2], out.T], -1)


def bias_rows(head_bias, up_bias):
    return [
        jnp.concatenate(
            [head_bias[0:1], jnp.zeros((1, head_bias.shape[1]), F32), head_bias[1:2]], -1
        ),
        up_bias.reshape(1, -1),
    ]


def run_forward(patches, lengths, enc, dec, vectors, bridge, fast):
    enc_vectors, dec_vectors = vectors
    bridge_weight, bridge_bias = bridge
    planes = lengths.shape[0]
    strip, wide = patches.shape
    narrow = bridge_weight.shape[1]
    rows = -(-strip // 32) * 32
    attns, heads, feeds = [], [], []
    for block in (enc, dec):
        _, _, proj, head_bias, out, _, _, _, up, up_bias, down, _ = block
        attns.append((proj, out))
        heads.append((head_bias, up_bias))
        feeds.append((up, down))
    small_shape = (8, feeds[0][0].shape[1])
    packed = [(proj.shape[1], 4 * proj.shape[2]) for proj, _ in attns]
    mat_shapes = []
    for (tall, columns), (up, _) in zip(packed, feeds):
        mat_shapes += [(2, 2, 2, 2, tall // 16, columns), (2, 2, 2, 2, up.shape[0] // 8, up.shape[1])]
    layouts = [ONE, PAIR] * 2
    count = len(mat_shapes)
    small_whole = wholes = None
    if not fast:
        spread = lambda m: lax.all_gather(m, "mp", axis=0)
        wholes = []
        for attn, (up, down) in zip(attns, feeds):
            wholes += [as_one(spread(pack_attention(*attn))), as_pair(spread(up), spread(down))]
        small = stack_rows([r for pair in heads for r in bias_rows(*pair)], small_shape[1])
        small_whole = spread(small)

    def block_outs(columns, width, hidden, head_dim):
        return [
            ("store", (rows, columns), BF16),
            ("store", (planes, rows, whole_lanes(3 * width)), BF16),
            ("store", (planes, rows, whole_lanes(width)), BF16),
            ("store", (planes, width // head_dim, rows), F32),
            ("store", (rows, columns), F32),
            ("store", (rows, columns), BF16),
            ("store", (planes, rows, hidden), BF16),
            ("store", (planes, rows, hidden), BF16),
        ]

    outs = block_outs(wide, packed[0][1] // 4, mat_shapes[1][-1], HEAD)
    outs += block_outs(narrow, packed[1][1] // 4, mat_shapes[3][-1], DHEAD)
    outs += [
        ("store", (rows, wide), BF16),
        ("store", (rows, wide), BF16),
        ("store", (rows, narrow), F32),
        ("near", (strip, narrow), BF16),
    ]
    ins = [("near", lengths), ("near", patches)]
    ins += [("near", v) for v in enc_vectors + dec_vectors + (bridge_bias,)]
    ins += [("load", bridge_weight)]
    first = len(ins)
    scratch = [pltpu.VMEM((rows, wide), F32), pltpu.VMEM((rows, narrow), F32)]
    if fast:
        turned = [stands(*proj.shape[1:]) for proj, _ in attns]
        for (proj, out), turn in zip(attns, turned):
            ins += [("near", jnp.swapaxes(proj, 1, 2) if turn else proj), ("near", out)]
        ins += [("near", v) for pair in heads for v in pair]
        cut = lambda v: v.reshape(2, 2, 2, v.shape[0] // 8, v.shape[1])
        ins += [("raw", cut(v)) for pair in feeds for v in pair]
        outs += [("raw", (planes,) + shape, BF16) for shape in mat_shapes]
        scratch += [pltpu.VMEM((planes,) + shape, BF16) for shape in mat_shapes]
        scratch += [pltpu.VMEM((planes,) + small_shape, F32)]
        scratch += [pltpu.SemaphoreType.DMA((4,))]
        scratch += Gatherer.sems(count, planes)
    else:
        ins += [("load", w) for w in wholes] + [("near", small_whole)]

    def body(ins, outs, scratch):
        mp = lax.axis_index("mp")
        lengths, patches = ins[:2]
        enc, dec, bridge_bias = ins[2:8], ins[8:14], ins[14]
        enc_outs, dec_outs = outs[:8], outs[8:16]
        stream, bridge_input, bridged, decoded = outs[16:20]
        totals = scratch[:2]
        length = lengths[mp]
        if fast:
            weights, smalls = scratch[2 : 2 + count], scratch[2 + count]
            attn_refs, head_refs = ins[first : first + 4], ins[first + 4 : first + 8]
            gatherer = Gatherer(planes, layouts, weights, outs[20:], smalls, scratch[4 + count :])
            own_copies = []
            for k, ref in enumerate(ins[first + 8 : first + 12]):
                target = weights[1 + k // 2 * 2].at[mp, k % 2]
                own_copies.append(pltpu.make_async_copy(ref, target, scratch[3 + count].at[k]))
                own_copies[-1].start()
            entry_barrier(
                (mp, gatherer.across_core, gatherer.across_x, gatherer.across_y)
            )
            for m, k in ((0, 0), (2, 2)):
                own = pack_attention(attn_refs[k][...], attn_refs[k + 1][...], turned[k // 2])
                weights[m][mp] = own.reshape(weights[m].shape[1:])
                if m == 0:
                    gatherer.along_z(0)
                    head_values = [ref[...] for ref in head_refs]
                    small_rows = bias_rows(*head_values[:2]) + bias_rows(*head_values[2:])
                    smalls[mp] = stack_rows(small_rows, small_shape[1])
                    gatherer.begin_small()
            for copy in own_copies:
                copy.wait()
            for m in range(count):
                gatherer.flush(m, mp).start()
            gatherer.along_z(1)
            units = [(m, i) for m in range(count) for i in range(3)]
            lag = AG_LAG
            stages = (
                (0, gatherer.to_plane),
                (lag, gatherer.to_corner),
                (2 * lag, gatherer.to_core),
                (3 * lag, gatherer.whole),
            )

            def ticks(start, stop):
                for tick in range(start, stop):
                    for late, stage in stages:
                        if 0 <= tick - late < len(units):
                            stage(*units[tick - late])
                    if tick % 3 == 0 and 2 + tick // 3 < count:
                        gatherer.along_z(2 + tick // 3)

            def before_steps(cuts):
                def before(k):
                    for step in range(planes):

                        @pl.when(k == step)
                        def _():
                            ticks(cuts[step], cuts[step + 1])

                return before

            depth = 3 * lag + 1
            befores = []
            for m in range(count):
                done = depth + 3 * m
                first_cut = 0 if m == 0 else done - 1
                befores.append(before_steps((first_cut, first_cut, done, done + 1, done + 2)))
            order = lambda k: order_of(k, mp)
        else:
            weights, smalls = [w.use() for w in ins[first : first + count]], ins[first + count]
            order = lambda k: k
            befores = (nothing,) * 4

        tail = slice(rows - 32, rows)
        stream.ref[tail, :] = jnp.zeros((32, wide), BF16)
        stream.ref[:strip, :] = patches[...]
        stream.flush()
        if fast:
            gatherer.have_small()

        def bias(row, columns):
            return lambda p: smalls[p, row : row + 1, :columns]

        def block(source, vectors, weights, row, outs, head_dim, total, befores):
            gain, shift, out_bias, feed_gain, feed_shift, down_bias = vectors
            attn, feed = weights
            refs = [out.ref for out in outs]
            attn_forward(
                head_dim,
                length,
                source,
                attn,
                (gain, shift, out_bias),
                bias(row, attn.shape[-1] // 4 * 3),
                refs[:5],
                order,
                befores[0],
            )
            for out in outs[:5]:
                out.flush()
            feed_forward(
                refs[4],
                feed,
                (feed_gain, feed_shift, down_bias),
                bias(row + 1, refs[6].shape[2]),
                refs[5:8],
                total,
                order,
                befores[1],
            )
            for out in outs[5:8]:
                out.flush()

        block(stream.ref, enc, weights[:2], 0, enc_outs, HEAD, totals[0], befores[:2])
        bridge_input.ref[...] = totals[0][...].astype(BF16)
        bridge_input.flush()
        bridged.ref[...] = dot(bridge_input.ref[...], ins[first - 1].use()[...]) + as_row(bridge_bias)
        bridged.flush()
        block(bridged.ref, dec, weights[2:], 2, dec_outs, DHEAD, totals[1], befores[2:])
        decoded[...] = totals[1][:strip, :].astype(BF16)
        if fast:
            gatherer.drain()

    results = staged_call("forward", body, ins, outs, scratch, 0 if fast else None)

    def stored(outs, source):
        normed, triple, attended, logsum, middle, feed_input, hidden, slope = outs
        return (
            (hidden, slope, feed_input, middle),
            (attended, triple, logsum, normed, source),
        )

    stream, bridge_input, bridged, decoded, *gathered = results[16:]
    return (
        stored(results[:8], stream),
        stored(results[8:16], bridged),
        bridge_input,
        decoded,
        gathered if fast else wholes,
    )


def stands(tall, flat):
    return tall % 128 == 0 and flat % 128 != 0


def run_outputs(rows, early, late, enc_sums, dec_sums, bridge_sum, sizes, bridge_shape):
    planes, groups = sizes["mp"], sizes["dp"]
    decoded, patches_grad = rows
    strip = decoded.shape[0]
    wide, narrow = bridge_shape
    deep = wide // groups // planes

    def block_shapes(columns, mats):
        width, hidden = mats[0].shape[1] // 4, mats[1].shape[2]
        each, piece = columns // groups // planes, columns // groups
        return [
            (each,),
            (each,),
            (3, piece, width),
            (2, width // groups),
            (piece, width) if stands(width, piece) else (width, piece),
            (each,),
            (each,),
            (each,),
            (piece, hidden),
            (hidden // groups,),
            (piece, hidden) if stands(hidden, piece) else (hidden, piece),
            (each,),
        ]

    shapes = block_shapes(wide, enc_sums) + [(deep, narrow), (narrow // groups // planes,)]
    shapes += block_shapes(narrow, dec_sums)
    ins = [decoded, patches_grad, early, late, *enc_sums, *dec_sums, bridge_sum]

    def kernel(*refs):
        decoded, patches_grad, early, late = refs[:4]
        enc, dec, bridge_sum = refs[4:6], refs[6:8], refs[8]
        decoded_out, patches_out, *outs = refs[9:]
        decoded_out[...] = decoded[...]
        patches_out[...] = patches_grad[:strip, :]
        dp, mp = lax.axis_index("dp"), lax.axis_index("mp")
        lanes = early.shape[1]

        def cut(values, low, size):
            values = pltpu.roll(values, lax.rem(lanes - low, lanes), 1)
            return values[:, :size]

        def put_rows(values, targets):
            for k, target in enumerate(targets):
                target[...] = values[k]

        def block(mats, outs, columns, first, row, second, up_row, head_row):
            attn, (up, down) = mats[0], (mats[1].at[0], mats[1].at[1])
            width, hidden = attn.shape[1] // 4, up.shape[1]
            gain, shift, proj, head, out, out_bias, f_gain, f_shift, up_out, up_bias, down_out, d_bias = outs
            for j in range(3):
                proj[j] = attn[:, j * width : (j + 1) * width]
            out_grad = attn[:, 3 * width :]
            out[...] = out_grad if out.shape == out_grad.shape else out_grad.T
            up_out[...] = up[...]
            down_out[...] = down[...] if down_out.shape == down.shape else down[...].T
            each = columns // groups // planes
            low = (dp * planes + mp) * each
            put_rows(cut(first[row : row + 8, :], low, each), (gain, shift, out_bias))
            lane, ref = second
            put_rows(cut(ref[lane : lane + 8, :], low, each), (f_gain, f_shift, d_bias))
            line = up_row[0][pl.ds(up_row[1] + mp, 1), :]
            put_rows(cut(line, dp * (hidden // groups), hidden // groups), (up_bias,))
            line = head_row[0][pl.ds(head_row[1] + mp, 1), :]
            piece = width // groups
            head[0:1, :] = cut(line, dp * piece, piece)
            head[1:2, :] = cut(line, 2 * width + dp * piece, piece)

        at = EARLY_DEC
        block(enc, outs[:12], wide, late, 0, (0, early), (early, 3), (late, 3))
        block(dec, outs[14:], narrow, early, at, (at + 8, early), (early, at + 3), (early, at + 11))
        outs[12][...] = bridge_sum[:deep, :]
        each = narrow // groups // planes
        line = cut(early[at + 15 : at + 16, :], (dp * planes + mp) * each, each)
        put_rows(line, (outs[13],))

    results = pl.pallas_call(
        kernel,
        out_shape=[
            jax.ShapeDtypeStruct(decoded.shape, BF16),
            jax.ShapeDtypeStruct((strip, wide), BF16),
        ]
        + [jax.ShapeDtypeStruct(shape, F32) for shape in shapes],
        in_specs=[IN_VMEM] * len(ins),
        out_specs=[IN_VMEM] * (2 + len(shapes)),
        compiler_params=pltpu.CompilerParams(vmem_limit_bytes=VMEM_BYTES),
        name="outputs",
    )(*ins)
    first, second = list(results[2:14]), list(results[16:28])
    for block, mats in ((first, enc_sums), (second, dec_sums)):
        for at, (tall, flat) in ((4, (mats[0].shape[1] // 4, mats[0].shape[0])), (10, mats[1].shape[:0:-1])):
            block[at] = block[at] if block[at].shape == (tall, flat) else block[at].T
    return (*results[:2], *first, *results[14:16], *second)


def shards(sizes, *inputs):
    patches, lengths = inputs[:2]
    cotangent = inputs[28]
    planes, groups = sizes["mp"], sizes["dp"]
    fast = groups == 8 and planes == 4
    strip, wide = patches.shape
    enc, (bridge_weight, bridge_bias), dec = inputs[2:14], inputs[14:16], inputs[16:28]

    def vectors_of(block):
        gain, shift, _, _, _, out_bias, f_gain, f_shift, _, _, _, d_bias = block
        return (gain, shift, out_bias, f_gain, f_shift, d_bias)

    enc_vectors, dec_vectors = vectors_of(enc), vectors_of(dec)
    enc_stored, dec_stored, bridge_input, decoded, wholes = run_forward(
        patches, lengths, enc, dec, (enc_vectors, dec_vectors), (bridge_weight, bridge_bias), fast
    )
    dec_gains, enc_gains = (dec[0], dec[6]), (enc[0], enc[6])
    down = run_backward(
        fast, (cotangent,), dec_stored, wholes[2:], dec_gains, lengths, DHEAD
    )
    dec_sums = {key: down[key] for key in SUM_NAMES}
    bridge = (down["input_grad"], bridge_input, bridge_weight)
    on = run_backward(
        fast,
        bridge,
        enc_stored,
        wholes[:2],
        enc_gains,
        lengths,
        HEAD,
        down["attn_part"] if fast else None,
        dec_sums,
    )
    if fast:
        rows_of = lambda v: v.reshape(-1, v.shape[-1])
        enc_grads = (rows_of(on["attn_sum"]), on["feed_sum"])
        dec_grads = (rows_of(on["carry_sum"]), down["feed_sum"])
        early, late, bridge_sum = on["early"], on["late"], rows_of(on["bridge_grad_sum"])
    else:
        feed_sums = [on[key] for key in ("f_gain", "f_shift", "down_bias", "up_bias")]
        rows = early_rows(feed_sums, [dec_sums[key] for key in SUM_NAMES], on["bridge"])
        early = stack_rows(rows, wide)
        late = stack_rows(late_rows(*(on[key] for key in SUM_NAMES[:4])), wide)
        early, late = lax.psum(early, ("dp", "mp")), lax.psum(late, ("dp", "mp"))

        def in_groups(grad):
            return collect(grad.reshape(planes, groups, -1, grad.shape[-1]), sizes)

        def block_grads(result):
            attn, feed = result["attn_part"], result["feed_part"]
            return in_groups(attn), jnp.stack([in_groups(feed[:, 0]), in_groups(feed[:, 1])])

        dec_grads, enc_grads = block_grads(down), block_grads(on)
        deep = wide // planes // groups
        bridge_part = on["bridge_grad"].reshape(groups, planes, deep, -1).transpose(1, 0, 2, 3)
        bridge_sum = collect(bridge_part, sizes)
    patches_grad = on["input_grad"]
    return run_outputs(
        (decoded, patches_grad),
        early,
        late,
        enc_grads,
        dec_grads,
        bridge_sum,
        sizes,
        bridge_weight.shape,
    )


def solution(mesh):
    block_in = (
        P(),
        P(),
        P(None, None, "mp"),
        P(None, "mp"),
        P("mp", None),
        P(),
        P(),
        P(),
        P(None, "mp"),
        P("mp"),
        P("mp", None),
        P(),
    )
    both = P(("dp", "mp"))
    block_out = (
        both,
        both,
        P(None, "dp", "mp"),
        P(None, ("mp", "dp")),
        P("mp", "dp"),
        both,
        both,
        both,
        P("dp", "mp"),
        P(("mp", "dp")),
        P("mp", "dp"),
        both,
    )
    rows = P(("dp", "mp"), None)
    return jax.shard_map(
        partial(shards, dict(mesh.shape)),
        mesh=mesh,
        in_specs=(rows, P("dp")) + block_in + (P(), P()) + block_in + (rows,),
        out_specs=(rows, rows) + block_out + (rows, both) + block_out,
        check_vma=False,
    )
```
